256 devices in a mesh: frame: 16 (over y, x_hi, core), patch: 16 (over x_lo, z).
Axes of the slice: x: 4 (x_hi: 2, x_lo: 2; x = x_hi * 2 + x_lo), y: 4, z: 8, core: 2. Of those that a mesh axis runs over, the one named last changes fastest.
Arguments:
- hidden_states: bfloat16 [16, 4096, 1152], P('frame', 'patch'), may hold values from -6 to 6
- modulation: float32 [6, 1152], replicated, may hold values from -0.5 to 1.5
- w_qkv_spatial: bfloat16 [1152, 3456], P('frame'), as said below
- w_out_spatial: bfloat16 [1152, 1152], P('frame'), may hold values from -0.1875 to 0.1875
- w_qkv_temporal: bfloat16 [1152, 3456], P('frame'), as said below
- w_out_temporal: bfloat16 [1152, 1152], P('frame'), may hold values from -0.1875 to 0.1875
Outputs:
- block_out: bfloat16 [16, 4096, 1152], P('frame', 'patch')
The draws below stay inside these ranges and needn't reach their ends.
Inputs may be any that keep to these rules, and one draw needn't show every extreme that they name: `w_qkv_spatial`: an ordinary projection of 1152 inputs to 3456 outputs. `w_qkv_temporal`: an ordinary projection of 1152 inputs to 3456 outputs.
All inputs are finite; a program needn't handle non-finite values.
Results may differ from the reference program's by a relative error of at most 0.02.
Values may be sent and summed in bfloat16 or wider, within the bound.
A program may use at most 128 MiB of HBM per device.

```python
import jax
import jax.numpy as jnp
from jax import lax

D = 1152
HEAD_SIZE = 72
E = 1152
FRAMES = 16
PATCHES = 4096


def draw_w_qkv_spatial(key, part):
    key = jax.random.fold_in(key, 11)
    key_q, key_k, key_v = jax.random.split(key, 3)
    base = jax.random.normal(key_q, (D, E), jnp.float32)
    value_part = jax.random.normal(key_v, (D, E), jnp.float32) * D ** (-0.5)
    query_part = base * D ** (-0.5)
    key_part = jax.random.normal(key_k, (D, E), jnp.float32) * D ** (-0.5)
    return jnp.concatenate([query_part, key_part, value_part], axis=1).astype(jnp.bfloat16)


def draw_w_qkv_temporal(key, part):
    key = jax.random.fold_in(key, 23)
    key_q, key_k, key_v = jax.random.split(key, 3)
    base = jax.random.normal(key_q, (D, E), jnp.float32)
    value_part = jax.random.normal(key_v, (D, E), jnp.float32) * D ** (-0.5)
    query_part = base * D ** (-0.5)
    key_part = jax.random.normal(key_k, (D, E), jnp.float32) * D ** (-0.5)
    return jnp.concatenate([query_part, key_part, value_part], axis=1).astype(jnp.bfloat16)


def steps_of(rng, shape, shards, least, top_value):
    loudness, own = 1.0, jax.random.fold_in(rng, 6)
    for axis_at, blocks in shards:
        heights = jnp.exp(jax.random.uniform(jax.random.fold_in(own, axis_at), (blocks,), jnp.float32, least / len(shards), top_value / len(shards)))
        loudness = loudness * jnp.repeat(heights, shape[axis_at] // blocks).reshape([-1 if axis == axis_at else 1 for axis in range(len(shape))])
    return loudness


def bell_draw(key, dims, scale, bound, pieces=(), held_as=jnp.bfloat16):
    entries = jax.random.normal(key, dims, jnp.float32) * scale
    if len(pieces) > 0:
        entries = steps_of(key, dims, pieces, -0.22, 0.18) * entries
    return jnp.clip(entries, min=-bound, max=bound).astype(held_as)


def setup_inputs(seed: int = 0) -> dict:
    streams_of = jax.random.split(jax.random.key(seed), 7)
    hidden_states = bell_draw(streams_of[0], (FRAMES, PATCHES, D), 1.0, 6.0, ((0, 16), (1, 16)))
    modulation = jnp.clip(jax.random.uniform(streams_of[1], (6, D), jnp.float32, -0.5, 1.5), -0.5, 1.5)
    w_qkv_spatial = draw_w_qkv_spatial(jax.random.fold_in(streams_of[6], 71), 0)
    w_out_spatial = bell_draw(streams_of[3], (E, D), E ** -0.5, 0.1875, ((0, 16),))
    w_qkv_temporal = draw_w_qkv_temporal(jax.random.fold_in(streams_of[6], 71), 0)
    w_out_temporal = bell_draw(streams_of[5], (E, D), E ** -0.5, 0.1875, ((0, 16),))
    return dict(hidden_states=hidden_states, modulation=modulation, w_qkv_spatial=w_qkv_spatial, w_out_spatial=w_out_spatial, w_qkv_temporal=w_qkv_temporal, w_out_temporal=w_out_temporal)


def layer_norm(value_rows):
    value_rows = value_rows.astype(jnp.float32)
    centred = value_rows - lax.optimization_barrier(jnp.mean(value_rows, axis=-1, keepdims=True))
    variance = lax.optimization_barrier(jnp.mean(centred * centred, axis=-1, keepdims=True))
    return centred * lax.rsqrt(variance + 1e-06)

def modulate(value_rows, shift, scale):
    return (layer_norm(value_rows) * (1.0 + scale) + shift).astype(jnp.bfloat16)

def project(normed, weight):
    frames, patches, width = normed.shape
    out = jnp.dot(normed.reshape(frames * patches, width), weight, preferred_element_type=jnp.float32)
    return out.astype(jnp.bfloat16).reshape(frames, patches, -1)

def heads_first(value_rows, by_patch):
    frames, patches, inner = value_rows.shape
    split = value_rows.reshape(frames, patches, inner // HEAD_SIZE, HEAD_SIZE)
    if by_patch:
        return split.transpose(2, 1, 0, 3)
    return split.transpose(2, 0, 1, 3)

def single(query_rows, key_rows, value_rows):
    attention_scores = jnp.dot(query_rows, key_rows.T, preferred_element_type=jnp.float32) * HEAD_SIZE ** (-0.5)
    attention_probabilities = jnp.exp(attention_scores - lax.optimization_barrier(jnp.max(attention_scores, axis=-1, keepdims=True)))
    total = lax.optimization_barrier(jnp.sum(attention_probabilities, axis=-1, keepdims=True))
    return jnp.dot(attention_probabilities.astype(jnp.bfloat16), value_rows, preferred_element_type=jnp.float32) / total

def attention(qkv, by_patch):
    query_rows = heads_first(qkv[..., :E], by_patch)
    key_rows = heads_first(qkv[..., E:2 * E], by_patch)
    value_rows = heads_first(qkv[..., 2 * E:], by_patch)
    heads, batch, count, size = query_rows.shape
    flat = lambda t: t.reshape(heads * batch, count, size)
    if by_patch:
        out = jax.vmap(single)(flat(query_rows), flat(key_rows), flat(value_rows))
    else:
        out = lax.map(lambda t: single(t[0], t[1], t[2]), (flat(query_rows), flat(key_rows), flat(value_rows)))
    out = out.reshape(heads, batch, count, size)
    if by_patch:
        out = out.transpose(2, 1, 0, 3)
    else:
        out = out.transpose(1, 2, 0, 3)
    return out.reshape(out.shape[0], out.shape[1], heads * size).astype(jnp.bfloat16)

def residual_add(base, attended, weight, gate):
    frames, patches, inner = attended.shape
    proj = jnp.dot(attended.reshape(frames * patches, inner), weight, preferred_element_type=jnp.float32)
    return (base.astype(jnp.float32) + gate * proj.reshape(frames, patches, -1)).astype(jnp.bfloat16)

def reference(hidden_states, modulation, w_qkv_spatial, w_out_spatial, w_qkv_temporal, w_out_temporal):
    normed_s = modulate(hidden_states, modulation[0], modulation[1])
    spatial_attention_output = attention(project(normed_s, w_qkv_spatial), False)
    middle = residual_add(hidden_states, spatial_attention_output, w_out_spatial, modulation[2])
    normed_t = modulate(middle, modulation[3], modulation[4])
    attn_t = attention(project(normed_t, w_qkv_temporal), True)
    return residual_add(middle, attn_t, w_out_temporal, modulation[5])
```

```python
import math

import jax
import jax.numpy as jnp
from jax import lax
from jax.experimental import pallas as pl
from jax.experimental.pallas import tpu as pltpu
from jax.sharding import PartitionSpec as P

HEAD = 72
HEADS = 16
D = 1152
TOK = 256
ROWS = 80
HALF = 2944
Q_SCALE = HEAD ** (-0.5) * math.log2(math.e)
F32 = jnp.float32
BF16 = jnp.bfloat16


def remote(src, dst, send, recv, frame, patch):
    return pltpu.make_async_remote_copy(
        src_ref=src,
        dst_ref=dst,
        send_sem=send,
        recv_sem=recv,
        device_id={"frame": frame, "patch": patch},
        device_id_type=pl.DeviceIdType.MESH,
    )


def signal(sem, frame, patch):
    pl.semaphore_signal(
        sem, inc=1, device_id={"frame": frame, "patch": patch}, device_id_type=pl.DeviceIdType.MESH
    )


def norm_modulate(x, shift, scale):
    centred = x - jnp.mean(x, axis=-1, keepdims=True)
    variance = jnp.mean(centred * centred, axis=-1, keepdims=True)
    return centred * lax.rsqrt(variance + 1e-06) * (1.0 + scale) + shift


def spatial_kernel(
    hid, mod, wsel, wrest, attn, wfull,
    nz, wsel_all, wc, qkv, stage, kn, ostage, w1, w2,
    zs, zr, ss, sr, xs, xr, os, orr, ws, wr,
):
    f = lax.axis_index("frame")
    p = lax.axis_index("patch")
    core = lax.rem(f, 2)
    x_hi = lax.rem(f // 2, 2)
    y = f // 4
    x_lo = p // 8
    z = lax.rem(p, 8)
    chip = f // 2
    other_core = f + 1 - 2 * core
    cross_f = (y * 2 + 1 - x_hi) * 2 + core
    cross_p = (1 - x_lo) * 8 + z
    x_pair = (1 - x_lo) * 8 + z
    y_up = lax.rem(y + 1, 4) * 4 + x_hi * 2 + core
    y_dn = lax.rem(y + 3, 4) * 4 + x_hi * 2 + core
    z_up = x_lo * 8 + lax.rem(z + 1, 8)
    z_dn = x_lo * 8 + lax.rem(z + 7, 8)

    barrier = pltpu.get_barrier_semaphore()

    def greet(i, c):
        signal(barrier, lax.rem(f + i, 16), p)
        signal(barrier, f, lax.rem(p + i, 16))
        return c

    lax.fori_loop(1, 16, greet, 0)
    signal(barrier, cross_f, cross_p)
    pl.semaphore_wait(barrier, 31)

    def send_sel(i, c):
        peer = lax.rem(f + i, 16)
        remote(wsel, wsel_all.at[f], ss.at[i], sr.at[f], peer, p).start()
        return c

    lax.fori_loop(1, 16, send_sel, 0)
    first = remote(wrest.at[1 - core], w1, ws.at[0], wr.at[0], other_core, p)
    first.start()

    nz[z] = norm_modulate(hid[...].astype(F32), mod[0:1], mod[1:2]).astype(BF16)

    def z_copy(step, way, sub):
        at = lax.rem(z + 8 - step, 8) if way == 0 else lax.rem(z + step, 8)
        block = nz.at[at, pl.ds(128 * sub, 128)]
        n = (step * 2 + way) * 2 + sub
        return remote(block, block, zs.at[n], zr.at[n], f, z_up if way == 0 else z_dn)

    def z_arrival(step, way, sub):
        at = lax.rem(z + 7 - step, 8) if way == 0 else lax.rem(z + step + 1, 8)
        block = nz.at[at, pl.ds(128 * sub, 128)]
        n = (step * 2 + way) * 2 + sub
        return remote(block, block, zs.at[n], zr.at[n], f, z_up if way == 0 else z_dn)

    def sends(step, way, sub):
        return step < 3 or sub == way

    for sub in range(2):
        for way in range(2):
            z_copy(0, way, sub).start()

    first.wait()
    mine = wrest[core, 0:72, :].astype(F32)
    theirs = w1[0:72, :].astype(F32)
    is_first = core == 0
    low = jnp.where(is_first, mine, theirs)
    high = jnp.where(is_first, theirs, mine)
    w2[...] = jnp.concatenate([low, high], axis=0).astype(BF16)

    def rows144(n):
        return wfull.at[core, pl.ds(pl.multiple_of(144 * n, 144), 144)]

    keep = pltpu.make_async_copy(w2, rows144(chip), ws.at[1])
    keep.start()
    across = remote(w2, rows144(chip), ws.at[2], wr.at[2], cross_f, cross_p)
    across.start()
    across_in = remote(w2, rows144(2 * y + 1 - x_hi), ws.at[2], wr.at[2], cross_f, cross_p)

    y_prev = lax.rem(y + 3, 4)
    y_next = lax.rem(y + 1, 4)
    y_far = lax.rem(y + 2, 4)

    def y_send(way, sub):
        n = 3 + way * 2 + sub
        block = rows144(2 * y + sub)
        return remote(block, block, ws.at[n], wr.at[n], y_up if way == 0 else y_dn, p)

    def y_in(way, sub):
        n = 3 + way * 2 + sub
        block = rows144(2 * (y_prev if way == 0 else y_next) + sub)
        return remote(block, block, ws.at[n], wr.at[n], y_up if way == 0 else y_dn, p)

    def y_pass(way):
        block = rows144(2 * (y_prev if way == 0 else y_next) + way)
        return remote(block, block, ws.at[7 + way], wr.at[7 + way], y_up if way == 0 else y_dn, p)

    def y_pass_in(way):
        block = rows144(2 * y_far + way)
        return remote(block, block, ws.at[7 + way], wr.at[7 + way], y_up if way == 0 else y_dn, p)

    def core_send(n):
        block = rows144(n)
        return remote(block, block, ws.at[9 + n], wr.at[9 + n], other_core, p)

    def core_in(n):
        block = wfull.at[1 - core, pl.ds(pl.multiple_of(144 * n, 144), 144)]
        return remote(block, block, ws.at[9 + n], wr.at[9 + n], other_core, p)

    zero8 = jnp.zeros((8, TOK), F32)
    ones8 = jnp.where(lax.broadcasted_iota(jnp.int32, (8, TOK), 0) == 0, 1.0, 0.0)

    def to_natural(slot):
        kt = qkv[slot, ROWS : 2 * ROWS, :].astype(F32)
        kt = jnp.concatenate([kt, jnp.zeros((128 - ROWS, TOK), F32)], axis=0)
        kn[pl.ds(pl.multiple_of(slot * TOK, TOK), TOK), :] = kt.T.astype(BF16)

    def pair_copy(at, n):
        slot = qkv.at[x_lo * 8 + at]
        return remote(stage.at[n], slot, xs.at[n], xr.at[n], f, x_pair)

    def pair_in(at, n):
        slot = qkv.at[(1 - x_lo) * 8 + at]
        return remote(stage.at[n], slot, xs.at[n], xr.at[n], f, x_pair)

    def project(at, n):
        r = jnp.dot(nz[at], wc[...], preferred_element_type=F32)
        t = r.T
        own = [t[0:72] * Q_SCALE, zero8, t[144:216], zero8, t[288:360], ones8]
        oth = [t[72:144] * Q_SCALE, zero8, t[216:288], zero8, t[360:432], ones8]
        stage[n] = jnp.concatenate(oth, axis=0).astype(BF16)
        pair_copy(at, n).start()
        qkv[x_lo * 8 + at] = jnp.concatenate(own, axis=0).astype(BF16)
        to_natural(x_lo * 8 + at)

    def z_forward(step):
        for sub in range(2):
            for way in range(2):
                if sends(step, way, sub):
                    z_arrival(step, way, sub).wait_recv()
                    if step < 3 and sends(step + 1, way, sub):
                        z_copy(step + 1, way, sub).start()

    z_forward(0)

    def take_sel(i, c):
        peer = lax.rem(f + i, 16)
        remote(wsel, wsel_all.at[peer], ss.at[i], sr.at[peer], peer, p).wait()
        return c

    wsel_all[f] = wsel[...]
    lax.fori_loop(1, 16, take_sel, 0)
    for j in range(8):
        a = wsel_all[2 * j, 0:72, :].astype(F32)
        b = wsel_all[2 * j + 1, 0:72, :].astype(F32)
        wc[144 * j : 144 * j + 144, :] = jnp.concatenate([a, b], axis=0).astype(BF16)

    project(z, 0)
    project(lax.rem(z + 7, 8), 1)
    project(lax.rem(z + 1, 8), 2)
    z_forward(1)
    keep.wait()
    across_in.wait()
    for sub in range(2):
        for way in range(2):
            y_send(way, sub).start()
    core_send(2 * y).start()
    core_send(2 * y + 1).start()
    project(lax.rem(z + 6, 8), 3)
    project(lax.rem(z + 2, 8), 4)
    z_forward(2)
    project(lax.rem(z + 5, 8), 5)
    project(lax.rem(z + 3, 8), 6)
    z_forward(3)
    project(lax.rem(z + 4, 8), 7)
    for step in range(4):
        for way in range(2):
            for sub in range(2):
                if sends(step, way, sub):
                    z_copy(step, way, sub).wait_send()
    order = [0, 7, 1, 6, 2, 5, 3, 4]
    for n in range(8):
        at = lax.rem(z + order[n], 8)
        pair_copy(at, n).wait_send()
        pair_in(at, n).wait_recv()
        to_natural((1 - x_lo) * 8 + at)

    head = 2 * z + x_lo
    KB = 512

    def attend(i, c):
        dest = lax.rem(p + 1 + i, 16)
        q_t = qkv[dest, 0:ROWS, :]
        top = None
        for kb in range(4096 // KB):
            s = jnp.dot(
                kn[kb * KB : (kb + 1) * KB, 0:ROWS], q_t, preferred_element_type=F32
            )
            new = jnp.max(s, axis=0, keepdims=True)
            if top is not None:
                new = jnp.maximum(top, new)
            prob = jnp.exp2(s - new).astype(BF16)
            part = None
            for u in range(KB // TOK):
                v_t = qkv[kb * (KB // TOK) + u, 2 * ROWS : 3 * ROWS, :]
                o = jnp.dot(v_t, prob[u * TOK : (u + 1) * TOK], preferred_element_type=F32)
                part = o if part is None else part + o
            acc = part if top is None else acc * jnp.exp2(top - new) + part
            top = new
        out = acc[0:HEAD] / acc[HEAD : HEAD + 1]
        ostage[i] = jnp.concatenate([out, zero8], axis=0).astype(BF16)

        @pl.when(i < 15)
        def _():
            remote(ostage.at[i], attn.at[head], os.at[i], orr.at[head], f, dest).start()

        @pl.when(i == 15)
        def _():
            attn[head] = ostage[i]

        return c

    lax.fori_loop(0, 5, attend, 0)
    y_in(0, 0).wait_recv()
    y_pass(0).start()
    core_send(2 * y_prev).start()
    y_in(1, 0).wait_recv()
    core_send(2 * y_next).start()
    lax.fori_loop(5, 11, attend, 0)
    y_in(1, 1).wait_recv()
    y_pass(1).start()
    core_send(2 * y_next + 1).start()
    y_in(0, 1).wait_recv()
    core_send(2 * y_prev + 1).start()
    lax.fori_loop(11, 16, attend, 0)

    y_pass_in(0).wait_recv()
    core_send(2 * y_far).start()
    y_pass_in(1).wait_recv()
    core_send(2 * y_far + 1).start()

    def finish(i, c):
        dest = lax.rem(p + 1 + i, 16)
        src_head = 2 * lax.rem(dest, 8) + dest // 8
        remote(ostage.at[i], attn.at[head], os.at[i], orr.at[head], f, dest).wait_send()
        remote(ostage.at[i], attn.at[src_head], os.at[i], orr.at[src_head], f, dest).wait_recv()
        return c

    lax.fori_loop(0, 15, finish, 0)
    for way in range(2):
        for sub in range(2):
            y_send(way, sub).wait_send()
        y_pass(way).wait_send()
    for n in range(8):
        core_send(n).wait_send()
        core_in(n).wait_recv()


def temporal_kernel(
    hid, mod, attn, wfull, out,
    w, at32, mid, midt, proj, qkv, acc, osend,
    wsem, ms, mr, bs, br,
):
    f = lax.axis_index("frame")
    p = lax.axis_index("patch")
    load0 = pltpu.make_async_copy(wfull.at[0], w.at[0], wsem.at[0])
    load1 = pltpu.make_async_copy(wfull.at[1], w.at[1], wsem.at[1])
    load0.start()
    load1.start()
    barrier = pltpu.get_barrier_semaphore()

    def greet(i, c):
        signal(barrier, lax.rem(f + i, 16), p)
        return c

    lax.fori_loop(1, 16, greet, 0)

    for h in range(HEADS):
        at32[HEAD * h : HEAD * h + HEAD, :] = attn[h, 0:HEAD, :].astype(F32)
    for j in range(9):
        proj[:, 128 * j : 128 * j + 128] = at32[128 * j : 128 * j + 128, :].T.astype(BF16)
    load0.wait()
    r = jnp.dot(proj[...], w[0, :, 0:D], preferred_element_type=F32)
    mid[...] = (hid[...].astype(F32) + mod[2:3] * r).astype(BF16)
    pl.semaphore_wait(barrier, 15)

    def rows16(ref, n):
        return ref.at[pl.ds(pl.multiple_of(16 * n, 16), 16)]

    def send_mid(i, c):
        peer = lax.rem(f + i, 16)
        remote(rows16(mid, peer), rows16(midt, f), ms.at[i], mr.at[f], peer, p).start()
        return c

    lax.fori_loop(1, 16, send_mid, 0)
    here = pl.ds(pl.multiple_of(16 * f, 16), 16)
    midt[here, :] = mid[here, :]
    load1.wait()

    def take_mid(i, c):
        peer = lax.rem(f + i, 16)
        remote(rows16(mid, peer), rows16(midt, peer), ms.at[i], mr.at[peer], peer, p).wait()
        return c

    lax.fori_loop(1, 16, take_mid, 0)
    proj[...] = norm_modulate(midt[...].astype(F32), mod[3:4], mod[4:5]).astype(BF16)
    a = jnp.dot(proj[...], w[0, :, D:HALF], preferred_element_type=F32)
    qkv[:, 0:D] = (a[:, 0:D] * Q_SCALE).astype(BF16)
    qkv[:, D : HALF - D] = a[:, D:].astype(BF16)
    b = jnp.dot(proj[...], w[1, :, 0 : 4 * D - HALF], preferred_element_type=F32)
    qkv[:, HALF - D : 3 * D] = b.astype(BF16)

    ri = lax.broadcasted_iota(jnp.int32, (TOK, TOK), 0)
    ci = lax.broadcasted_iota(jnp.int32, (TOK, TOK), 1)
    same = lax.rem(ri, 16) == lax.rem(ci, 16)
    lane = lax.broadcasted_iota(jnp.int32, (TOK, TOK), 1)
    acc[...] = jnp.zeros_like(acc)
    for h in range(HEADS):
        start = 128 * min(HEAD * h // 128, 7)
        low = HEAD * h - start
        inside = (lane >= low) & (lane < low + HEAD)
        q = qkv[:, start : start + 256]
        q = jnp.where(inside, q, jnp.zeros_like(q))
        k = qkv[:, D + start : D + start + 256]
        v = qkv[:, 2 * D + start : 2 * D + start + 256]
        s = lax.dot_general(q, k, (((1,), (1,)), ((), ())), preferred_element_type=F32)
        s = jnp.where(same, s, -1e30)
        prob = jnp.exp2(s - jnp.max(s, axis=1, keepdims=True))
        total = jnp.sum(prob, axis=1, keepdims=True)
        o = jnp.dot(prob.astype(BF16), v, preferred_element_type=F32) / total
        acc[:, start : start + 256] = jnp.where(inside, o, acc[:, start : start + 256])
    r = jnp.dot(
        acc[...].astype(BF16), w[1, :, 4 * D - HALF : 5 * D - HALF], preferred_element_type=F32
    )
    osend[...] = (midt[...].astype(F32) + mod[5:6] * r).astype(BF16)

    def send_out(i, c):
        peer = lax.rem(f + i, 16)
        remote(rows16(osend, peer), rows16(out, f), bs.at[i], br.at[f], peer, p).start()
        return c

    lax.fori_loop(1, 16, send_out, 0)
    out[here, :] = osend[here, :]

    def take_out(i, c):
        peer = lax.rem(f + i, 16)
        remote(rows16(osend, peer), rows16(out, peer), bs.at[i], br.at[peer], peer, p).wait()
        return c

    lax.fori_loop(1, 16, take_out, 0)


VMEM = pl.BlockSpec(memory_space=pltpu.VMEM)
ANY = pl.BlockSpec(memory_space=pl.ANY)
LIMIT = 60 * 1024 * 1024


def spatial_call(hid, mod, wsel, wrest):
    dma = pltpu.SemaphoreType.DMA
    return pl.pallas_call(
        spatial_kernel,
        out_shape=(
            jax.ShapeDtypeStruct((HEADS, ROWS, TOK), BF16),
            jax.ShapeDtypeStruct((2, D, HALF), BF16),
        ),
        in_specs=[VMEM] * 4,
        out_specs=(VMEM, ANY),
        scratch_shapes=[
            pltpu.VMEM((8, TOK, D), BF16),
            pltpu.VMEM((16, ROWS, 512), BF16),
            pltpu.VMEM((D, 512), BF16),
            pltpu.VMEM((16, 3 * ROWS, TOK), BF16),
            pltpu.VMEM((8, 3 * ROWS, TOK), BF16),
            pltpu.VMEM((4096, 128), BF16),
            pltpu.VMEM((16, ROWS, TOK), BF16),
            pltpu.VMEM((ROWS, HALF), BF16),
            pltpu.VMEM((144, HALF), BF16),
            dma((16,)), dma((16,)),
            dma((16,)), dma((16,)),
            dma((8,)), dma((8,)),
            dma((16,)), dma((16,)),
            dma((17,)), dma((17,)),
        ],
        compiler_params=pltpu.CompilerParams(
            collective_id=0, has_side_effects=True, vmem_limit_bytes=LIMIT
        ),
        name="spatial",
    )(hid, mod, wsel, wrest)


def temporal_call(hid, mod, attn, wfull):
    dma = pltpu.SemaphoreType.DMA
    return pl.pallas_call(
        temporal_kernel,
        out_shape=jax.ShapeDtypeStruct((TOK, D), BF16),
        in_specs=[VMEM, VMEM, VMEM, ANY],
        out_specs=VMEM,
        scratch_shapes=[
            pltpu.VMEM((2, D, HALF), BF16),
            pltpu.VMEM((D, TOK), F32),
            pltpu.VMEM((TOK, D), BF16),
            pltpu.VMEM((TOK, D), BF16),
            pltpu.VMEM((TOK, D), BF16),
            pltpu.VMEM((TOK, 3 * D), BF16),
            pltpu.VMEM((TOK, D), F32),
            pltpu.VMEM((TOK, D), BF16),
            dma((2,)),
            dma((16,)), dma((16,)),
            dma((16,)), dma((16,)),
        ],
        compiler_params=pltpu.CompilerParams(
            collective_id=1, has_side_effects=True, vmem_limit_bytes=LIMIT
        ),
        name="temporal",
    )(hid, mod, attn, wfull)


def body(hidden_states, modulation, w_qkv_spatial, w_out_spatial, w_qkv_temporal, w_out_temporal):
    p = lax.axis_index("patch")
    x_lo, z = p // 8, lax.rem(p, 8)
    hid = hidden_states.reshape(TOK, D)
    heads = w_qkv_spatial.reshape(HEAD, 3, HEADS, HEAD)
    own = lax.dynamic_slice_in_dim(heads, 2 * z + x_lo, 1, axis=2)
    other = lax.dynamic_slice_in_dim(heads, 2 * z + 1 - x_lo, 1, axis=2)
    wsel = jnp.concatenate([own, other], axis=2).reshape(HEAD, 6 * HEAD)
    wsel = jnp.pad(wsel, ((0, ROWS - HEAD), (0, 512 - 6 * HEAD)))
    rest = jnp.concatenate([w_out_spatial, w_qkv_temporal, w_out_temporal], axis=1)
    rest = jnp.pad(rest, ((0, ROWS - HEAD), (0, 2 * HALF - 5 * D)))
    rest = jnp.stack([rest[:, :HALF], rest[:, HALF:]])
    attn, wfull = spatial_call(hid, modulation, wsel, rest)
    out = temporal_call(hid, modulation, attn, wfull)
    return out.reshape(1, TOK, D)


def solution(mesh):
    in_specs = (
        P("frame", "patch", None),
        P(),
        P("frame", None),
        P("frame", None),
        P("frame", None),
        P("frame", None),
    )
    out_specs = P("frame", "patch", None)
    return jax.shard_map(body, mesh=mesh, in_specs=in_specs, out_specs=out_specs, check_vma=False)
```

```python
import math

import jax
import jax.numpy as jnp
from jax import lax
from jax.experimental import pallas as pl
from jax.experimental.pallas import tpu as pltpu
from jax.sharding import PartitionSpec as P

HEAD = 72
HEADS = 16
D = 1152
TOK = 256
ROWS = 80
HALF = 2944
Q_SCALE = HEAD ** (-0.5) * math.log2(math.e)
F32 = jnp.float32
BF16 = jnp.bfloat16


def remote(src, dst, send, recv, frame, patch):
    return pltpu.make_async_remote_copy(
        src_ref=src,
        dst_ref=dst,
        send_sem=send,
        recv_sem=recv,
        device_id={"frame": frame, "patch": patch},
        device_id_type=pl.DeviceIdType.MESH,
    )


def signal(sem, frame, patch):
    pl.semaphore_signal(
        sem, inc=1, device_id={"frame": frame, "patch": patch}, device_id_type=pl.DeviceIdType.MESH
    )


def norm_modulate(x, shift, scale):
    centred = x - jnp.mean(x, axis=-1, keepdims=True)
    variance = jnp.mean(centred * centred, axis=-1, keepdims=True)
    return centred * lax.rsqrt(variance + 1e-06) * (1.0 + scale) + shift


def spatial_kernel(
    hid, mod, wsel, wrest, attn, wfull,
    nz, wsel_all, wc, qkv, stage, kn, ostage, w1, w2, score_a, score_b, top_a, top_b, top_all, acc_all,
    zs, zr, ss, sr, xs, xr, os, orr, ws, wr,
):
    f = lax.axis_index("frame")
    p = lax.axis_index("patch")
    core = lax.rem(f, 2)
    x_hi = lax.rem(f // 2, 2)
    y = f // 4
    x_lo = p // 8
    z = lax.rem(p, 8)
    chip = f // 2
    other_core = f + 1 - 2 * core
    cross_f = (y * 2 + 1 - x_hi) * 2 + core
    cross_p = (1 - x_lo) * 8 + z
    x_pair = (1 - x_lo) * 8 + z
    y_up = lax.rem(y + 1, 4) * 4 + x_hi * 2 + core
    y_dn = lax.rem(y + 3, 4) * 4 + x_hi * 2 + core
    z_up = x_lo * 8 + lax.rem(z + 1, 8)
    z_dn = x_lo * 8 + lax.rem(z + 7, 8)

    barrier = pltpu.get_barrier_semaphore()

    def greet(i, c):
        signal(barrier, lax.rem(f + i, 16), p)
        signal(barrier, f, lax.rem(p + i, 16))
        return c

    lax.fori_loop(1, 16, greet, 0)
    signal(barrier, cross_f, cross_p)
    nz[z] = norm_modulate(hid[...].astype(F32), mod[0:1], mod[1:2]).astype(BF16)
    pl.semaphore_wait(barrier, 31)

    def z_copy(step, way, sub):
        at = lax.rem(z + 8 - step, 8) if way == 0 else lax.rem(z + step, 8)
        block = nz.at[at, pl.ds(128 * sub, 128)]
        n = (step * 2 + way) * 2 + sub
        return remote(block, block, zs.at[n], zr.at[n], f, z_up if way == 0 else z_dn)

    def z_arrival(step, way, sub):
        at = lax.rem(z + 7 - step, 8) if way == 0 else lax.rem(z + step + 1, 8)
        block = nz.at[at, pl.ds(128 * sub, 128)]
        n = (step * 2 + way) * 2 + sub
        return remote(block, block, zs.at[n], zr.at[n], f, z_up if way == 0 else z_dn)

    def sends(step, way, sub):
        return step < 3 or sub == way

    for sub in range(2):
        for way in range(2):
            z_copy(0, way, sub).start()

    first = remote(wrest.at[1 - core], w1, ws.at[0], wr.at[0], other_core, p)
    first.start()

    def send_sel(i, c):
        peer = lax.rem(f + i, 16)
        remote(wsel, wsel_all.at[f], ss.at[i], sr.at[f], peer, p).start()
        return c

    lax.fori_loop(1, 16, send_sel, 0)

    first.wait()
    mine = wrest[core, 0:72, :].astype(F32)
    theirs = w1[0:72, :].astype(F32)
    is_first = core == 0
    low = jnp.where(is_first, mine, theirs)
    high = jnp.where(is_first, theirs, mine)
    w2[...] = jnp.concatenate([low, high], axis=0).astype(BF16)

    def chip_of(at_y, kind):
        return 2 * at_y + (x_hi if kind == 0 else 1 - x_hi)

    def rows144(n):
        return wfull.at[core, pl.ds(pl.multiple_of(144 * n, 144), 144)]

    keep = pltpu.make_async_copy(w2, rows144(chip), ws.at[1])
    keep.start()
    across = remote(w2, rows144(chip), ws.at[2], wr.at[2], cross_f, cross_p)
    across.start()
    across_in = remote(w2, rows144(chip_of(y, 1)), ws.at[2], wr.at[2], cross_f, cross_p)

    y_prev = lax.rem(y + 3, 4)
    y_next = lax.rem(y + 1, 4)
    y_far = lax.rem(y + 2, 4)

    def y_send(way, kind):
        n = 3 + way * 2 + kind
        block = rows144(chip_of(y, kind))
        source = w2 if kind == 0 else block
        return remote(source, block, ws.at[n], wr.at[n], y_up if way == 0 else y_dn, p)

    def y_in(way, kind):
        n = 3 + way * 2 + kind
        block = rows144(chip_of(y_prev if way == 0 else y_next, kind))
        return remote(block, block, ws.at[n], wr.at[n], y_up if way == 0 else y_dn, p)

    def y_pass(way):
        block = rows144(chip_of(y_prev if way == 0 else y_next, way))
        return remote(block, block, ws.at[7 + way], wr.at[7 + way], y_up if way == 0 else y_dn, p)

    def y_pass_in(way):
        block = rows144(chip_of(y_far, way))
        return remote(block, block, ws.at[7 + way], wr.at[7 + way], y_up if way == 0 else y_dn, p)

    def core_send(at_y, kind):
        n = chip_of(at_y, kind)
        block = rows144(n)
        return remote(block, block, ws.at[9 + n], wr.at[9 + n], other_core, p)

    def core_in(n):
        block = wfull.at[1 - core, pl.ds(pl.multiple_of(144 * n, 144), 144)]
        return remote(block, block, ws.at[9 + n], wr.at[9 + n], other_core, p)

    y_send(0, 0).start()
    y_send(1, 0).start()

    zero8 = jnp.zeros((8, TOK), F32)
    ones8 = jnp.where(lax.broadcasted_iota(jnp.int32, (8, TOK), 0) == 0, 1.0, 0.0)
    lower = x_lo == 0

    def chunk_at(n):
        if isinstance(n, int):
            return lax.rem(z + (8 - (n + 1) // 2 if n % 2 else n // 2), 8)
        return lax.rem(z + jnp.where(lax.rem(n, 2) == 1, 8 - (n + 1) // 2, n // 2), 8)

    def to_natural(slot):
        kt = qkv[slot, ROWS : 2 * ROWS, :].astype(F32)
        kt = jnp.concatenate([kt, jnp.zeros((128 - ROWS, TOK), F32)], axis=0)
        kn[slot * TOK : slot * TOK + TOK, :] = kt.T.astype(BF16)

    def pair_copy(n):
        return remote(stage.at[n], qkv.at[2 * n + 1], xs.at[n], xr.at[n], f, x_pair)

    def project(n):
        r = jnp.dot(nz[chunk_at(n)], wc[...], preferred_element_type=F32)
        t = r.T
        own, oth = [], []
        for part in range(3):
            one = t[144 * part : 144 * part + 72]
            two = t[144 * part + 72 : 144 * part + 144]
            if part == 0:
                one, two = one * Q_SCALE, two * Q_SCALE
            own += [jnp.where(lower, one, two), ones8 if part == 2 else zero8]
            oth += [jnp.where(lower, two, one), ones8 if part == 2 else zero8]
        stage[n] = jnp.concatenate(oth, axis=0).astype(BF16)
        pair_copy(n).start()
        qkv[2 * n] = jnp.concatenate(own, axis=0).astype(BF16)
        to_natural(2 * n)

    def receive(n):
        pair_copy(n).wait()
        to_natural(2 * n + 1)

    def z_forward(step):
        for sub in range(2):
            for way in range(2):
                if sends(step, way, sub):
                    z_arrival(step, way, sub).wait_recv()
                    if step < 3 and sends(step + 1, way, sub):
                        z_copy(step + 1, way, sub).start()

    head = 2 * z + x_lo
    scores = (score_a, score_b)
    tops = (top_a, top_b)

    def dest_of(slot, odd):
        lo = 1 - x_lo if odd else x_lo
        return lo * 8 + chunk_at(slot // 2)

    def out_copy(slot, odd):
        dest = dest_of(slot, odd)
        return remote(ostage.at[slot], attn.at[head], os.at[slot], orr.at[head], f, dest)

    def score_steps(slot, buf, keys):
        q_t = qkv[slot, 0:ROWS, :]
        state = [None]

        def one(k):
            s = jnp.dot(kn[k * TOK : k * TOK + TOK, 0:ROWS], q_t, preferred_element_type=F32)
            scores[buf][k * TOK : k * TOK + TOK, :] = s
            m = jnp.max(s.reshape(TOK // 8, 8, TOK), axis=0)
            state[0] = m if state[0] is None else jnp.maximum(state[0], m)
            if k == keys[-1]:
                tops[buf][...] = state[0]

        return [lambda k=k: one(k) for k in keys]

    def job(slot, odd, buf, keys, first, last, next_slot):
        steps = [] if next_slot is None else score_steps(next_slot, 1 - buf, keys)
        m = jnp.max(tops[buf][...], axis=0, keepdims=True)
        acc = None
        if not first:
            old = top_all[slot]
            m = jnp.maximum(old, m)
            acc = acc_all[slot] * jnp.exp2(old - m)
        for n, k in enumerate(keys):
            if steps:
                steps[n]()
            prob = jnp.exp2(scores[buf][k * TOK : k * TOK + TOK, :] - m).astype(BF16)
            part = jnp.dot(qkv[k, 2 * ROWS : 3 * ROWS, :], prob, preferred_element_type=F32)
            acc = part if acc is None else acc + part
        if not last:
            top_all[slot] = m
            acc_all[slot] = acc
            return
        out = acc[0:HEAD] / acc[HEAD : HEAD + 1]
        ostage[slot] = jnp.concatenate([out, zero8], axis=0).astype(BF16)
        if odd:
            out_copy(slot, odd).start()
        else:
            @pl.when(slot > 0)
            def _():
                out_copy(slot, odd).start()

            @pl.when(slot == 0)
            def _():
                attn[head] = ostage[slot]

    def attend(q0, q1, k0, k1, first, last):
        keys = list(range(k0, k1))
        for step in score_steps(q1 - 2, 0, keys):
            step()
        if q1 - q0 == 2:
            job(q0, False, 0, keys, first, last, q0 + 1)
            job(q0 + 1, True, 1, keys, first, last, None)
            return

        def two(i, c):
            slot = q1 - 2 - 2 * i
            job(slot, False, 0, keys, first, last, slot + 1)
            job(slot + 1, True, 1, keys, first, last, jnp.maximum(slot - 2, q0))
            return c

        lax.fori_loop(0, (q1 - q0) // 2, two, 0)

    z_forward(0)

    def take_sel(i, c):
        peer = lax.rem(f + i, 16)
        remote(wsel, wsel_all.at[peer], ss.at[i], sr.at[peer], peer, p).wait()
        return c

    wsel_all[f] = wsel[...]
    lax.fori_loop(1, 16, take_sel, 0)
    for j in range(8):
        a = wsel_all[2 * j, 0:72, :].astype(F32)
        b = wsel_all[2 * j + 1, 0:72, :].astype(F32)
        wc[144 * j : 144 * j + 144, :] = jnp.concatenate([a, b], axis=0).astype(BF16)

    project(0)
    project(1)
    project(2)
    receive(0)
    attend(0, 2, 0, 2, True, False)
    z_forward(1)
    keep.wait()
    core_send(y, 0).start()
    across_in.wait()
    y_send(0, 1).start()
    y_send(1, 1).start()
    core_send(y, 1).start()
    project(3)
    project(4)
    y_in(0, 0).wait_recv()
    y_pass(0).start()
    core_send(y_prev, 0).start()
    y_in(1, 0).wait_recv()
    core_send(y_next, 0).start()
    receive(1)
    receive(2)
    attend(0, 2, 2, 6, False, False)
    attend(2, 6, 0, 6, True, False)
    z_forward(2)
    project(5)
    project(6)
    receive(3)
    receive(4)
    attend(0, 6, 6, 10, False, False)
    attend(6, 10, 0, 10, True, False)
    z_forward(3)
    project(7)
    y_in(1, 1).wait_recv()
    y_pass(1).start()
    core_send(y_next, 1).start()
    y_in(0, 1).wait_recv()
    core_send(y_prev, 1).start()
    receive(5)
    receive(6)
    attend(0, 10, 10, 14, False, False)
    attend(10, 14, 0, 14, True, False)
    receive(7)
    attend(14, 16, 0, 16, True, True)
    attend(0, 14, 14, 16, False, True)

    y_pass_in(0).wait_recv()
    core_send(y_far, 0).start()
    y_pass_in(1).wait_recv()
    core_send(y_far, 1).start()
    for step in range(4):
        for way in range(2):
            for sub in range(2):
                if sends(step, way, sub):
                    z_copy(step, way, sub).wait_send()

    for slot in range(1, 16):
        src = dest_of(slot, slot % 2 == 1)
        src_head = 2 * lax.rem(src, 8) + src // 8
        out_copy(slot, slot % 2 == 1).wait_send()
        remote(
            ostage.at[slot], attn.at[src_head], os.at[slot], orr.at[src_head], f, src
        ).wait_recv()
    for way in range(2):
        for kind in range(2):
            y_send(way, kind).wait_send()
        y_pass(way).wait_send()
    for at_y in (y, y_prev, y_next, y_far):
        for kind in range(2):
            core_send(at_y, kind).wait_send()
            core_in(chip_of(at_y, kind)).wait_recv()


def temporal_kernel(
    hid, mod, attn, wfull, out,
    w, at32, mid, midt, proj, qkv, acc, osend,
    wsem, ms, mr, bs, br,
):
    f = lax.axis_index("frame")
    p = lax.axis_index("patch")
    load0 = pltpu.make_async_copy(wfull.at[0], w.at[0], wsem.at[0])
    load1 = pltpu.make_async_copy(wfull.at[1], w.at[1], wsem.at[1])
    load0.start()
    load1.start()
    barrier = pltpu.get_barrier_semaphore()

    def greet(i, c):
        signal(barrier, lax.rem(f + i, 16), p)
        return c

    lax.fori_loop(1, 16, greet, 0)

    for h in range(HEADS):
        at32[HEAD * h : HEAD * h + HEAD, :] = attn[h, 0:HEAD, :].astype(F32)
    for j in range(9):
        proj[:, 128 * j : 128 * j + 128] = at32[128 * j : 128 * j + 128, :].T.astype(BF16)
    load0.wait()
    r = jnp.dot(proj[...], w[0, :, 0:D], preferred_element_type=F32)
    mid[...] = (hid[...].astype(F32) + mod[2:3] * r).astype(BF16)
    pl.semaphore_wait(barrier, 15)

    def rows16(ref, n):
        return ref.at[pl.ds(pl.multiple_of(16 * n, 16), 16)]

    def send_mid(i, c):
        peer = lax.rem(f + i, 16)
        remote(rows16(mid, peer), rows16(midt, f), ms.at[i], mr.at[f], peer, p).start()
        return c

    lax.fori_loop(1, 16, send_mid, 0)
    here = pl.ds(pl.multiple_of(16 * f, 16), 16)
    midt[here, :] = mid[here, :]
    load1.wait()

    def take_mid(i, c):
        peer = lax.rem(f + i, 16)
        remote(rows16(mid, peer), rows16(midt, peer), ms.at[i], mr.at[peer], peer, p).wait()
        return c

    lax.fori_loop(1, 16, take_mid, 0)
    proj[...] = norm_modulate(midt[...].astype(F32), mod[3:4], mod[4:5]).astype(BF16)
    a = jnp.dot(proj[...], w[0, :, D:HALF], preferred_element_type=F32)
    qkv[:, 0:D] = (a[:, 0:D] * Q_SCALE).astype(BF16)
    qkv[:, D : HALF - D] = a[:, D:].astype(BF16)
    b = jnp.dot(proj[...], w[1, :, 0 : 4 * D - HALF], preferred_element_type=F32)
    qkv[:, HALF - D : 3 * D] = b.astype(BF16)

    ri = lax.broadcasted_iota(jnp.int32, (TOK, TOK), 0)
    ci = lax.broadcasted_iota(jnp.int32, (TOK, TOK), 1)
    same = lax.rem(ri, 16) == lax.rem(ci, 16)
    lane = lax.broadcasted_iota(jnp.int32, (TOK, TOK), 1)
    acc[...] = jnp.zeros_like(acc)
    for h in range(HEADS):
        start = 128 * min(HEAD * h // 128, 7)
        low = HEAD * h - start
        inside = (lane >= low) & (lane < low + HEAD)
        q = qkv[:, start : start + 256]
        q = jnp.where(inside, q, jnp.zeros_like(q))
        k = qkv[:, D + start : D + start + 256]
        v = qkv[:, 2 * D + start : 2 * D + start + 256]
        s = lax.dot_general(q, k, (((1,), (1,)), ((), ())), preferred_element_type=F32)
        s = jnp.where(same, s, -1e30)
        prob = jnp.exp2(s - jnp.max(s, axis=1, keepdims=True))
        total = jnp.sum(prob, axis=1, keepdims=True)
        o = jnp.dot(prob.astype(BF16), v, preferred_element_type=F32) / total
        acc[:, start : start + 256] = jnp.where(inside, o, acc[:, start : start + 256])
    r = jnp.dot(
        acc[...].astype(BF16), w[1, :, 4 * D - HALF : 5 * D - HALF], preferred_element_type=F32
    )
    osend[...] = (midt[...].astype(F32) + mod[5:6] * r).astype(BF16)

    def send_out(i, c):
        peer = lax.rem(f + i, 16)
        remote(rows16(osend, peer), rows16(out, f), bs.at[i], br.at[f], peer, p).start()
        return c

    lax.fori_loop(1, 16, send_out, 0)
    out[here, :] = osend[here, :]

    def take_out(i, c):
        peer = lax.rem(f + i, 16)
        remote(rows16(osend, peer), rows16(out, peer), bs.at[i], br.at[peer], peer, p).wait()
        return c

    lax.fori_loop(1, 16, take_out, 0)


VMEM = pl.BlockSpec(memory_space=pltpu.VMEM)
ANY = pl.BlockSpec(memory_space=pl.ANY)
LIMIT = 60 * 1024 * 1024


def spatial_call(hid, mod, wsel, wrest):
    dma = pltpu.SemaphoreType.DMA
    return pl.pallas_call(
        spatial_kernel,
        out_shape=(
            jax.ShapeDtypeStruct((HEADS, ROWS, TOK), BF16),
            jax.ShapeDtypeStruct((2, D, HALF), BF16),
        ),
        in_specs=[VMEM] * 4,
        out_specs=(VMEM, ANY),
        scratch_shapes=[
            pltpu.VMEM((8, TOK, D), BF16),
            pltpu.VMEM((16, ROWS, 512), BF16),
            pltpu.VMEM((D, 512), BF16),
            pltpu.VMEM((16, 3 * ROWS, TOK), BF16),
            pltpu.VMEM((8, 3 * ROWS, TOK), BF16),
            pltpu.VMEM((4096, 128), BF16),
            pltpu.VMEM((16, ROWS, TOK), BF16),
            pltpu.VMEM((ROWS, HALF), BF16),
            pltpu.VMEM((144, HALF), BF16),
            pltpu.VMEM((4096, TOK), F32),
            pltpu.VMEM((4096, TOK), F32),
            pltpu.VMEM((8, TOK), F32),
            pltpu.VMEM((8, TOK), F32),
            pltpu.VMEM((16, 1, TOK), F32),
            pltpu.VMEM((16, ROWS, TOK), F32),
            dma((16,)), dma((16,)),
            dma((16,)), dma((16,)),
            dma((8,)), dma((8,)),
            dma((16,)), dma((16,)),
            dma((17,)), dma((17,)),
        ],
        compiler_params=pltpu.CompilerParams(
            collective_id=0, has_side_effects=True, vmem_limit_bytes=LIMIT
        ),
        name="spatial",
    )(hid, mod, wsel, wrest)


def temporal_call(hid, mod, attn, wfull):
    dma = pltpu.SemaphoreType.DMA
    return pl.pallas_call(
        temporal_kernel,
        out_shape=jax.ShapeDtypeStruct((TOK, D), BF16),
        in_specs=[VMEM, VMEM, VMEM, ANY],
        out_specs=VMEM,
        scratch_shapes=[
            pltpu.VMEM((2, D, HALF), BF16),
            pltpu.VMEM((D, TOK), F32),
            pltpu.VMEM((TOK, D), BF16),
            pltpu.VMEM((TOK, D), BF16),
            pltpu.VMEM((TOK, D), BF16),
            pltpu.VMEM((TOK, 3 * D), BF16),
            pltpu.VMEM((TOK, D), F32),
            pltpu.VMEM((TOK, D), BF16),
            dma((2,)),
            dma((16,)), dma((16,)),
            dma((16,)), dma((16,)),
        ],
        compiler_params=pltpu.CompilerParams(
            collective_id=1, has_side_effects=True, vmem_limit_bytes=LIMIT
        ),
        name="temporal",
    )(hid, mod, attn, wfull)


def body(hidden_states, modulation, w_qkv_spatial, w_out_spatial, w_qkv_temporal, w_out_temporal):
    p = lax.axis_index("patch")
    z = lax.rem(p, 8)
    hid = hidden_states.reshape(TOK, D)
    parts = [
        lax.dynamic_slice_in_dim(w_qkv_spatial, D * part + 2 * HEAD * z, 2 * HEAD, axis=1)
        for part in range(3)
    ]
    wsel = jnp.pad(jnp.concatenate(parts, axis=1), ((0, ROWS - HEAD), (0, 512 - 6 * HEAD)))
    rest = jnp.concatenate([w_out_spatial, w_qkv_temporal, w_out_temporal], axis=1)
    rest = jnp.pad(rest, ((0, ROWS - HEAD), (0, 2 * HALF - 5 * D)))
    rest = jnp.stack([rest[:, :HALF], rest[:, HALF:]])
    attn, wfull = spatial_call(hid, modulation, wsel, rest)
    out = temporal_call(hid, modulation, attn, wfull)
    return out.reshape(1, TOK, D)


def solution(mesh):
    in_specs = (
        P("frame", "patch", None),
        P(),
        P("frame", None),
        P("frame", None),
        P("frame", None),
        P("frame", None),
    )
    out_specs = P("frame", "patch", None)
    return jax.shard_map(body, mesh=mesh, in_specs=in_specs, out_specs=out_specs, check_vma=False)
```

```python
import math

import jax
import jax.numpy as jnp
from jax import lax
from jax.experimental import pallas as pl
from jax.experimental.pallas import tpu as pltpu
from jax.sharding import PartitionSpec as P

HEAD = 72
HEADS = 16
D = 1152
TOK = 256
ROWS = 80
HALF = 2944
Q_SCALE = HEAD ** (-0.5) * math.log2(math.e)
F32 = jnp.float32
BF16 = jnp.bfloat16


def remote(src, dst, send, recv, frame, patch):
    return pltpu.make_async_remote_copy(
        src_ref=src,
        dst_ref=dst,
        send_sem=send,
        recv_sem=recv,
        device_id={"frame": frame, "patch": patch},
        device_id_type=pl.DeviceIdType.MESH,
    )


def signal(sem, frame, patch):
    pl.semaphore_signal(
        sem, inc=1, device_id={"frame": frame, "patch": patch}, device_id_type=pl.DeviceIdType.MESH
    )


def norm_modulate(x, shift, scale):
    centred = x - jnp.mean(x, axis=-1, keepdims=True)
    variance = jnp.mean(centred * centred, axis=-1, keepdims=True)
    return centred * lax.rsqrt(variance + 1e-06) * (1.0 + scale) + shift


def block_kernel(
    hid, mod, wsel, wrest, out,
    nz, wsel_all, wc, qkv, stage, kn, ostage, attn, w1, w, score_a, score_b, top_a, top_b, top_all, acc_all,
    at32, mid, midt, proj, qkv_t, acc_t, osend,
    zs, zr, ss, sr, xs, xr, os, orr, ws, wr, ms, mr, bs, br,
):
    f = lax.axis_index("frame")
    p = lax.axis_index("patch")
    core = lax.rem(f, 2)
    x_hi = lax.rem(f // 2, 2)
    y = f // 4
    x_lo = p // 8
    z = lax.rem(p, 8)
    chip = f // 2
    other_core = f + 1 - 2 * core
    cross_f = (y * 2 + 1 - x_hi) * 2 + core
    x_pair = (1 - x_lo) * 8 + z
    y_up = lax.rem(y + 1, 4) * 4 + x_hi * 2 + core
    y_dn = lax.rem(y + 3, 4) * 4 + x_hi * 2 + core
    z_up = x_lo * 8 + lax.rem(z + 1, 8)
    z_dn = x_lo * 8 + lax.rem(z + 7, 8)

    barrier = pltpu.get_barrier_semaphore()

    def greet(i, c):
        signal(barrier, lax.rem(f + i, 16), p)
        signal(barrier, f, lax.rem(p + i, 16))
        return c

    lax.fori_loop(1, 16, greet, 0)
    signal(barrier, cross_f, x_pair)
    nz[0] = norm_modulate(hid[...].astype(F32), mod[0:1], mod[1:2]).astype(BF16)
    pl.semaphore_wait(barrier, 31)

    def z_block(g, way):
        return nz.at[g, pl.ds(128 * way, 128)]

    def z_hop(g, way):
        if g <= 2:
            source = nz.at[0, pl.ds(128 * (g - 1), 128)]
        elif g <= 6:
            source = z_block(g - 2, way)
        else:
            source = z_block(5 + way, way)
        n = 2 * g + way
        return remote(source, z_block(g, way), zs.at[n], zr.at[n], f, z_dn if way else z_up)

    for g in (1, 2):
        for way in range(2):
            z_hop(g, way).start()

    def arrive(g):
        for way in range(2):
            z_hop(g, way).wait_recv()
            if g <= 4:
                z_hop(g + 2, way).start()
            elif g == 5 + way:
                z_hop(7, way).start()

    first = remote(wrest.at[1 - core], w1, ws.at[0], wr.at[0], other_core, p)
    first.start()

    def sel_copy(source, peer, n):
        return remote(source, wsel_all.at[n], ss.at[n], sr.at[n], peer, p)

    sel_copy(wsel, other_core, f).start()

    def sel_send(i, c):
        peer = lax.rem(f + 2 * i, 16)
        remote(wsel, wsel_all.at[f], ss.at[peer], sr.at[f], peer, p).start()
        return c

    lax.fori_loop(1, 8, sel_send, 0)
    wsel_all[f] = wsel[...]

    first.wait()
    mine = wrest[core, 0:72, :].astype(F32)
    theirs = w1[0:72, :].astype(F32)
    is_first = core == 0
    low = jnp.where(is_first, mine, theirs)
    high = jnp.where(is_first, theirs, mine)
    w[core, pl.ds(pl.multiple_of(144 * chip, 144), 144), :] = jnp.concatenate(
        [low, high], axis=0
    ).astype(BF16)

    def chip_of(at_y, kind):
        return 2 * at_y + (x_hi if kind == 0 else 1 - x_hi)

    def rows(half, n, start, size):
        return w.at[half, pl.ds(pl.multiple_of(144 * n + start, 16), size)]

    y_prev = lax.rem(y + 3, 4)
    y_next = lax.rem(y + 1, 4)
    y_far = lax.rem(y + 2, 4)

    def cross_send(far):
        block = rows(core, chip_of(y_far if far else y, 0), 0, 144)
        return remote(block, block, ws.at[1 + far], wr.at[1 + far], cross_f, x_pair)

    def y_send(way, kind):
        n = 3 + way * 2 + kind
        block = rows(core, chip_of(y, kind), 0, 144)
        return remote(block, block, ws.at[n], wr.at[n], y_dn if way else y_up, p)

    def y_pass(way):
        block = rows(core, chip_of(y_next if way else y_prev, 0), 80 * way, 64 if way else 80)
        return remote(block, block, ws.at[7 + way], wr.at[7 + way], y_dn if way else y_up, p)

    def core_send(at_y, kind):
        n = chip_of(at_y, kind)
        block = rows(core, n, 0, 144)
        return remote(block, block, ws.at[9 + n], wr.at[9 + n], other_core, p)

    cross_send(0).start()
    for way in range(2):
        y_send(way, 0).start()
    core_send(y, 0).start()

    zero8 = jnp.zeros((8, TOK), F32)
    ones8 = jnp.where(lax.broadcasted_iota(jnp.int32, (8, TOK), 0) == 0, 1.0, 0.0)
    lower = x_lo == 0

    def to_natural(slot):
        kt = qkv[slot, ROWS : 2 * ROWS, :].astype(F32)
        kt = jnp.concatenate([kt, jnp.zeros((128 - ROWS, TOK), F32)], axis=0)
        kn[slot * TOK : slot * TOK + TOK, :] = kt.T.astype(BF16)

    def pair_copy(g):
        return remote(stage.at[g], qkv.at[2 * g + 1], xs.at[g], xr.at[g], f, x_pair)

    def project(g):
        r = jnp.dot(nz[g], wc[...], preferred_element_type=F32)
        t = r.T
        own, oth = [], []
        for part in range(3):
            one = t[144 * part : 144 * part + 72]
            two = t[144 * part + 72 : 144 * part + 144]
            if part == 0:
                one, two = one * Q_SCALE, two * Q_SCALE
            own += [jnp.where(lower, one, two), ones8 if part == 2 else zero8]
            oth += [jnp.where(lower, two, one), ones8 if part == 2 else zero8]
        stage[g] = jnp.concatenate(oth, axis=0).astype(BF16)
        pair_copy(g).start()
        qkv[2 * g] = jnp.concatenate(own, axis=0).astype(BF16)
        to_natural(2 * g)

    def receive(g):
        pair_copy(g).wait()
        to_natural(2 * g + 1)

    head = 2 * z + x_lo
    scores = (score_a, score_b)
    tops = (top_a, top_b)
    top_all[...] = jnp.full(top_all.shape, -1e30, F32)
    acc_all[...] = jnp.zeros(acc_all.shape, F32)

    def out_copy(g, odd, half):
        s = (g + 1) // 2
        if isinstance(g, int):
            j = half if g in (0, 7) else (g + 1) % 2
        else:
            j = lax.rem(g + 1, 2)
        to = (1 - x_lo if odd else x_lo) * 8 + lax.rem(z + (s if half else 8 - s), 8)
        n = 2 * odd + half
        return remote(
            ostage.at[g, n], attn.at[head, j], os.at[4 * g + n], orr.at[2 * head + j], f, to
        )

    def score_steps(gq, gk, buf):
        q_t = jnp.concatenate([qkv[2 * gq, 0:ROWS, :], qkv[2 * gq + 1, 0:ROWS, :]], axis=1)
        state = [None]

        def one(u):
            at = pl.ds(pl.multiple_of(2 * TOK * gk + TOK * u, TOK), TOK)
            s = jnp.dot(kn[at, 0:ROWS], q_t, preferred_element_type=F32)
            scores[buf][TOK * u : TOK * u + TOK, :] = s
            m = jnp.max(s.reshape(TOK // 8, 8, 2 * TOK), axis=0)
            state[0] = m if state[0] is None else jnp.maximum(state[0], m)
            if u == 1:
                tops[buf][...] = state[0]

        return [lambda: one(0), lambda: one(1)]

    def job(gq, gk, buf, following, last):
        steps = score_steps(*following, 1 - buf) if following else None
        old = top_all[gq]
        m = jnp.maximum(old, jnp.max(tops[buf][...], axis=0, keepdims=True))
        acc = acc_all[gq] * jnp.exp2(old - m)
        for u in range(2):
            if steps:
                steps[u]()
            prob = jnp.exp2(scores[buf][TOK * u : TOK * u + TOK, :] - m).astype(BF16)
            acc += jnp.dot(
                qkv[2 * gk + u, 2 * ROWS : 3 * ROWS, :], prob, preferred_element_type=F32
            )
        if not last:
            top_all[gq] = m
            acc_all[gq] = acc
            return
        o = acc[0:HEAD] / acc[HEAD : HEAD + 1]
        o = jnp.concatenate([o, jnp.zeros((8, 2 * TOK), F32)], axis=0).astype(BF16)
        for odd in range(2):
            for half in range(2):
                n = 2 * odd + half
                ostage[gq, n] = o[:, 128 * n : 128 * n + 128]
                if isinstance(gq, int) and gq == 0 and odd == 0:
                    attn[head, half] = ostage[gq, n]
                else:
                    out_copy(gq, odd, half).start()

    def jobs(pick, count, last):
        for step in score_steps(*pick(0), 0):
            step()
        rest = 1 if count % 2 else 2

        def two(i, c):
            job(*pick(2 * i), 0, pick(2 * i + 1), last == "all")
            job(*pick(2 * i + 1), 1, pick(2 * i + 2), last == "all")
            return c

        if count > rest:
            lax.fori_loop(0, (count - rest) // 2, two, 0)
        for t in range(count - rest, count):
            following = pick(t + 1) if t + 1 < count else None
            end = last == "all" or (last == "end" and t == count - 1)
            job(*pick(t), (t - count + rest) % 2, following, end)

    def group_jobs(g):
        def pick(t):
            if isinstance(t, int):
                return (t, g) if t < g else (g, t - g)
            return jnp.where(t < g, t, g), jnp.where(t < g, g, t - g)

        jobs(pick, 2 * g + 1, "")

    arrive(1)

    def sel_take(i, c):
        peer = lax.rem(f + 2 * i, 16)
        sel_copy(wsel, peer, peer).wait_recv()
        remote(
            wsel_all.at[peer], wsel_all.at[peer], ss.at[peer + 1 - 2 * core], sr.at[peer], other_core, p
        ).start()
        return c

    lax.fori_loop(1, 8, sel_take, 0)

    def sel_swapped(i, c):
        n = lax.rem(other_core + 2 * i, 16)
        sel_copy(wsel, other_core, n).wait_recv()
        return c

    lax.fori_loop(0, 8, sel_swapped, 0)
    for j in range(8):
        a = wsel_all[2 * j, 0:72, :].astype(F32)
        b = wsel_all[2 * j + 1, 0:72, :].astype(F32)
        wc[144 * j : 144 * j + 144, :] = jnp.concatenate([a, b], axis=0).astype(BF16)
    project(0)
    project(1)
    arrive(2)
    project(2)
    receive(0)
    receive(1)
    group_jobs(0)
    group_jobs(1)
    arrive(3)
    project(3)
    receive(2)
    group_jobs(2)
    arrive(4)
    cross_send(0).wait_recv()
    for way in range(2):
        y_send(way, 0).wait_recv()
        y_pass(way).start()
    for way in range(2):
        y_send(way, 1).start()
    core_send(y, 1).start()
    core_send(y_prev, 0).start()
    core_send(y_next, 0).start()
    project(4)
    receive(3)
    group_jobs(3)
    arrive(5)
    project(5)
    receive(4)
    group_jobs(4)
    arrive(6)
    far = [rows(core, chip_of(y_far, 0), 80 * way, 64 if way else 80) for way in range(2)]
    for way in range(2):
        remote(far[way], far[way], ws.at[7 + way], wr.at[7 + way], other_core, p).wait_recv()
    cross_send(1).start()
    core_send(y_far, 0).start()
    project(6)
    receive(5)
    group_jobs(5)
    arrive(7)
    project(7)
    receive(6)
    group_jobs(6)
    receive(7)
    jobs(lambda t: (6 - t, 7), 7, "all")
    jobs(lambda t: (7, t), 8, "end")

    for way in range(2):
        y_send(way, 1).wait_recv()
    core_send(y_prev, 1).start()
    core_send(y_next, 1).start()
    cross_send(1).wait_recv()
    core_send(y_far, 1).start()

    def out_take(i, c):
        src = lax.rem(p + i, 16)
        n = 2 * (2 * lax.rem(src, 8) + src // 8)
        for j in range(2):
            here = attn.at[n // 2, j]
            remote(ostage.at[0, 0], here, os.at[0], orr.at[n + j], f, src).wait_recv()
        return c

    lax.fori_loop(1, 16, out_take, 0)
    for h in range(HEADS):
        at32[HEAD * h : HEAD * h + HEAD, :] = jnp.concatenate(
            [attn[h, 0, 0:HEAD, :], attn[h, 1, 0:HEAD, :]], axis=1
        ).astype(F32)
    for j in range(9):
        proj[:, 128 * j : 128 * j + 128] = at32[128 * j : 128 * j + 128, :].T.astype(BF16)

    for at_y in (y, y_prev, y_next, y_far):
        for kind in range(2):
            n = chip_of(at_y, kind)
            block = rows(1 - core, n, 0, 144)
            remote(block, block, ws.at[9 + n], wr.at[9 + n], other_core, p).wait_recv()

    r = jnp.dot(proj[...], w[0, :, 0:D], preferred_element_type=F32)
    mid[...] = (hid[...].astype(F32) + mod[2:3] * r).astype(BF16)

    def rows16(ref, n):
        return ref.at[pl.ds(pl.multiple_of(16 * n, 16), 16)]

    def send_mid(i, c):
        peer = lax.rem(f + i, 16)
        remote(rows16(mid, peer), rows16(midt, f), ms.at[i], mr.at[f], peer, p).start()
        return c

    lax.fori_loop(1, 16, send_mid, 0)
    here = pl.ds(pl.multiple_of(16 * f, 16), 16)
    midt[here, :] = mid[here, :]

    for g in range(1, 8):
        for way in range(2):
            z_hop(g, way).wait_send()

    def sel_sent(i, c):
        sel_copy(wsel, other_core, lax.rem(f + 2 * i, 16)).wait_send()
        sel_copy(wsel, other_core, lax.rem(other_core + 2 * i, 16)).wait_send()
        return c

    lax.fori_loop(1, 8, sel_sent, 0)
    sel_copy(wsel, other_core, f).wait_send()

    def out_sent(n, c):
        remote(ostage.at[0, 0], attn.at[0, 0], os.at[n], orr.at[0], f, x_pair).wait_send()
        return c

    lax.fori_loop(2, 32, out_sent, 0)
    for way in range(2):
        cross_send(way).wait_send()
        y_pass(way).wait_send()
        for kind in range(2):
            y_send(way, kind).wait_send()
    for at_y in (y, y_prev, y_next, y_far):
        for kind in range(2):
            core_send(at_y, kind).wait_send()

    def take_mid(i, c):
        peer = lax.rem(f + i, 16)
        remote(rows16(mid, peer), rows16(midt, peer), ms.at[i], mr.at[peer], peer, p).wait()
        return c

    lax.fori_loop(1, 16, take_mid, 0)
    proj[...] = norm_modulate(midt[...].astype(F32), mod[3:4], mod[4:5]).astype(BF16)
    a = jnp.dot(proj[...], w[0, :, D:HALF], preferred_element_type=F32)
    qkv_t[:, 0:D] = (a[:, 0:D] * Q_SCALE).astype(BF16)
    qkv_t[:, D : HALF - D] = a[:, D:].astype(BF16)
    b = jnp.dot(proj[...], w[1, :, 0 : 4 * D - HALF], preferred_element_type=F32)
    qkv_t[:, HALF - D : 3 * D] = b.astype(BF16)

    ri = lax.broadcasted_iota(jnp.int32, (TOK, TOK), 0)
    ci = lax.broadcasted_iota(jnp.int32, (TOK, TOK), 1)
    same = lax.rem(ri, 16) == lax.rem(ci, 16)
    acc_t[...] = jnp.zeros_like(acc_t)
    for h in range(HEADS):
        start = 128 * min(HEAD * h // 128, 7)
        low = HEAD * h - start
        inside = (ci >= low) & (ci < low + HEAD)
        q = qkv_t[:, start : start + 256]
        q = jnp.where(inside, q, jnp.zeros_like(q))
        k = qkv_t[:, D + start : D + start + 256]
        v = qkv_t[:, 2 * D + start : 2 * D + start + 256]
        s = lax.dot_general(q, k, (((1,), (1,)), ((), ())), preferred_element_type=F32)
        s = jnp.where(same, s, -1e30)
        prob = jnp.exp2(s - jnp.max(s, axis=1, keepdims=True))
        total = jnp.sum(prob, axis=1, keepdims=True)
        o = jnp.dot(prob.astype(BF16), v, preferred_element_type=F32) / total
        acc_t[:, start : start + 256] = jnp.where(inside, o, acc_t[:, start : start + 256])
    r = jnp.dot(
        acc_t[...].astype(BF16), w[1, :, 4 * D - HALF : 5 * D - HALF], preferred_element_type=F32
    )
    osend[...] = (midt[...].astype(F32) + mod[5:6] * r).astype(BF16)

    def send_out(i, c):
        peer = lax.rem(f + i, 16)
        remote(rows16(osend, peer), rows16(out, f), bs.at[i], br.at[f], peer, p).start()
        return c

    lax.fori_loop(1, 16, send_out, 0)
    out[here, :] = osend[here, :]

    def take_out(i, c):
        peer = lax.rem(f + i, 16)
        remote(rows16(osend, peer), rows16(out, peer), bs.at[i], br.at[peer], peer, p).wait()
        return c

    lax.fori_loop(1, 16, take_out, 0)


VMEM = pl.BlockSpec(memory_space=pltpu.VMEM)


def block_call(hid, mod, wsel, wrest):
    dma = pltpu.SemaphoreType.DMA
    return pl.pallas_call(
        block_kernel,
        out_shape=jax.ShapeDtypeStruct((TOK, D), BF16),
        in_specs=[VMEM] * 4,
        out_specs=VMEM,
        scratch_shapes=[
            pltpu.VMEM((8, TOK, D), BF16),
            pltpu.VMEM((16, ROWS, 512), BF16),
            pltpu.VMEM((D, 512), BF16),
            pltpu.VMEM((16, 3 * ROWS, TOK), BF16),
            pltpu.VMEM((8, 3 * ROWS, TOK), BF16),
            pltpu.VMEM((4096, 128), BF16),
            pltpu.VMEM((8, 4, ROWS, 128), BF16),
            pltpu.VMEM((HEADS, 2, ROWS, 128), BF16),
            pltpu.VMEM((ROWS, HALF), BF16),
            pltpu.VMEM((2, D, HALF), BF16),
            pltpu.VMEM((2 * TOK, 2 * TOK), F32),
            pltpu.VMEM((2 * TOK, 2 * TOK), F32),
            pltpu.VMEM((8, 2 * TOK), F32),
            pltpu.VMEM((8, 2 * TOK), F32),
            pltpu.VMEM((8, 1, 2 * TOK), F32),
            pltpu.VMEM((8, ROWS, 2 * TOK), F32),
            pltpu.VMEM((D, TOK), F32),
            pltpu.VMEM((TOK, D), BF16),
            pltpu.VMEM((TOK, D), BF16),
            pltpu.VMEM((TOK, D), BF16),
            pltpu.VMEM((TOK, 3 * D), BF16),
            pltpu.VMEM((TOK, D), F32),
            pltpu.VMEM((TOK, D), BF16),
            dma((16,)), dma((16,)),
            dma((16,)), dma((16,)),
            dma((8,)), dma((8,)),
            dma((32,)), dma((32,)),
            dma((17,)), dma((17,)),
            dma((16,)), dma((16,)),
            dma((16,)), dma((16,)),
        ],
        compiler_params=pltpu.CompilerParams(
            collective_id=0, has_side_effects=True, vmem_limit_bytes=60 * 1024 * 1024
        ),
        name="block",
    )(hid, mod, wsel, wrest)


def body(hidden_states, modulation, w_qkv_spatial, w_out_spatial, w_qkv_temporal, w_out_temporal):
    p = lax.axis_index("patch")
    z = lax.rem(p, 8)
    hid = hidden_states.reshape(TOK, D)
    parts = [
        lax.dynamic_slice_in_dim(w_qkv_spatial, D * part + 2 * HEAD * z, 2 * HEAD, axis=1)
        for part in range(3)
    ]
    wsel = jnp.pad(jnp.concatenate(parts, axis=1), ((0, ROWS - HEAD), (0, 512 - 6 * HEAD)))
    rest = jnp.concatenate([w_out_spatial, w_qkv_temporal, w_out_temporal], axis=1)
    rest = jnp.pad(rest, ((0, ROWS - HEAD), (0, 2 * HALF - 5 * D)))
    rest = jnp.stack([rest[:, :HALF], rest[:, HALF:]])
    out = block_call(hid, modulation, wsel, rest)
    return out.reshape(1, TOK, D)


def solution(mesh):
    in_specs = (
        P("frame", "patch", None),
        P(),
        P("frame", None),
        P("frame", None),
        P("frame", None),
        P("frame", None),
    )
    out_specs = P("frame", "patch", None)
    return jax.shard_map(body, mesh=mesh, in_specs=in_specs, out_specs=out_specs, check_vma=False)
```

```python
import math

import jax
import jax.numpy as jnp
from jax import lax
from jax.experimental import pallas as pl
from jax.experimental.pallas import tpu as pltpu
from jax.sharding import PartitionSpec as P

HEAD = 72
HEADS = 16
D = 1152
TOK = 256
ROWS = 80
HALF = 2944
Q_SCALE = HEAD ** (-0.5) * math.log2(math.e)
F32 = jnp.float32
BF16 = jnp.bfloat16


def remote(src, dst, send, recv, frame, patch):
    return pltpu.make_async_remote_copy(
        src_ref=src,
        dst_ref=dst,
        send_sem=send,
        recv_sem=recv,
        device_id={"frame": frame, "patch": patch},
        device_id_type=pl.DeviceIdType.MESH,
    )


def signal(sem, frame, patch):
    pl.semaphore_signal(
        sem, inc=1, device_id={"frame": frame, "patch": patch}, device_id_type=pl.DeviceIdType.MESH
    )


def norm_modulate(x, shift, scale):
    centred = x - jnp.mean(x, axis=-1, keepdims=True)
    variance = jnp.mean(centred * centred, axis=-1, keepdims=True)
    return centred * lax.rsqrt(variance + 1e-06) * (1.0 + scale) + shift


def block_kernel(
    hid, mod, w_qkv_s, w_out_s, w_qkv_t, w_out_t, out,
    nz, wsel, wrest, wo, wsel_all, wc, qkv, stage, kn, ostage, attn, w1, w, score_a, score_b, top_a, top_b, top_all, acc_all,
    mid, midt, proj, qkv_t, acc_t, osend,
    zs, zr, ss, sr, xs, xr, os, orr, ws, wr, ms, mr, bs, br,
):
    f = lax.axis_index("frame")
    p = lax.axis_index("patch")
    core = lax.rem(f, 2)
    x_hi = lax.rem(f // 2, 2)
    y = f // 4
    x_lo = p // 8
    z = lax.rem(p, 8)
    chip = f // 2
    other_core = f + 1 - 2 * core
    cross_f = (y * 2 + 1 - x_hi) * 2 + core
    x_pair = (1 - x_lo) * 8 + z
    y_up = lax.rem(y + 1, 4) * 4 + x_hi * 2 + core
    y_dn = lax.rem(y + 3, 4) * 4 + x_hi * 2 + core
    z_up = x_lo * 8 + lax.rem(z + 1, 8)
    z_dn = x_lo * 8 + lax.rem(z + 7, 8)

    barrier = pltpu.get_barrier_semaphore()

    def greet(i, c):
        signal(barrier, lax.rem(f + i, 16), p)
        signal(barrier, f, lax.rem(p + i, 16))
        return c

    lax.fori_loop(1, 16, greet, 0)
    signal(barrier, cross_f, x_pair)
    nz[0] = norm_modulate(hid[...].astype(F32), mod[0:1], mod[1:2]).astype(BF16)

    lanes = lax.broadcasted_iota(jnp.int32, (HEAD, TOK), 1)
    parts = []
    for part in range(3):
        at = pl.ds(pl.multiple_of(D * part + 128 * z, 128), TOK)
        window = w_qkv_s[:, at].astype(F32)
        window = pltpu.roll(window, lax.rem(TOK - 16 * z + 16 * part, TOK), axis=1)
        inside = (lanes >= 16 * part) & (lanes < 16 * part + 2 * HEAD)
        parts.append(jnp.where(inside, window, 0.0))
    q, k, v = parts
    sel = jnp.concatenate(
        [q[:, 0:128], q[:, 128:] + k[:, 0:128], k[:, 128:] + v[:, 0:128], v[:, 128:]], axis=1
    )

    def to_rows(value):
        tail = jnp.zeros((ROWS - HEAD, value.shape[1]), F32)
        return jnp.concatenate([value.astype(F32), tail], axis=0).astype(BF16)

    wsel[...] = to_rows(sel)
    cut = HALF - D
    wrest[0, :, 0:D] = to_rows(w_out_s[...])
    wrest[0, :, D:HALF] = to_rows(w_qkv_t[:, 0:cut])
    wrest[1, :, 0 : 3 * D - cut] = to_rows(w_qkv_t[:, cut:])
    wrest[1, :, 3 * D - cut : 4 * D - cut] = to_rows(w_out_t[...])
    wrest[1, :, 4 * D - cut :] = jnp.zeros((ROWS, HALF - 4 * D + cut), BF16)
    pl.semaphore_wait(barrier, 31)

    def z_block(g, way):
        return nz.at[g, pl.ds(128 * way, 128)]

    def z_hop(g, way):
        if g <= 2:
            source = nz.at[0, pl.ds(128 * (g - 1), 128)]
        elif g <= 6:
            source = z_block(g - 2, way)
        else:
            source = z_block(5 + way, way)
        n = 2 * g + way
        return remote(source, z_block(g, way), zs.at[n], zr.at[n], f, z_dn if way else z_up)

    for g in (1, 2):
        for way in range(2):
            z_hop(g, way).start()

    def arrive(g):
        for way in range(2):
            z_hop(g, way).wait_recv()
            if g <= 4:
                z_hop(g + 2, way).start()
            elif g == 5 + way:
                z_hop(7, way).start()

    first = remote(wrest.at[1 - core], w1, ws.at[0], wr.at[0], other_core, p)
    first.start()

    def sel_copy(source, peer, n):
        return remote(source, wsel_all.at[n], ss.at[n], sr.at[n], peer, p)

    sel_copy(wsel, other_core, f).start()

    def sel_send(i, c):
        peer = lax.rem(f + 2 * i, 16)
        remote(wsel, wsel_all.at[f], ss.at[peer], sr.at[f], peer, p).start()
        return c

    lax.fori_loop(1, 8, sel_send, 0)
    wsel_all[f] = wsel[...]

    first.wait()
    mine = wrest[core, 0:72, :].astype(F32)
    theirs = w1[0:72, :].astype(F32)
    is_first = core == 0
    low = jnp.where(is_first, mine, theirs)
    high = jnp.where(is_first, theirs, mine)
    w[core, pl.ds(pl.multiple_of(144 * chip, 144), 144), :] = jnp.concatenate(
        [low, high], axis=0
    ).astype(BF16)

    def chip_of(at_y, kind):
        return 2 * at_y + (x_hi if kind == 0 else 1 - x_hi)

    def rows(half, n, start, size):
        return w.at[half, pl.ds(pl.multiple_of(144 * n + start, 16), size)]

    y_prev = lax.rem(y + 3, 4)
    y_next = lax.rem(y + 1, 4)
    y_far = lax.rem(y + 2, 4)

    def cross_send(far):
        block = rows(core, chip_of(y_far if far else y, 0), 0, 144)
        return remote(block, block, ws.at[1 + far], wr.at[1 + far], cross_f, x_pair)

    def y_send(way, kind):
        n = 3 + way * 2 + kind
        block = rows(core, chip_of(y, kind), 0, 144)
        return remote(block, block, ws.at[n], wr.at[n], y_dn if way else y_up, p)

    def y_pass(way):
        block = rows(core, chip_of(y_next if way else y_prev, 0), 80 * way, 64 if way else 80)
        return remote(block, block, ws.at[7 + way], wr.at[7 + way], y_dn if way else y_up, p)

    def core_send(at_y, kind):
        n = chip_of(at_y, kind)
        block = rows(core, n, 0, 144)
        return remote(block, block, ws.at[9 + n], wr.at[9 + n], other_core, p)

    cross_send(0).start()
    for way in range(2):
        y_send(way, 0).start()
    core_send(y, 0).start()

    zero8 = jnp.zeros((8, TOK), F32)
    ones8 = jnp.where(lax.broadcasted_iota(jnp.int32, (8, TOK), 0) == 0, 1.0, 0.0)
    lower = x_lo == 0

    def to_natural(slot):
        kt = qkv[slot, ROWS : 2 * ROWS, :].astype(F32)
        kt = jnp.concatenate([kt, jnp.zeros((128 - ROWS, TOK), F32)], axis=0)
        kn[slot * TOK : slot * TOK + TOK, :] = kt.T.astype(BF16)

    def pair_copy(g):
        return remote(stage.at[g], qkv.at[2 * g + 1], xs.at[g], xr.at[g], f, x_pair)

    def project(g):
        r = jnp.dot(nz[g], wc[...], preferred_element_type=F32)
        t = r.T
        own, oth = [], []
        for part in range(3):
            one = t[144 * part : 144 * part + 72]
            two = t[144 * part + 72 : 144 * part + 144]
            if part == 0:
                one, two = one * Q_SCALE, two * Q_SCALE
            own += [jnp.where(lower, one, two), ones8 if part == 2 else zero8]
            oth += [jnp.where(lower, two, one), ones8 if part == 2 else zero8]
        stage[g] = jnp.concatenate(oth, axis=0).astype(BF16)
        pair_copy(g).start()
        qkv[2 * g] = jnp.concatenate(own, axis=0).astype(BF16)
        to_natural(2 * g)

    def receive(g):
        pair_copy(g).wait()
        to_natural(2 * g + 1)

    head = 2 * z + x_lo
    scores = (score_a, score_b)
    tops = (top_a, top_b)
    top_all[...] = jnp.full(top_all.shape, -1e30, F32)
    acc_all[...] = jnp.zeros(acc_all.shape, F32)

    def out_copy(d, odd, half):
        to = (1 - x_lo if odd else x_lo) * 8 + lax.rem(z + (d if half else 8 - d), 8)
        n = 2 * odd + half
        return remote(ostage.at[d, n], attn.at[head], os.at[4 * d + n], orr.at[head], f, to)

    def emit(d, odd, half, first_rows, last_rows):
        n = 2 * odd + half
        ostage[d, n] = jnp.concatenate([first_rows, last_rows], axis=0).astype(BF16)
        if isinstance(d, int) and d == 0 and odd == 0:
            attn[head] = ostage[d, n]
        else:
            out_copy(d, odd, half).start()

    def emit_single(d, o):
        for odd in range(2):
            at = 256 * odd
            emit(d, odd, 0, o[:, at : at + 128], o[:, at + 128 : at + 256])

    def emit_pair(d, o0, o1):
        for odd in range(2):
            for half in range(2):
                at = 128 * (2 * odd + half)
                emit(d, odd, half, o0[:, at : at + 128], o1[:, at : at + 128])

    def score_steps(gq, gk, buf):
        q_t = jnp.concatenate([qkv[2 * gq, 0:ROWS, :], qkv[2 * gq + 1, 0:ROWS, :]], axis=1)
        state = [None]

        def one(u):
            at = pl.ds(pl.multiple_of(2 * TOK * gk + TOK * u, TOK), TOK)
            s = jnp.dot(kn[at, 0:ROWS], q_t, preferred_element_type=F32)
            scores[buf][TOK * u : TOK * u + TOK, :] = s
            m = jnp.max(s.reshape(TOK // 8, 8, 2 * TOK), axis=0)
            state[0] = m if state[0] is None else jnp.maximum(state[0], m)
            if u == 1:
                tops[buf][...] = state[0]

        return [lambda: one(0), lambda: one(1)]

    def job(gq, gk, buf, following, last):
        steps = score_steps(*following, 1 - buf) if following else None
        old = top_all[gq]
        m = jnp.maximum(old, jnp.max(tops[buf][...], axis=0, keepdims=True))
        acc = acc_all[gq] * jnp.exp2(old - m)
        for u in range(2):
            if steps:
                steps[u]()
            prob = jnp.exp2(scores[buf][TOK * u : TOK * u + TOK, :] - m).astype(BF16)
            acc += jnp.dot(
                qkv[2 * gk + u, 2 * ROWS : 3 * ROWS, :], prob, preferred_element_type=F32
            )
        if last:
            return acc[0:HEAD] / acc[HEAD : HEAD + 1]
        top_all[gq] = m
        acc_all[gq] = acc

    def jobs(pick, count, finish=None):
        last = finish is not None
        for step in score_steps(*pick(0), 0):
            step()
        rest = 1 if count % 2 else 2

        def two(i, c):
            o1 = job(*pick(2 * i), 0, pick(2 * i + 1), last)
            o0 = job(*pick(2 * i + 1), 1, pick(2 * i + 2), last)
            if last:
                finish(i, o0, o1)
            return c

        if count > rest:
            lax.fori_loop(0, (count - rest) // 2, two, 0)
        for t in range(count - rest, count):
            following = pick(t + 1) if t + 1 < count else None
            o = job(*pick(t), (t - count + rest) % 2, following, last)
        if last:
            finish(None, o, None)

    def group_jobs(g, begin, end):
        def pick(t):
            t = t + begin
            if isinstance(t, int):
                return (t, g) if t < g else (g, t - g)
            return jnp.where(t < g, t, g), jnp.where(t < g, g, t - g)

        jobs(pick, end - begin)

    arrive(1)

    def sel_take(i, c):
        peer = lax.rem(f + 2 * i, 16)
        sel_copy(wsel, peer, peer).wait_recv()
        remote(
            wsel_all.at[peer], wsel_all.at[peer], ss.at[peer + 1 - 2 * core], sr.at[peer], other_core, p
        ).start()
        return c

    lax.fori_loop(1, 8, sel_take, 0)

    def sel_swapped(i, c):
        n = lax.rem(other_core + 2 * i, 16)
        sel_copy(wsel, other_core, n).wait_recv()
        return c

    lax.fori_loop(0, 8, sel_swapped, 0)
    for j in range(8):
        a = wsel_all[2 * j, 0:72, :].astype(F32)
        b = wsel_all[2 * j + 1, 0:72, :].astype(F32)
        wc[144 * j : 144 * j + 144, :] = jnp.concatenate([a, b], axis=0).astype(BF16)
    project(0)
    project(1)
    arrive(2)
    project(2)
    receive(0)
    receive(1)
    group_jobs(0, 0, 1)
    group_jobs(1, 0, 3)
    arrive(3)
    project(3)
    receive(2)
    group_jobs(2, 0, 5)
    arrive(4)
    cross_send(0).wait_recv()
    for way in range(2):
        y_send(way, 0).wait_recv()
        y_pass(way).start()
    for way in range(2):
        y_send(way, 1).start()
    core_send(y, 1).start()
    core_send(y_prev, 0).start()
    core_send(y_next, 0).start()
    project(4)
    receive(3)
    group_jobs(3, 0, 7)
    arrive(5)
    project(5)
    receive(4)
    group_jobs(4, 0, 9)
    receive(5)
    group_jobs(5, 0, 4)
    arrive(6)
    project(6)
    group_jobs(5, 4, 11)
    far = [rows(core, chip_of(y_far, 0), 80 * way, 64 if way else 80) for way in range(2)]
    for way in range(2):
        remote(far[way], far[way], ws.at[7 + way], wr.at[7 + way], other_core, p).wait_recv()
    cross_send(1).start()
    core_send(y_far, 0).start()
    receive(6)
    group_jobs(6, 0, 4)
    arrive(7)
    project(7)
    group_jobs(6, 4, 13)
    receive(7)

    def finish_near(i, o0, o1):
        if i is None:
            emit_single(0, o0)
        else:
            emit_pair(3 - i, o0, o1)

    jobs(lambda t: (6 - t, 7), 7, finish_near)
    jobs(lambda t: (7, t), 7)
    jobs(lambda t: (7, 7), 1, lambda i, o0, o1: emit_single(4, o0))

    for way in range(2):
        y_send(way, 1).wait_recv()
    core_send(y_prev, 1).start()
    core_send(y_next, 1).start()
    cross_send(1).wait_recv()
    core_send(y_far, 1).start()

    for at_y in (y, y_prev, y_next, y_far):
        for kind in range(2):
            n = chip_of(at_y, kind)
            block = rows(1 - core, n, 0, 144)
            remote(block, block, ws.at[9 + n], wr.at[9 + n], other_core, p).wait_recv()

    for h in range(HEADS):
        at = HEAD * h // 16 * 16
        off = HEAD * h - at
        wo[h] = to_rows(w[0, at : at + ROWS, 0:D].astype(F32)[off : off + HEAD])
    acc_t[...] = jnp.zeros_like(acc_t)

    def out_take(i, c):
        d = jnp.where(i < 12, 3 - i // 4, jnp.where(i < 14, 0, 4))
        odd = jnp.where(i < 12, lax.rem(i, 4) // 2, lax.rem(i, 2))
        lo = jnp.where(odd == 1, 1 - x_lo, x_lo)
        zs_at = lax.rem(z + jnp.where(lax.rem(i, 2) == 1, d, 8 - d), 8)
        h = 2 * zs_at + lo

        @pl.when(i != 12)
        def _():
            remote(
                ostage.at[0, 0], attn.at[h], os.at[0], orr.at[h], f, lo * 8 + zs_at
            ).wait_recv()

        block = attn[h].astype(F32)
        block = jnp.concatenate([block[0:HEAD], block[HEAD : 2 * HEAD]], axis=1)
        block = jnp.concatenate([block, jnp.zeros((128 - HEAD, TOK), F32)], axis=0)
        x = block.T.astype(BF16)
        acc_t[...] += jnp.dot(x[:, 0:ROWS], wo[h], preferred_element_type=F32)
        return c

    lax.fori_loop(0, 16, out_take, 0)
    mid[...] = (hid[...].astype(F32) + mod[2:3] * acc_t[...]).astype(BF16)

    def rows16(ref, n):
        return ref.at[pl.ds(pl.multiple_of(16 * n, 16), 16)]

    def send_mid(i, c):
        peer = lax.rem(f + i, 16)
        remote(rows16(mid, peer), rows16(midt, f), ms.at[i], mr.at[f], peer, p).start()
        return c

    lax.fori_loop(1, 16, send_mid, 0)
    here = pl.ds(pl.multiple_of(16 * f, 16), 16)
    midt[here, :] = mid[here, :]

    for g in range(1, 8):
        for way in range(2):
            z_hop(g, way).wait_send()

    def sel_sent(i, c):
        sel_copy(wsel, other_core, lax.rem(f + 2 * i, 16)).wait_send()
        sel_copy(wsel, other_core, lax.rem(other_core + 2 * i, 16)).wait_send()
        return c

    lax.fori_loop(1, 8, sel_sent, 0)
    sel_copy(wsel, other_core, f).wait_send()

    for d in range(5):
        for odd in range(2):
            for half in range(2 if 0 < d < 4 else 1):
                if d + odd > 0:
                    out_copy(d, odd, half).wait_send()
    for way in range(2):
        cross_send(way).wait_send()
        y_pass(way).wait_send()
        for kind in range(2):
            y_send(way, kind).wait_send()
    for at_y in (y, y_prev, y_next, y_far):
        for kind in range(2):
            core_send(at_y, kind).wait_send()

    def take_mid(i, c):
        peer = lax.rem(f + i, 16)
        remote(rows16(mid, peer), rows16(midt, peer), ms.at[i], mr.at[peer], peer, p).wait()
        return c

    lax.fori_loop(1, 16, take_mid, 0)
    proj[...] = norm_modulate(midt[...].astype(F32), mod[3:4], mod[4:5]).astype(BF16)
    a = jnp.dot(proj[...], w[0, :, D:HALF], preferred_element_type=F32)
    qkv_t[:, 0:D] = (a[:, 0:D] * Q_SCALE).astype(BF16)
    qkv_t[:, D : HALF - D] = a[:, D:].astype(BF16)
    b = jnp.dot(proj[...], w[1, :, 0 : 4 * D - HALF], preferred_element_type=F32)
    qkv_t[:, HALF - D : 3 * D] = b.astype(BF16)

    ri = lax.broadcasted_iota(jnp.int32, (TOK, TOK), 0)
    ci = lax.broadcasted_iota(jnp.int32, (TOK, TOK), 1)
    same = lax.rem(ri, 16) == lax.rem(ci, 16)
    acc_t[...] = jnp.zeros_like(acc_t)
    for h in range(HEADS):
        start = 128 * min(HEAD * h // 128, 7)
        low = HEAD * h - start
        inside = (ci >= low) & (ci < low + HEAD)
        q = qkv_t[:, start : start + 256]
        q = jnp.where(inside, q, jnp.zeros_like(q))
        k = qkv_t[:, D + start : D + start + 256]
        v = qkv_t[:, 2 * D + start : 2 * D + start + 256]
        s = lax.dot_general(q, k, (((1,), (1,)), ((), ())), preferred_element_type=F32)
        s = jnp.where(same, s, -1e30)
        prob = jnp.exp2(s - jnp.max(s, axis=1, keepdims=True))
        total = jnp.sum(prob, axis=1, keepdims=True)
        o = jnp.dot(prob.astype(BF16), v, preferred_element_type=F32) / total
        acc_t[:, start : start + 256] = jnp.where(inside, o, acc_t[:, start : start + 256])
    r = jnp.dot(
        acc_t[...].astype(BF16), w[1, :, 4 * D - HALF : 5 * D - HALF], preferred_element_type=F32
    )
    osend[...] = (midt[...].astype(F32) + mod[5:6] * r).astype(BF16)

    def send_out(i, c):
        peer = lax.rem(f + i, 16)
        remote(rows16(osend, peer), rows16(out, f), bs.at[i], br.at[f], peer, p).start()
        return c

    lax.fori_loop(1, 16, send_out, 0)
    out[here, :] = osend[here, :]

    def take_out(i, c):
        peer = lax.rem(f + i, 16)
        remote(rows16(osend, peer), rows16(out, peer), bs.at[i], br.at[peer], peer, p).wait()
        return c

    lax.fori_loop(1, 16, take_out, 0)


VMEM = pl.BlockSpec(memory_space=pltpu.VMEM)


def block_call(*args):
    dma = pltpu.SemaphoreType.DMA
    return pl.pallas_call(
        block_kernel,
        out_shape=jax.ShapeDtypeStruct((TOK, D), BF16),
        in_specs=[VMEM] * 6,
        out_specs=VMEM,
        scratch_shapes=[
            pltpu.VMEM((8, TOK, D), BF16),
            pltpu.VMEM((ROWS, 512), BF16),
            pltpu.VMEM((2, ROWS, HALF), BF16),
            pltpu.VMEM((HEADS, ROWS, D), BF16),
            pltpu.VMEM((16, ROWS, 512), BF16),
            pltpu.VMEM((D, 512), BF16),
            pltpu.VMEM((16, 3 * ROWS, TOK), BF16),
            pltpu.VMEM((8, 3 * ROWS, TOK), BF16),
            pltpu.VMEM((4096, 128), BF16),
            pltpu.VMEM((5, 4, 2 * HEAD, 128), BF16),
            pltpu.VMEM((HEADS, 2 * HEAD, 128), BF16),
            pltpu.VMEM((ROWS, HALF), BF16),
            pltpu.VMEM((2, D, HALF), BF16),
            pltpu.VMEM((2 * TOK, 2 * TOK), F32),
            pltpu.VMEM((2 * TOK, 2 * TOK), F32),
            pltpu.VMEM((8, 2 * TOK), F32),
            pltpu.VMEM((8, 2 * TOK), F32),
            pltpu.VMEM((8, 1, 2 * TOK), F32),
            pltpu.VMEM((8, ROWS, 2 * TOK), F32),
            pltpu.VMEM((TOK, D), BF16),
            pltpu.VMEM((TOK, D), BF16),
            pltpu.VMEM((TOK, D), BF16),
            pltpu.VMEM((TOK, 3 * D), BF16),
            pltpu.VMEM((TOK, D), F32),
            pltpu.VMEM((TOK, D), BF16),
            dma((16,)), dma((16,)),
            dma((16,)), dma((16,)),
            dma((8,)), dma((8,)),
            dma((20,)), dma((16,)),
            dma((17,)), dma((17,)),
            dma((16,)), dma((16,)),
            dma((16,)), dma((16,)),
        ],
        compiler_params=pltpu.CompilerParams(
            collective_id=0, has_side_effects=True, vmem_limit_bytes=60 * 1024 * 1024
        ),
        name="block",
    )(*args)


def body(hidden_states, modulation, w_qkv_spatial, w_out_spatial, w_qkv_temporal, w_out_temporal):
    out = block_call(
        hidden_states.reshape(TOK, D),
        modulation,
        w_qkv_spatial,
        w_out_spatial,
        w_qkv_temporal,
        w_out_temporal,
    )
    return out.reshape(1, TOK, D)


def solution(mesh):
    in_specs = (
        P("frame", "patch", None),
        P(),
        P("frame", None),
        P("frame", None),
        P("frame", None),
        P("frame", None),
    )
    out_specs = P("frame", "patch", None)
    return jax.shard_map(body, mesh=mesh, in_specs=in_specs, out_specs=out_specs, check_vma=False)
```

```python
import math

import jax
import jax.numpy as jnp
from jax import lax
from jax.experimental import pallas as pl
from jax.experimental.pallas import tpu as pltpu
from jax.sharding import PartitionSpec as P

HEAD = 72
HEADS = 16
D = 1152
TOK = 256
ROWS = 80
HALF = 2944
EARLY = 640
Q_SCALE = HEAD ** (-0.5) * math.log2(math.e)
F32 = jnp.float32
BF16 = jnp.bfloat16


def remote(src, dst, send, recv, frame, patch):
    return pltpu.make_async_remote_copy(
        src_ref=src,
        dst_ref=dst,
        send_sem=send,
        recv_sem=recv,
        device_id={"frame": frame, "patch": patch},
        device_id_type=pl.DeviceIdType.MESH,
    )


def signal(sem, frame, patch):
    pl.semaphore_signal(
        sem, inc=1, device_id={"frame": frame, "patch": patch}, device_id_type=pl.DeviceIdType.MESH
    )


def norm_modulate(x, shift, scale):
    centred = x - jnp.mean(x, axis=-1, keepdims=True)
    variance = jnp.mean(centred * centred, axis=-1, keepdims=True)
    return centred * lax.rsqrt(variance + 1e-06) * (1.0 + scale) + shift


def block_kernel(
    hid, mod, w_qkv_s, w_out_s, w_qkv_t, w_out_t, out,
    nz, wsel, wrest, wo, heads, wsel_all, wc, qkv, stage, kn, ostage, attn, w1, w, score_a, score_b, top_a, top_b, top_all, acc_all,
    mid, midt, proj, qkv_t, acc_t, osend,
    zs, zr, ss, sr, xs, xr, os, orr, ws, wr, ms, mr, bs, br,
):
    f = lax.axis_index("frame")
    p = lax.axis_index("patch")
    core = lax.rem(f, 2)
    x_hi = lax.rem(f // 2, 2)
    y = f // 4
    x_lo = p // 8
    z = lax.rem(p, 8)
    chip = f // 2
    other_core = f + 1 - 2 * core
    cross_f = (y * 2 + 1 - x_hi) * 2 + core
    x_pair = (1 - x_lo) * 8 + z
    y_up = lax.rem(y + 1, 4) * 4 + x_hi * 2 + core
    y_dn = lax.rem(y + 3, 4) * 4 + x_hi * 2 + core
    z_up = x_lo * 8 + lax.rem(z + 1, 8)
    z_dn = x_lo * 8 + lax.rem(z + 7, 8)

    barrier = pltpu.get_barrier_semaphore()

    def greet(i, c):
        signal(barrier, lax.rem(f + i, 16), p)
        signal(barrier, f, lax.rem(p + i, 16))
        return c

    lax.fori_loop(1, 16, greet, 0)
    signal(barrier, cross_f, x_pair)
    nz[0] = norm_modulate(hid[...].astype(F32), mod[0:1], mod[1:2]).astype(BF16)

    lanes = lax.broadcasted_iota(jnp.int32, (HEAD, TOK), 1)
    own, other = [], []
    for part in range(3):
        at = pl.ds(pl.multiple_of(D * part + 128 * z, 128), TOK)
        window = w_qkv_s[:, at].astype(F32)
        inside = (lanes >= HEAD * part) & (lanes < HEAD * part + HEAD)
        for which, found in ((x_lo, own), (1 - x_lo, other)):
            shift = lax.rem(2 * TOK - 16 * z - HEAD * which + HEAD * part, TOK)
            found.append(jnp.where(inside, pltpu.roll(window, shift, axis=1), 0.0))
    sel = jnp.concatenate([own[0] + own[1] + own[2], other[0] + other[1] + other[2]], axis=1)

    def to_rows(value):
        tail = jnp.zeros((ROWS - HEAD, value.shape[1]), F32)
        return jnp.concatenate([value.astype(F32), tail], axis=0).astype(BF16)

    wsel[...] = to_rows(sel)
    wrest[0, :, 0:EARLY] = to_rows(w_out_s[:, 0:EARLY])
    wrest[0, :, EARLY:HALF] = to_rows(w_qkv_t[:, 0 : 2 * D])
    wrest[1, :, 0 : D - EARLY] = to_rows(w_out_s[:, EARLY:D])
    wrest[1, :, D - EARLY : EARLY] = jnp.zeros((ROWS, 2 * EARLY - D), BF16)
    wrest[1, :, EARLY : EARLY + D] = to_rows(w_qkv_t[:, 2 * D : 3 * D])
    wrest[1, :, EARLY + D : HALF] = to_rows(w_out_t[...])
    pl.semaphore_wait(barrier, 31)

    def z_block(g, way):
        return nz.at[g, pl.ds(128 * way, 128)]

    def z_hop(g, way):
        if g <= 2:
            source = nz.at[0, pl.ds(128 * (g - 1), 128)]
        elif g <= 6:
            source = z_block(g - 2, way)
        else:
            source = z_block(5 + way, way)
        n = 2 * g + way
        return remote(source, z_block(g, way), zs.at[n], zr.at[n], f, z_dn if way else z_up)

    for g in (1, 2):
        for way in range(2):
            z_hop(g, way).start()

    def arrive(g):
        for way in range(2):
            z_hop(g, way).wait_recv()
            if g <= 4:
                z_hop(g + 2, way).start()
            elif g == 5 + way:
                z_hop(7, way).start()

    first = remote(wrest.at[1 - core], w1, ws.at[0], wr.at[0], other_core, p)
    first.start()

    def sel_copy(source, peer, n):
        return remote(source, wsel_all.at[n], ss.at[n], sr.at[n], peer, p)

    sel_copy(wsel, other_core, f).start()

    def sel_send(i, c):
        peer = lax.rem(f + 2 * i, 16)
        remote(wsel, wsel_all.at[f], ss.at[peer], sr.at[f], peer, p).start()
        return c

    lax.fori_loop(1, 8, sel_send, 0)
    wsel_all[f] = wsel[...]

    first.wait()
    mine = wrest[core, 0:72, :].astype(F32)
    theirs = w1[0:72, :].astype(F32)
    is_first = core == 0
    low = jnp.where(is_first, mine, theirs)
    high = jnp.where(is_first, theirs, mine)
    w[core, pl.ds(pl.multiple_of(144 * chip, 144), 144), :] = jnp.concatenate(
        [low, high], axis=0
    ).astype(BF16)

    def chip_of(at_y, kind):
        return 2 * at_y + (x_hi if kind == 0 else 1 - x_hi)

    def rows(half, n, start, size, part):
        at = pl.ds(pl.multiple_of(144 * n + start, 16), size)
        return w.at[half, at, pl.ds(EARLY * part, HALF - EARLY if part else EARLY)]

    y_prev = lax.rem(y + 3, 4)
    y_next = lax.rem(y + 1, 4)
    y_far = lax.rem(y + 2, 4)

    def weight_copy(block, n, part, to_f, to_p):
        n = n + 17 * part
        return remote(block, block, ws.at[n], wr.at[n], to_f, to_p)

    def cross_send(far, part):
        block = rows(core, chip_of(y_far if far else y, 0), 0, 144, part)
        return weight_copy(block, 1 + far, part, cross_f, x_pair)

    def y_send(way, kind, part):
        block = rows(core, chip_of(y, kind), 0, 144, part)
        return weight_copy(block, 3 + way * 2 + kind, part, y_dn if way else y_up, p)

    def y_pass(way, part):
        n = chip_of(y_next if way else y_prev, 0)
        block = rows(core, n, 80 * way, 64 if way else 80, part)
        return weight_copy(block, 7 + way, part, y_dn if way else y_up, p)

    def y_pass_in(way, part):
        block = rows(core, chip_of(y_far, 0), 80 * way, 64 if way else 80, part)
        return weight_copy(block, 7 + way, part, other_core, p)

    def core_send(at_y, kind, part):
        n = chip_of(at_y, kind)
        return weight_copy(rows(core, n, 0, 144, part), 9 + n, part, other_core, p)

    def core_in(at_y, kind, part):
        n = chip_of(at_y, kind)
        return weight_copy(rows(1 - core, n, 0, 144, part), 9 + n, part, other_core, p)

    def near_rows(part):
        cross_send(0, part).wait_recv()
        for way in range(2):
            y_send(way, 0, part).wait_recv()
            y_pass(way, part).start()
        for way in range(2):
            y_send(way, 1, part).start()
        core_send(y, 1, part).start()
        core_send(y_prev, 0, part).start()
        core_send(y_next, 0, part).start()

    def far_rows(part):
        for way in range(2):
            y_pass_in(way, part).wait_recv()
        cross_send(1, part).start()
        core_send(y_far, 0, part).start()

    def crossed_rows(part):
        for way in range(2):
            y_send(way, 1, part).wait_recv()
        core_send(y_prev, 1, part).start()
        core_send(y_next, 1, part).start()

    def last_rows(part):
        cross_send(1, part).wait_recv()
        core_send(y_far, 1, part).start()

    def all_rows(part):
        for at_y in (y, y_prev, y_next, y_far):
            for kind in range(2):
                core_in(at_y, kind, part).wait_recv()

    for part in range(2):
        cross_send(0, part).start()
        for way in range(2):
            y_send(way, 0, part).start()
        core_send(y, 0, part).start()

    zero8 = jnp.zeros((8, TOK), F32)
    ones8 = jnp.where(lax.broadcasted_iota(jnp.int32, (8, TOK), 0) == 0, 1.0, 0.0)

    def to_natural(slot):
        kt = qkv[slot, ROWS : 2 * ROWS, :].astype(F32)
        kt = jnp.concatenate([kt, jnp.zeros((128 - ROWS, TOK), F32)], axis=0)
        kn[slot * TOK : slot * TOK + TOK, :] = kt.T.astype(BF16)

    def pair_copy(g):
        return remote(stage.at[g], qkv.at[2 * g + 1], xs.at[g], xr.at[g], f, x_pair)

    def project(g):
        for lane in (256, 0):
            r = jnp.dot(nz[g], wc[:, lane : lane + 256], preferred_element_type=F32)
            t = r.T
            block = [t[0:72] * Q_SCALE, zero8, t[72:144], zero8, t[144:216], ones8]
            block = jnp.concatenate(block, axis=0).astype(BF16)
            if lane:
                stage[g] = block
                pair_copy(g).start()
            else:
                qkv[2 * g] = block
        to_natural(2 * g)

    def receive(g):
        pair_copy(g).wait()
        to_natural(2 * g + 1)

    head = 2 * z + x_lo
    scores = (score_a, score_b)
    tops = (top_a, top_b)
    top_all[...] = jnp.full(top_all.shape, -1e30, F32)
    acc_all[...] = jnp.zeros(acc_all.shape, F32)

    def out_copy(d, odd, half):
        to = (1 - x_lo if odd else x_lo) * 8 + lax.rem(z + (d if half else 8 - d), 8)
        n = 2 * odd + half
        return remote(ostage.at[d, n], attn.at[head], os.at[4 * d + n], orr.at[head], f, to)

    def emit(d, odd, half, first_rows, last_rows):
        n = 2 * odd + half
        ostage[d, n] = jnp.concatenate([first_rows, last_rows], axis=0).astype(BF16)
        if isinstance(d, int) and d == 0 and odd == 0:
            attn[head] = ostage[d, n]
        else:
            out_copy(d, odd, half).start()

    def emit_single(d, o):
        for odd in range(2):
            at = 256 * odd
            emit(d, odd, 0, o[:, at : at + 128], o[:, at + 128 : at + 256])

    def emit_pair(d, o0, o1):
        for odd in range(2):
            for half in range(2):
                at = 128 * (2 * odd + half)
                emit(d, odd, half, o0[:, at : at + 128], o1[:, at : at + 128])

    def score_steps(gq, gk, buf):
        q_t = jnp.concatenate([qkv[2 * gq, 0:ROWS, :], qkv[2 * gq + 1, 0:ROWS, :]], axis=1)
        state = [None]

        def one(u):
            at = pl.ds(pl.multiple_of(2 * TOK * gk + TOK * u, TOK), TOK)
            s = jnp.dot(kn[at, 0:ROWS], q_t, preferred_element_type=F32)
            scores[buf][TOK * u : TOK * u + TOK, :] = s
            m = jnp.max(s.reshape(TOK // 8, 8, 2 * TOK), axis=0)
            state[0] = m if state[0] is None else jnp.maximum(state[0], m)
            if u == 1:
                tops[buf][...] = state[0]

        return [lambda: one(0), lambda: one(1)]

    def job(gq, gk, buf, following, last):
        steps = score_steps(*following, 1 - buf) if following else None
        old = top_all[gq]
        m = jnp.maximum(old, jnp.max(tops[buf][...], axis=0, keepdims=True))
        acc = acc_all[gq] * jnp.exp2(old - m)
        for u in range(2):
            if steps:
                steps[u]()
            prob = jnp.exp2(scores[buf][TOK * u : TOK * u + TOK, :] - m).astype(BF16)
            acc += jnp.dot(
                qkv[2 * gk + u, 2 * ROWS : 3 * ROWS, :], prob, preferred_element_type=F32
            )
        if last:
            return acc[0:HEAD] / acc[HEAD : HEAD + 1]
        top_all[gq] = m
        acc_all[gq] = acc

    def jobs(pick, count, finish=None):
        last = finish is not None
        for step in score_steps(*pick(0), 0):
            step()
        rest = 1 if count % 2 else 2

        def two(i, c):
            o1 = job(*pick(2 * i), 0, pick(2 * i + 1), last)
            o0 = job(*pick(2 * i + 1), 1, pick(2 * i + 2), last)
            if last:
                finish(i, o0, o1)
            return c

        if count > rest:
            lax.fori_loop(0, (count - rest) // 2, two, 0)
        for t in range(count - rest, count):
            following = pick(t + 1) if t + 1 < count else None
            o = job(*pick(t), (t - count + rest) % 2, following, last)
        if last:
            finish(None, o, None)

    def group_jobs(g, begin, end):
        def pick(t):
            t = t + begin
            if isinstance(t, int):
                return (t, g) if t < g else (g, t - g)
            return jnp.where(t < g, t, g), jnp.where(t < g, g, t - g)

        jobs(pick, end - begin)

    arrive(1)

    def sel_take(i, c):
        peer = lax.rem(f + 2 * i, 16)
        sel_copy(wsel, peer, peer).wait_recv()
        remote(
            wsel_all.at[peer], wsel_all.at[peer], ss.at[peer + 1 - 2 * core], sr.at[peer], other_core, p
        ).start()
        return c

    lax.fori_loop(1, 8, sel_take, 0)

    def sel_swapped(i, c):
        n = lax.rem(other_core + 2 * i, 16)
        sel_copy(wsel, other_core, n).wait_recv()
        return c

    lax.fori_loop(0, 8, sel_swapped, 0)
    for j in range(8):
        a = wsel_all[2 * j, 0:72, :].astype(F32)
        b = wsel_all[2 * j + 1, 0:72, :].astype(F32)
        wc[144 * j : 144 * j + 144, :] = jnp.concatenate([a, b], axis=0).astype(BF16)
    project(0)
    project(1)
    arrive(2)
    project(2)
    receive(0)
    receive(1)
    group_jobs(0, 0, 1)
    group_jobs(1, 0, 3)
    arrive(3)
    near_rows(0)
    project(3)
    receive(2)
    group_jobs(2, 0, 5)
    arrive(4)
    near_rows(1)
    project(4)
    receive(3)
    group_jobs(3, 0, 7)
    arrive(5)
    far_rows(0)
    project(5)
    receive(4)
    group_jobs(4, 0, 9)
    receive(5)
    group_jobs(5, 0, 4)
    arrive(6)
    crossed_rows(0)
    project(6)
    group_jobs(5, 4, 11)
    far_rows(1)
    receive(6)
    group_jobs(6, 0, 4)
    arrive(7)
    project(7)
    last_rows(0)
    group_jobs(6, 4, 13)
    receive(7)

    def finish_near(i, o0, o1):
        if i is None:
            emit_single(0, o0)
        else:
            emit_pair(3 - i, o0, o1)

    jobs(lambda t: (6 - t, 7), 7, finish_near)
    jobs(lambda t: (7, t), 7)
    jobs(lambda t: (7, 7), 1, lambda i, o0, o1: emit_single(4, o0))

    all_rows(0)
    crossed_rows(1)

    def source(i):
        d = jnp.where(i < 12, 3 - i // 4, jnp.where(i < 14, 0, 4))
        odd = jnp.where(i < 12, lax.rem(i, 4) // 2, lax.rem(i, 2))
        lo = jnp.where(odd == 1, 1 - x_lo, x_lo)
        at_z = lax.rem(z + jnp.where(lax.rem(i, 2) == 1, d, 8 - d), 8)
        return lo, at_z

    def lay_out(i, c):
        lo, at_z = source(i)
        first = HEAD * (2 * at_z + lo)
        from_row = first // 16 * 16
        shifted = first > from_row
        for half, lane, size in ((0, 0, EARLY), (1, EARLY, D - EARLY)):
            block = w[half, pl.ds(pl.multiple_of(from_row, 16), ROWS), 0:size].astype(F32)
            block = jnp.where(shifted, block[ROWS - HEAD :], block[:HEAD])
            block = jnp.concatenate([block, jnp.zeros((128 - HEAD, size), F32)], axis=0)
            to = pl.ds(pl.multiple_of(128 * i, 128), 128)
            wo[to, lane : lane + size] = block.astype(BF16)
        return c

    lax.fori_loop(0, HEADS, lay_out, 0)

    def out_take(i, c):
        lo, at_z = source(i)
        h = 2 * at_z + lo

        @pl.when(i != 12)
        def _():
            remote(
                ostage.at[0, 0], attn.at[h], os.at[0], orr.at[h], f, lo * 8 + at_z
            ).wait_recv()

        block = attn[h].astype(F32)
        block = jnp.concatenate([block[0:HEAD], block[HEAD : 2 * HEAD]], axis=1)
        block = jnp.concatenate([block, jnp.zeros((128 - HEAD, TOK), F32)], axis=0)
        heads[:, pl.ds(pl.multiple_of(128 * i, 128), 128)] = block.T.astype(BF16)
        return c

    lax.fori_loop(0, 12, out_take, 0)
    acc_t[...] = jnp.dot(heads[:, 0:1536], wo[0:1536, :], preferred_element_type=F32)
    lax.fori_loop(12, 16, out_take, 0)
    r = jnp.dot(heads[:, 1536:2048], wo[1536:2048, :], preferred_element_type=F32)
    mid[...] = (hid[...].astype(F32) + mod[2:3] * (acc_t[...] + r)).astype(BF16)

    def rows16(ref, n):
        return ref.at[pl.ds(pl.multiple_of(16 * n, 16), 16)]

    def send_mid(i, c):
        peer = lax.rem(f + i, 16)
        remote(rows16(mid, peer), rows16(midt, f), ms.at[i], mr.at[f], peer, p).start()
        return c

    lax.fori_loop(1, 16, send_mid, 0)
    here = pl.ds(pl.multiple_of(16 * f, 16), 16)
    midt[here, :] = mid[here, :]

    for g in range(1, 8):
        for way in range(2):
            z_hop(g, way).wait_send()

    def sel_sent(i, c):
        sel_copy(wsel, other_core, lax.rem(f + 2 * i, 16)).wait_send()
        sel_copy(wsel, other_core, lax.rem(other_core + 2 * i, 16)).wait_send()
        return c

    lax.fori_loop(1, 8, sel_sent, 0)
    sel_copy(wsel, other_core, f).wait_send()

    for d in range(5):
        for odd in range(2):
            for half in range(2 if 0 < d < 4 else 1):
                if d + odd > 0:
                    out_copy(d, odd, half).wait_send()
    last_rows(1)
    for part in range(2):
        for way in range(2):
            cross_send(way, part).wait_send()
            y_pass(way, part).wait_send()
            for kind in range(2):
                y_send(way, kind, part).wait_send()
        for at_y in (y, y_prev, y_next, y_far):
            for kind in range(2):
                core_send(at_y, kind, part).wait_send()
    all_rows(1)

    def take_mid(i, c):
        peer = lax.rem(f + i, 16)
        remote(rows16(mid, peer), rows16(midt, peer), ms.at[i], mr.at[peer], peer, p).wait()
        return c

    lax.fori_loop(1, 16, take_mid, 0)
    proj[...] = norm_modulate(midt[...].astype(F32), mod[3:4], mod[4:5]).astype(BF16)
    a = jnp.dot(proj[...], w[0, :, EARLY:HALF], preferred_element_type=F32)
    qkv_t[:, 0:D] = (a[:, 0:D] * Q_SCALE).astype(BF16)
    qkv_t[:, D : 2 * D] = a[:, D:].astype(BF16)
    b = jnp.dot(proj[...], w[1, :, EARLY : EARLY + D], preferred_element_type=F32)
    qkv_t[:, 2 * D :] = b.astype(BF16)

    ri = lax.broadcasted_iota(jnp.int32, (TOK, TOK), 0)
    ci = lax.broadcasted_iota(jnp.int32, (TOK, TOK), 1)
    same = lax.rem(ri, 16) == lax.rem(ci, 16)
    acc_t[...] = jnp.zeros_like(acc_t)
    for h in range(HEADS):
        start = 128 * min(HEAD * h // 128, 7)
        low = HEAD * h - start
        inside = (ci >= low) & (ci < low + HEAD)
        q = qkv_t[:, start : start + 256]
        q = jnp.where(inside, q, jnp.zeros_like(q))
        k = qkv_t[:, D + start : D + start + 256]
        v = qkv_t[:, 2 * D + start : 2 * D + start + 256]
        s = lax.dot_general(q, k, (((1,), (1,)), ((), ())), preferred_element_type=F32)
        s = jnp.where(same, s, -1e30)
        prob = jnp.exp2(s - jnp.max(s, axis=1, keepdims=True))
        total = jnp.sum(prob, axis=1, keepdims=True)
        o = jnp.dot(prob.astype(BF16), v, preferred_element_type=F32) / total
        acc_t[:, start : start + 256] = jnp.where(inside, o, acc_t[:, start : start + 256])
    r = jnp.dot(acc_t[...].astype(BF16), w[1, :, EARLY + D : HALF], preferred_element_type=F32)
    osend[...] = (midt[...].astype(F32) + mod[5:6] * r).astype(BF16)

    def send_out(i, c):
        peer = lax.rem(f + i, 16)
        remote(rows16(osend, peer), rows16(out, f), bs.at[i], br.at[f], peer, p).start()
        return c

    lax.fori_loop(1, 16, send_out, 0)
    out[here, :] = osend[here, :]

    def take_out(i, c):
        peer = lax.rem(f + i, 16)
        remote(rows16(osend, peer), rows16(out, peer), bs.at[i], br.at[peer], peer, p).wait()
        return c

    lax.fori_loop(1, 16, take_out, 0)


VMEM = pl.BlockSpec(memory_space=pltpu.VMEM)


def block_call(*args):
    dma = pltpu.SemaphoreType.DMA
    return pl.pallas_call(
        block_kernel,
        out_shape=jax.ShapeDtypeStruct((TOK, D), BF16),
        in_specs=[VMEM] * 6,
        out_specs=VMEM,
        scratch_shapes=[
            pltpu.VMEM((8, TOK, D), BF16),
            pltpu.VMEM((ROWS, 512), BF16),
            pltpu.VMEM((2, ROWS, HALF), BF16),
            pltpu.VMEM((HEADS * 128, D), BF16),
            pltpu.VMEM((TOK, HEADS * 128), BF16),
            pltpu.VMEM((16, ROWS, 512), BF16),
            pltpu.VMEM((D, 512), BF16),
            pltpu.VMEM((16, 3 * ROWS, TOK), BF16),
            pltpu.VMEM((8, 3 * ROWS, TOK), BF16),
            pltpu.VMEM((4096, 128), BF16),
            pltpu.VMEM((5, 4, 2 * HEAD, 128), BF16),
            pltpu.VMEM((HEADS, 2 * HEAD, 128), BF16),
            pltpu.VMEM((ROWS, HALF), BF16),
            pltpu.VMEM((2, D, HALF), BF16),
            pltpu.VMEM((2 * TOK, 2 * TOK), F32),
            pltpu.VMEM((2 * TOK, 2 * TOK), F32),
            pltpu.VMEM((8, 2 * TOK), F32),
            pltpu.VMEM((8, 2 * TOK), F32),
            pltpu.VMEM((8, 1, 2 * TOK), F32),
            pltpu.VMEM((8, ROWS, 2 * TOK), F32),
            pltpu.VMEM((TOK, D), BF16),
            pltpu.VMEM((TOK, D), BF16),
            pltpu.VMEM((TOK, D), BF16),
            pltpu.VMEM((TOK, 3 * D), BF16),
            pltpu.VMEM((TOK, D), F32),
            pltpu.VMEM((TOK, D), BF16),
            dma((16,)), dma((16,)),
            dma((16,)), dma((16,)),
            dma((8,)), dma((8,)),
            dma((20,)), dma((16,)),
            dma((34,)), dma((34,)),
            dma((16,)), dma((16,)),
            dma((16,)), dma((16,)),
        ],
        compiler_params=pltpu.CompilerParams(
            collective_id=0, has_side_effects=True, vmem_limit_bytes=60 * 1024 * 1024
        ),
        name="block",
    )(*args)


def body(hidden_states, modulation, w_qkv_spatial, w_out_spatial, w_qkv_temporal, w_out_temporal):
    out = block_call(
        hidden_states.reshape(TOK, D),
        modulation,
        w_qkv_spatial,
        w_out_spatial,
        w_qkv_temporal,
        w_out_temporal,
    )
    return out.reshape(1, TOK, D)


def solution(mesh):
    in_specs = (
        P("frame", "patch", None),
        P(),
        P("frame", None),
        P("frame", None),
        P("frame", None),
        P("frame", None),
    )
    out_specs = P("frame", "patch", None)
    return jax.shard_map(body, mesh=mesh, in_specs=in_specs, out_specs=out_specs, check_vma=False)
```

```python
import math

import jax
import jax.numpy as jnp
from jax import lax
from jax.experimental import pallas as pl
from jax.experimental.pallas import tpu as pltpu
from jax.sharding import PartitionSpec as P

HEAD = 72
HEADS = 16
D = 1152
TOK = 256
ROWS = 80
HALF = 2944
EARLY = 640
Q_SCALE = HEAD ** (-0.5) * math.log2(math.e)
F32 = jnp.float32
BF16 = jnp.bfloat16


def remote(src, dst, send, recv, frame, patch):
    return pltpu.make_async_remote_copy(
        src_ref=src,
        dst_ref=dst,
        send_sem=send,
        recv_sem=recv,
        device_id={"frame": frame, "patch": patch},
        device_id_type=pl.DeviceIdType.MESH,
    )


def signal(sem, frame, patch):
    pl.semaphore_signal(
        sem, inc=1, device_id={"frame": frame, "patch": patch}, device_id_type=pl.DeviceIdType.MESH
    )


def norm_modulate(x, shift, scale):
    centred = x - jnp.mean(x, axis=-1, keepdims=True)
    variance = jnp.mean(centred * centred, axis=-1, keepdims=True)
    return centred * lax.rsqrt(variance + 1e-06) * (1.0 + scale) + shift


def block_kernel(
    hid, mod, w_qkv_s, w_out_s, w_qkv_t, w_out_t, out,
    nz, wsel, wrest, wo, heads, wsel_all, wc, qkv, stage, kn, ostage, attn, w1, w, score_a, score_b, top_a, top_b, top_all, acc_all,
    midp, midt, qkv_t, acc_t, osend, outp,
    zs, zr, ss, sr, xs, xr, os, orr, ws, wr, ms, mr, bs, br,
):
    f = lax.axis_index("frame")
    p = lax.axis_index("patch")
    core = lax.rem(f, 2)
    x_hi = lax.rem(f // 2, 2)
    y = f // 4
    x_lo = p // 8
    z = lax.rem(p, 8)
    chip = f // 2
    other_core = f + 1 - 2 * core
    cross_f = (y * 2 + 1 - x_hi) * 2 + core
    x_pair = (1 - x_lo) * 8 + z
    y_up = lax.rem(y + 1, 4) * 4 + x_hi * 2 + core
    y_dn = lax.rem(y + 3, 4) * 4 + x_hi * 2 + core
    z_up = x_lo * 8 + lax.rem(z + 1, 8)
    z_dn = x_lo * 8 + lax.rem(z + 7, 8)

    barrier = pltpu.get_barrier_semaphore()

    def greet(i, c):
        signal(barrier, lax.rem(f + i, 16), p)
        signal(barrier, f, lax.rem(p + i, 16))
        return c

    lax.fori_loop(1, 16, greet, 0)
    signal(barrier, cross_f, x_pair)
    nz[0] = norm_modulate(hid[...].astype(F32), mod[0:1], mod[1:2]).astype(BF16)

    lanes = lax.broadcasted_iota(jnp.int32, (HEAD, TOK), 1)
    own, other = [], []
    for part in range(3):
        at = pl.ds(pl.multiple_of(D * part + 128 * z, 128), TOK)
        window = w_qkv_s[:, at].astype(F32)
        inside = (lanes >= HEAD * part) & (lanes < HEAD * part + HEAD)
        for which, found in ((x_lo, own), (1 - x_lo, other)):
            shift = lax.rem(2 * TOK - 16 * z - HEAD * which + HEAD * part, TOK)
            found.append(jnp.where(inside, pltpu.roll(window, shift, axis=1), 0.0))
    sel = jnp.concatenate([own[0] + own[1] + own[2], other[0] + other[1] + other[2]], axis=1)

    def to_rows(value):
        tail = jnp.zeros((ROWS - HEAD, value.shape[1]), F32)
        return jnp.concatenate([value.astype(F32), tail], axis=0).astype(BF16)

    wsel[...] = to_rows(sel)
    wrest[0, :, 0:EARLY] = to_rows(w_out_s[:, 0:EARLY])
    wrest[0, :, EARLY:HALF] = to_rows(w_qkv_t[:, 0 : 2 * D])
    wrest[1, :, 0 : D - EARLY] = to_rows(w_out_s[:, EARLY:D])
    wrest[1, :, D - EARLY : EARLY] = jnp.zeros((ROWS, 2 * EARLY - D), BF16)
    wrest[1, :, EARLY : EARLY + D] = to_rows(w_qkv_t[:, 2 * D : 3 * D])
    wrest[1, :, EARLY + D : HALF] = to_rows(w_out_t[...])
    pl.semaphore_wait(barrier, 31)

    def z_block(g, way):
        return nz.at[g, pl.ds(128 * way, 128)]

    def z_hop(g, way):
        if g <= 2:
            source = nz.at[0, pl.ds(128 * (g - 1), 128)]
        elif g <= 6:
            source = z_block(g - 2, way)
        else:
            source = z_block(5 + way, way)
        n = 2 * g + way
        return remote(source, z_block(g, way), zs.at[n], zr.at[n], f, z_dn if way else z_up)

    for g in (1, 2):
        for way in range(2):
            z_hop(g, way).start()

    def arrive(g):
        for way in range(2):
            z_hop(g, way).wait_recv()
            if g <= 4:
                z_hop(g + 2, way).start()
            elif g == 5 + way:
                z_hop(7, way).start()

    first = remote(wrest.at[1 - core], w1, ws.at[0], wr.at[0], other_core, p)
    first.start()

    def sel_copy(source, peer, n):
        return remote(source, wsel_all.at[n], ss.at[n], sr.at[n], peer, p)

    sel_copy(wsel, other_core, f).start()

    def sel_send(i, c):
        peer = lax.rem(f + 2 * i, 16)
        remote(wsel, wsel_all.at[f], ss.at[peer], sr.at[f], peer, p).start()
        return c

    lax.fori_loop(1, 8, sel_send, 0)
    wsel_all[f] = wsel[...]

    first.wait()
    mine = wrest[core, 0:72, :].astype(F32)
    theirs = w1[0:72, :].astype(F32)
    is_first = core == 0
    low = jnp.where(is_first, mine, theirs)
    high = jnp.where(is_first, theirs, mine)
    w[core, pl.ds(pl.multiple_of(144 * chip, 144), 144), :] = jnp.concatenate(
        [low, high], axis=0
    ).astype(BF16)

    def chip_of(at_y, kind):
        return 2 * at_y + (x_hi if kind == 0 else 1 - x_hi)

    def rows(half, n, start, size, part):
        at = pl.ds(pl.multiple_of(144 * n + start, 16), size)
        return w.at[half, at, pl.ds(EARLY * part, HALF - EARLY if part else EARLY)]

    y_prev = lax.rem(y + 3, 4)
    y_next = lax.rem(y + 1, 4)
    y_far = lax.rem(y + 2, 4)

    def weight_copy(block, n, part, to_f, to_p):
        n = n + 17 * part
        return remote(block, block, ws.at[n], wr.at[n], to_f, to_p)

    def cross_send(far, part):
        block = rows(core, chip_of(y_far if far else y, 0), 0, 144, part)
        return weight_copy(block, 1 + far, part, cross_f, x_pair)

    def y_send(way, kind, part):
        block = rows(core, chip_of(y, kind), 0, 144, part)
        return weight_copy(block, 3 + way * 2 + kind, part, y_dn if way else y_up, p)

    def y_pass(way, part):
        n = chip_of(y_next if way else y_prev, 0)
        block = rows(core, n, 80 * way, 64 if way else 80, part)
        return weight_copy(block, 7 + way, part, y_dn if way else y_up, p)

    def y_pass_in(way, part):
        block = rows(core, chip_of(y_far, 0), 80 * way, 64 if way else 80, part)
        return weight_copy(block, 7 + way, part, other_core, p)

    def core_send(at_y, kind, part):
        n = chip_of(at_y, kind)
        return weight_copy(rows(core, n, 0, 144, part), 9 + n, part, other_core, p)

    def core_in(at_y, kind, part):
        n = chip_of(at_y, kind)
        return weight_copy(rows(1 - core, n, 0, 144, part), 9 + n, part, other_core, p)

    def near_rows(part):
        cross_send(0, part).wait_recv()
        for way in range(2):
            y_send(way, 0, part).wait_recv()
            y_pass(way, part).start()
        for way in range(2):
            y_send(way, 1, part).start()
        core_send(y, 1, part).start()
        core_send(y_prev, 0, part).start()
        core_send(y_next, 0, part).start()

    def far_rows(part):
        for way in range(2):
            y_pass_in(way, part).wait_recv()
        cross_send(1, part).start()
        core_send(y_far, 0, part).start()

    def crossed_rows(part):
        for way in range(2):
            y_send(way, 1, part).wait_recv()
        core_send(y_prev, 1, part).start()
        core_send(y_next, 1, part).start()

    def last_rows(part):
        cross_send(1, part).wait_recv()
        core_send(y_far, 1, part).start()

    def all_rows(part):
        for at_y in (y, y_prev, y_next, y_far):
            for kind in range(2):
                core_in(at_y, kind, part).wait_recv()

    for part in range(2):
        cross_send(0, part).start()
        for way in range(2):
            y_send(way, 0, part).start()
        core_send(y, 0, part).start()

    zero8 = jnp.zeros((8, TOK), F32)
    ones8 = jnp.where(lax.broadcasted_iota(jnp.int32, (8, TOK), 0) == 0, 1.0, 0.0)

    def to_natural(slot):
        kt = qkv[slot, ROWS : 2 * ROWS, :].astype(F32)
        kt = jnp.concatenate([kt, jnp.zeros((128 - ROWS, TOK), F32)], axis=0)
        kn[slot * TOK : slot * TOK + TOK, :] = kt.T.astype(BF16)

    def pair_copy(g):
        return remote(stage.at[g], qkv.at[2 * g + 1], xs.at[g], xr.at[g], f, x_pair)

    def project(g):
        for lane in (256, 0):
            r = jnp.dot(nz[g], wc[:, lane : lane + 256], preferred_element_type=F32)
            t = r.T
            block = [t[0:72] * Q_SCALE, zero8, t[72:144], zero8, t[144:216], ones8]
            block = jnp.concatenate(block, axis=0).astype(BF16)
            if lane:
                stage[g] = block
                pair_copy(g).start()
            else:
                qkv[2 * g] = block
        to_natural(2 * g)

    def receive(g):
        pair_copy(g).wait()
        to_natural(2 * g + 1)

    head = 2 * z + x_lo
    scores = (score_a, score_b)
    tops = (top_a, top_b)
    top_all[...] = jnp.full(top_all.shape, -1e30, F32)
    acc_all[...] = jnp.zeros(acc_all.shape, F32)

    def out_copy(g, odd, half):
        s = (g + 1) // 2
        if isinstance(g, int):
            batch = half if g in (0, 7) else (g + 1) % 2
        else:
            batch = lax.rem(g + 1, 2)
        to = (1 - x_lo if odd else x_lo) * 8 + lax.rem(z + (s if half else 8 - s), 8)
        n = 2 * odd + half
        return remote(
            ostage.at[g, n], attn.at[head, batch], os.at[4 * g + n], orr.at[2 * head + batch], f, to
        )

    def emit(g, o):
        both = isinstance(g, int) and g in (0, 7)
        o = jnp.concatenate([o, jnp.zeros((8, 2 * TOK), F32)], axis=0).astype(BF16)
        for odd in range(2):
            for half in range(2):
                n = 2 * odd + half
                ostage[g, n] = o[:, 128 * n : 128 * n + 128]
                if both and g + odd == 0:
                    attn[head, half] = ostage[g, n]
                elif not (both and half):
                    out_copy(g, odd, half).start()

    def score_steps(gq, gk, buf):
        q_t = jnp.concatenate([qkv[2 * gq, 0:ROWS, :], qkv[2 * gq + 1, 0:ROWS, :]], axis=1)
        state = [None]

        def one(u):
            at = pl.ds(pl.multiple_of(2 * TOK * gk + TOK * u, TOK), TOK)
            s = jnp.dot(kn[at, 0:ROWS], q_t, preferred_element_type=F32)
            scores[buf][TOK * u : TOK * u + TOK, :] = s
            m = jnp.max(s.reshape(TOK // 8, 8, 2 * TOK), axis=0)
            state[0] = m if state[0] is None else jnp.maximum(state[0], m)
            if u == 1:
                tops[buf][...] = state[0]

        return [lambda: one(0), lambda: one(1)]

    def job(gq, gk, buf, following, last):
        steps = score_steps(*following, 1 - buf) if following else None
        old = top_all[gq]
        m = jnp.maximum(old, jnp.max(tops[buf][...], axis=0, keepdims=True))
        acc = acc_all[gq] * jnp.exp2(old - m)
        for u in range(2):
            if steps:
                steps[u]()
            prob = jnp.exp2(scores[buf][TOK * u : TOK * u + TOK, :] - m).astype(BF16)
            acc += jnp.dot(
                qkv[2 * gk + u, 2 * ROWS : 3 * ROWS, :], prob, preferred_element_type=F32
            )
        if last:
            return acc[0:HEAD] / acc[HEAD : HEAD + 1]
        top_all[gq] = m
        acc_all[gq] = acc

    def jobs(pick, count, finish=False):
        for step in score_steps(*pick(0), 0):
            step()
        rest = 1 if count % 2 else 2

        def one(at, buf, following):
            o = job(*at, buf, following, finish)
            if finish:
                emit(at[0], o)

        def two(i, c):
            one(pick(2 * i), 0, pick(2 * i + 1))
            one(pick(2 * i + 1), 1, pick(2 * i + 2))
            return c

        if count > rest:
            lax.fori_loop(0, (count - rest) // 2, two, 0)
        for t in range(count - rest, count):
            following = pick(t + 1) if t + 1 < count else None
            one(pick(t), (t - count + rest) % 2, following)

    def group_jobs(g, begin, end):
        def pick(t):
            t = t + begin
            if isinstance(t, int):
                return (t, g) if t < g else (g, t - g)
            return jnp.where(t < g, t, g), jnp.where(t < g, g, t - g)

        jobs(pick, end - begin)

    arrive(1)

    def sel_take(i, c):
        peer = lax.rem(f + 2 * i, 16)
        sel_copy(wsel, peer, peer).wait_recv()
        remote(
            wsel_all.at[peer], wsel_all.at[peer], ss.at[peer + 1 - 2 * core], sr.at[peer], other_core, p
        ).start()
        return c

    lax.fori_loop(1, 8, sel_take, 0)

    def sel_swapped(i, c):
        n = lax.rem(other_core + 2 * i, 16)
        sel_copy(wsel, other_core, n).wait_recv()
        return c

    lax.fori_loop(0, 8, sel_swapped, 0)
    for j in range(8):
        a = wsel_all[2 * j, 0:72, :].astype(F32)
        b = wsel_all[2 * j + 1, 0:72, :].astype(F32)
        wc[144 * j : 144 * j + 144, :] = jnp.concatenate([a, b], axis=0).astype(BF16)
    project(0)
    project(1)
    arrive(2)
    project(2)
    receive(0)
    receive(1)
    group_jobs(0, 0, 1)
    group_jobs(1, 0, 3)
    arrive(3)
    near_rows(0)
    project(3)
    receive(2)
    group_jobs(2, 0, 5)
    arrive(4)
    near_rows(1)
    project(4)
    receive(3)
    group_jobs(3, 0, 7)
    arrive(5)
    far_rows(0)
    project(5)
    receive(4)
    group_jobs(4, 0, 9)
    receive(5)
    group_jobs(5, 0, 4)
    arrive(6)
    crossed_rows(0)
    project(6)
    group_jobs(5, 4, 11)
    far_rows(1)
    receive(6)
    group_jobs(6, 0, 4)
    arrive(7)
    project(7)
    last_rows(0)
    group_jobs(6, 4, 13)
    receive(7)

    jobs(lambda t: (0 if isinstance(t, int) and t == 3 else 5 - 2 * t, 7), 4, True)
    jobs(lambda t: (7, t), 7)
    jobs(lambda t: (7, 7), 1, True)
    for g, odd in ((7, 0), (7, 1), (0, 1)):
        out_copy(g, odd, 1).start()
    jobs(lambda t: (6 - 2 * t, 7), 3, True)

    all_rows(0)
    crossed_rows(1)

    def source(i):
        d = jnp.where(i < 12, 3 - i // 4, jnp.where(i < 14, 0, 4))
        odd = jnp.where(i < 12, lax.rem(i, 4) // 2, lax.rem(i, 2))
        lo = jnp.where(odd == 1, 1 - x_lo, x_lo)
        at_z = lax.rem(z + jnp.where(lax.rem(i, 2) == 1, d, 8 - d), 8)
        return lo, at_z

    def lay_out(i, c):
        lo, at_z = source(i)
        first = HEAD * (2 * at_z + lo)
        from_row = first // 16 * 16
        shifted = first > from_row
        for half, lane, size in ((0, 0, EARLY), (1, EARLY, D - EARLY)):
            block = w[half, pl.ds(pl.multiple_of(from_row, 16), ROWS), 0:size].astype(F32)
            block = jnp.where(shifted, block[ROWS - HEAD :], block[:HEAD])
            block = jnp.concatenate([block, jnp.zeros((128 - HEAD, size), F32)], axis=0)
            to = pl.ds(pl.multiple_of(128 * i, 128), 128)
            wo[to, lane : lane + size] = block.astype(BF16)
        return c

    lax.fori_loop(0, HEADS, lay_out, 0)

    def rows16(ref, n):
        return ref.at[pl.ds(pl.multiple_of(16 * n, 16), 16)]

    def pack(value):
        rest = jnp.concatenate([value[:, EARLY:], jnp.zeros((128, 2 * EARLY - D), F32)], axis=1)
        sides = [value[:, :EARLY].reshape(16, 8, EARLY), rest.reshape(16, 8, EARLY)]
        return jnp.concatenate(sides, axis=1).reshape(TOK, EARLY).astype(BF16)

    def unpack(ref):
        value = ref[...].astype(F32).reshape(16, 16, EARLY)
        return jnp.concatenate([value[:, 0:8], value[:, 8:16, 0 : D - EARLY]], axis=2).reshape(128, D)

    def swap_start(source, target, ssem, rsem, b):
        def send(i, c):
            peer = lax.rem(f + i, 16)
            remote(
                rows16(source.at[b], peer), rows16(target.at[b], f),
                ssem.at[16 * b + i], rsem.at[16 * b + f], peer, p,
            ).start()
            return c

        lax.fori_loop(1, 16, send, 0)
        here = pl.ds(pl.multiple_of(16 * f, 16), 16)
        target[b, here, :] = source[b, here, :]

    def swap_wait(source, target, ssem, rsem, b):
        def take(i, c):
            peer = lax.rem(f + i, 16)
            remote(
                rows16(source.at[b], peer), rows16(target.at[b], peer),
                ssem.at[16 * b + i], rsem.at[16 * b + peer], peer, p,
            ).wait()
            return c

        lax.fori_loop(1, 16, take, 0)

    for b in range(2):
        def out_take(i, c, b=b):
            lo, at_z = source(i)
            h = 2 * at_z + lo

            @pl.when(i != 12)
            def _():
                remote(
                    ostage.at[0, 0], attn.at[h, b], os.at[0], orr.at[2 * h + b], f, lo * 8 + at_z
                ).wait_recv()

            block = attn[h, b].astype(F32)
            block = jnp.concatenate([block, jnp.zeros((128 - ROWS, 128), F32)], axis=0)
            heads[:, pl.ds(pl.multiple_of(128 * i, 128), 128)] = block.T.astype(BF16)
            return c

        lax.fori_loop(0, HEADS, out_take, 0)
        r = jnp.dot(heads[...], wo[...], preferred_element_type=F32)
        mid = hid[128 * b : 128 * b + 128, :].astype(F32) + mod[2:3] * r
        midp[b] = pack(mid)
        swap_start(midp, midt, ms, mr, b)

    for g in range(1, 8):
        for way in range(2):
            z_hop(g, way).wait_send()

    def sel_sent(i, c):
        sel_copy(wsel, other_core, lax.rem(f + 2 * i, 16)).wait_send()
        sel_copy(wsel, other_core, lax.rem(other_core + 2 * i, 16)).wait_send()
        return c

    lax.fori_loop(1, 8, sel_sent, 0)
    sel_copy(wsel, other_core, f).wait_send()
    for g in range(8):
        for odd in range(2):
            for half in range(2):
                if g + odd > 0:
                    out_copy(g, odd, half).wait_send()
    last_rows(1)
    for part in range(2):
        for way in range(2):
            cross_send(way, part).wait_send()
            y_pass(way, part).wait_send()
            for kind in range(2):
                y_send(way, kind, part).wait_send()
        for at_y in (y, y_prev, y_next, y_far):
            for kind in range(2):
                core_send(at_y, kind, part).wait_send()
    all_rows(1)

    ri = lax.broadcasted_iota(jnp.int32, (128, 128), 0)
    ci = lax.broadcasted_iota(jnp.int32, (128, 128), 1)
    same = lax.rem(ri, 8) == lax.rem(ci, 8)
    lane = lax.broadcasted_iota(jnp.int32, (128, TOK), 1)
    for b in range(2):
        swap_wait(midp, midt, ms, mr, b)
        value = unpack(midt.at[b])
        normed = norm_modulate(value, mod[3:4], mod[4:5]).astype(BF16)
        r = jnp.dot(normed, w[0, :, EARLY:HALF], preferred_element_type=F32)
        qkv_t[:, 0:D] = (r[:, 0:D] * Q_SCALE).astype(BF16)
        qkv_t[:, D : 2 * D] = r[:, D:].astype(BF16)
        r = jnp.dot(normed, w[1, :, EARLY : EARLY + D], preferred_element_type=F32)
        qkv_t[:, 2 * D :] = r.astype(BF16)
        acc_t[...] = jnp.zeros_like(acc_t)
        for h in range(HEADS):
            start = 128 * min(HEAD * h // 128, 7)
            low = HEAD * h - start
            inside = (lane >= low) & (lane < low + HEAD)
            q = qkv_t[:, start : start + 256]
            q = jnp.where(inside, q, jnp.zeros_like(q))
            k = qkv_t[:, D + start : D + start + 256]
            v = qkv_t[:, 2 * D + start : 2 * D + start + 256]
            s = lax.dot_general(q, k, (((1,), (1,)), ((), ())), preferred_element_type=F32)
            s = jnp.where(same, s, -1e30)
            prob = jnp.exp2(s - jnp.max(s, axis=1, keepdims=True))
            total = jnp.sum(prob, axis=1, keepdims=True)
            o = jnp.dot(prob.astype(BF16), v, preferred_element_type=F32) / total
            acc_t[:, start : start + 256] = jnp.where(inside, o, acc_t[:, start : start + 256])
        r = jnp.dot(acc_t[...].astype(BF16), w[1, :, EARLY + D : HALF], preferred_element_type=F32)
        osend[b] = pack(unpack(midt.at[b]) + mod[5:6] * r)
        swap_start(osend, outp, bs, br, b)
    for b in range(2):
        swap_wait(osend, outp, bs, br, b)
        out[128 * b : 128 * b + 128, :] = unpack(outp.at[b]).astype(BF16)


VMEM = pl.BlockSpec(memory_space=pltpu.VMEM)


def block_call(*args):
    dma = pltpu.SemaphoreType.DMA
    return pl.pallas_call(
        block_kernel,
        out_shape=jax.ShapeDtypeStruct((TOK, D), BF16),
        in_specs=[VMEM] * 6,
        out_specs=VMEM,
        scratch_shapes=[
            pltpu.VMEM((8, TOK, D), BF16),
            pltpu.VMEM((ROWS, 512), BF16),
            pltpu.VMEM((2, ROWS, HALF), BF16),
            pltpu.VMEM((HEADS * 128, D), BF16),
            pltpu.VMEM((128, HEADS * 128), BF16),
            pltpu.VMEM((16, ROWS, 512), BF16),
            pltpu.VMEM((D, 512), BF16),
            pltpu.VMEM((16, 3 * ROWS, TOK), BF16),
            pltpu.VMEM((8, 3 * ROWS, TOK), BF16),
            pltpu.VMEM((4096, 128), BF16),
            pltpu.VMEM((8, 4, ROWS, 128), BF16),
            pltpu.VMEM((HEADS, 2, ROWS, 128), BF16),
            pltpu.VMEM((ROWS, HALF), BF16),
            pltpu.VMEM((2, D, HALF), BF16),
            pltpu.VMEM((2 * TOK, 2 * TOK), F32),
            pltpu.VMEM((2 * TOK, 2 * TOK), F32),
            pltpu.VMEM((8, 2 * TOK), F32),
            pltpu.VMEM((8, 2 * TOK), F32),
            pltpu.VMEM((8, 1, 2 * TOK), F32),
            pltpu.VMEM((8, ROWS, 2 * TOK), F32),
            pltpu.VMEM((2, TOK, EARLY), BF16),
            pltpu.VMEM((2, TOK, EARLY), BF16),
            pltpu.VMEM((128, 3 * D), BF16),
            pltpu.VMEM((128, D), F32),
            pltpu.VMEM((2, TOK, EARLY), BF16),
            pltpu.VMEM((2, TOK, EARLY), BF16),
            dma((16,)), dma((16,)),
            dma((16,)), dma((16,)),
            dma((8,)), dma((8,)),
            dma((32,)), dma((32,)),
            dma((34,)), dma((34,)),
            dma((32,)), dma((32,)),
            dma((32,)), dma((32,)),
        ],
        compiler_params=pltpu.CompilerParams(
            collective_id=0, has_side_effects=True, vmem_limit_bytes=60 * 1024 * 1024
        ),
        name="block",
    )(*args)


def body(hidden_states, modulation, w_qkv_spatial, w_out_spatial, w_qkv_temporal, w_out_temporal):
    out = block_call(
        hidden_states.reshape(TOK, D),
        modulation,
        w_qkv_spatial,
        w_out_spatial,
        w_qkv_temporal,
        w_out_temporal,
    )
    return out.reshape(1, TOK, D)


def solution(mesh):
    in_specs = (
        P("frame", "patch", None),
        P(),
        P("frame", None),
        P("frame", None),
        P("frame", None),
        P("frame", None),
    )
    out_specs = P("frame", "patch", None)
    return jax.shard_map(body, mesh=mesh, in_specs=in_specs, out_specs=out_specs, check_vma=False)
```

```python
import math

import jax
import jax.numpy as jnp
from jax import lax
from jax.experimental import pallas as pl
from jax.experimental.pallas import tpu as pltpu
from jax.sharding import PartitionSpec as P

HEAD = 72
HEADS = 16
D = 1152
TOK = 256
ROWS = 80
HALF = 2944
EARLY = 640
Q_SCALE = HEAD ** (-0.5) * math.log2(math.e)
F32 = jnp.float32
BF16 = jnp.bfloat16


def remote(src, dst, send, recv, frame, patch):
    return pltpu.make_async_remote_copy(
        src_ref=src,
        dst_ref=dst,
        send_sem=send,
        recv_sem=recv,
        device_id={"frame": frame, "patch": patch},
        device_id_type=pl.DeviceIdType.MESH,
    )


def signal(sem, frame, patch):
    pl.semaphore_signal(
        sem, inc=1, device_id={"frame": frame, "patch": patch}, device_id_type=pl.DeviceIdType.MESH
    )


def norm_modulate(x, shift, scale):
    centred = x - jnp.mean(x, axis=-1, keepdims=True)
    variance = jnp.mean(centred * centred, axis=-1, keepdims=True)
    return centred * lax.rsqrt(variance + 1e-06) * (1.0 + scale) + shift


def block_kernel(
    hid, mod, w_qkv_s, w_out_s, w_qkv_t, w_out_t, out,
    nz, wsel, wrest, wo, heads, wsel_all, wc, qkv, stage, kn, ostage, attn, w1, w, score_a, score_b, top_a, top_b, top_all, acc_all,
    midp, midt, qkv_t, acc_t, osend, outp, done,
    zs, zr, ss, sr, xs, xr, os, orr, ws, wr, ms, mr, bs, br, ls,
):
    f = lax.axis_index("frame")
    p = lax.axis_index("patch")
    core = lax.rem(f, 2)
    x_hi = lax.rem(f // 2, 2)
    y = f // 4
    x_lo = p // 8
    z = lax.rem(p, 8)
    chip = f // 2
    other_core = f + 1 - 2 * core
    cross_f = (y * 2 + 1 - x_hi) * 2 + core
    x_pair = (1 - x_lo) * 8 + z
    y_up = lax.rem(y + 1, 4) * 4 + x_hi * 2 + core
    y_dn = lax.rem(y + 3, 4) * 4 + x_hi * 2 + core
    z_up = x_lo * 8 + lax.rem(z + 1, 8)
    z_dn = x_lo * 8 + lax.rem(z + 7, 8)

    barrier = pltpu.get_barrier_semaphore()

    for i in range(1, 16):
        signal(barrier, f, lax.rem(p + i, 16))
        signal(barrier, lax.rem(f + i, 16), p)
    signal(barrier, cross_f, x_pair)
    nz[0] = norm_modulate(hid[...].astype(F32), mod[0:1], mod[1:2]).astype(BF16)

    lanes = lax.broadcasted_iota(jnp.int32, (HEAD, TOK), 1)
    own, other = [], []
    for part in range(3):
        at = pl.ds(pl.multiple_of(D * part + 128 * z, 128), TOK)
        window = w_qkv_s[:, at].astype(F32)
        inside = (lanes >= HEAD * part) & (lanes < HEAD * part + HEAD)
        for which, found in ((x_lo, own), (1 - x_lo, other)):
            shift = lax.rem(2 * TOK - 16 * z - HEAD * which + HEAD * part, TOK)
            found.append(jnp.where(inside, pltpu.roll(window, shift, axis=1), 0.0))
    sel = jnp.concatenate([own[0] + own[1] + own[2], other[0] + other[1] + other[2]], axis=1)

    def to_rows(value):
        tail = jnp.zeros((ROWS - HEAD, value.shape[1]), F32)
        return jnp.concatenate([value.astype(F32), tail], axis=0).astype(BF16)

    wsel[...] = to_rows(sel)
    wrest[0, :, 0:EARLY] = to_rows(w_out_s[:, 0:EARLY])
    wrest[0, :, EARLY:HALF] = to_rows(w_qkv_t[:, 0 : 2 * D])
    wrest[1, :, 0 : D - EARLY] = to_rows(w_out_s[:, EARLY:D])
    wrest[1, :, D - EARLY : EARLY] = jnp.zeros((ROWS, 2 * EARLY - D), BF16)
    wrest[1, :, EARLY : EARLY + D] = to_rows(w_qkv_t[:, 2 * D : 3 * D])
    wrest[1, :, EARLY + D : HALF] = to_rows(w_out_t[...])
    pl.semaphore_wait(barrier, 31)

    def z_block(g, way):
        return nz.at[g, pl.ds(128 * way, 128)]

    def z_hop(g, way):
        if g <= 2:
            source = nz.at[0, pl.ds(128 * (g - 1), 128)]
        elif g <= 6:
            source = z_block(g - 2, way)
        else:
            source = z_block(5 + way, way)
        n = 2 * g + way
        return remote(source, z_block(g, way), zs.at[n], zr.at[n], f, z_dn if way else z_up)

    for g in (1, 2):
        for way in range(2):
            z_hop(g, way).start()

    def arrive(g):
        for way in range(2):
            z_hop(g, way).wait_recv()
            if g <= 4:
                z_hop(g + 2, way).start()
            elif g == 5 + way:
                z_hop(7, way).start()

    first = remote(wrest.at[1 - core], w1, ws.at[0], wr.at[0], other_core, p)
    first.start()

    def sel_copy(source, peer, n):
        return remote(source, wsel_all.at[n], ss.at[n], sr.at[n], peer, p)

    sel_copy(wsel, other_core, f).start()

    def sel_send(i, c):
        peer = lax.rem(f + 2 * i, 16)
        remote(wsel, wsel_all.at[f], ss.at[peer], sr.at[f], peer, p).start()
        return c

    lax.fori_loop(1, 8, sel_send, 0)
    wsel_all[f] = wsel[...]

    first.wait()
    mine = wrest[core, 0:72, :].astype(F32)
    theirs = w1[0:72, :].astype(F32)
    is_first = core == 0
    low = jnp.where(is_first, mine, theirs)
    high = jnp.where(is_first, theirs, mine)
    w[core, pl.ds(pl.multiple_of(144 * chip, 144), 144), :] = jnp.concatenate(
        [low, high], axis=0
    ).astype(BF16)

    def chip_of(at_y, kind):
        return 2 * at_y + (x_hi if kind == 0 else 1 - x_hi)

    def rows(half, n, start, size, part):
        at = pl.ds(pl.multiple_of(144 * n + start, 16), size)
        return w.at[half, at, pl.ds(EARLY * part, HALF - EARLY if part else EARLY)]

    y_prev = lax.rem(y + 3, 4)
    y_next = lax.rem(y + 1, 4)
    y_far = lax.rem(y + 2, 4)

    def weight_copy(block, n, part, to_f, to_p):
        n = n + 17 * part
        return remote(block, block, ws.at[n], wr.at[n], to_f, to_p)

    def cross_send(far, part):
        block = rows(core, chip_of(y_far if far else y, 0), 0, 144, part)
        return weight_copy(block, 1 + far, part, cross_f, x_pair)

    def y_send(way, kind, part):
        block = rows(core, chip_of(y, kind), 0, 144, part)
        return weight_copy(block, 3 + way * 2 + kind, part, y_dn if way else y_up, p)

    def y_pass(way, part):
        n = chip_of(y_next if way else y_prev, 0)
        block = rows(core, n, 80 * way, 64 if way else 80, part)
        return weight_copy(block, 7 + way, part, y_dn if way else y_up, p)

    def y_pass_in(way, part):
        block = rows(core, chip_of(y_far, 0), 80 * way, 64 if way else 80, part)
        return weight_copy(block, 7 + way, part, other_core, p)

    def core_send(at_y, kind, part):
        n = chip_of(at_y, kind)
        return weight_copy(rows(core, n, 0, 144, part), 9 + n, part, other_core, p)

    def core_in(at_y, kind, part):
        n = chip_of(at_y, kind)
        return weight_copy(rows(1 - core, n, 0, 144, part), 9 + n, part, other_core, p)

    def near_rows(part):
        cross_send(0, part).wait_recv()
        for way in range(2):
            y_send(way, 0, part).wait_recv()
            y_pass(way, part).start()
        for way in range(2):
            y_send(way, 1, part).start()
        core_send(y, 1, part).start()
        core_send(y_prev, 0, part).start()
        core_send(y_next, 0, part).start()

    def far_rows(part):
        for way in range(2):
            y_pass_in(way, part).wait_recv()
        cross_send(1, part).start()
        core_send(y_far, 0, part).start()

    def crossed_rows(part):
        for way in range(2):
            y_send(way, 1, part).wait_recv()
        core_send(y_prev, 1, part).start()
        core_send(y_next, 1, part).start()

    def last_rows(part):
        cross_send(1, part).wait_recv()
        core_send(y_far, 1, part).start()

    def all_rows(part):
        for at_y in (y, y_prev, y_next, y_far):
            for kind in range(2):
                core_in(at_y, kind, part).wait_recv()

    for part in range(2):
        cross_send(0, part).start()
        for way in range(2):
            y_send(way, 0, part).start()
        core_send(y, 0, part).start()

    zero8 = jnp.zeros((8, TOK), F32)
    ones8 = jnp.where(lax.broadcasted_iota(jnp.int32, (8, TOK), 0) == 0, 1.0, 0.0)

    def to_natural(slot):
        kt = qkv[slot, ROWS : 2 * ROWS, :].astype(F32)
        kt = jnp.concatenate([kt, jnp.zeros((128 - ROWS, TOK), F32)], axis=0)
        kn[slot * TOK : slot * TOK + TOK, :] = kt.T.astype(BF16)

    def pair_copy(g, start=0, size=3 * ROWS):
        n = 8 if g == 7 and start == 0 else g
        at = pl.ds(start, size)
        return remote(stage.at[g, at], qkv.at[2 * g + 1, at], xs.at[n], xr.at[n], f, x_pair)

    def project(g):
        for lane in (256, 0):
            r = jnp.dot(nz[g], wc[:, lane : lane + 256], preferred_element_type=F32)
            t = r.T
            block = [t[0:72] * Q_SCALE, zero8, t[72:144], zero8, t[144:216], ones8]
            block = jnp.concatenate(block, axis=0).astype(BF16)
            if lane:
                stage[g] = block
                if g == 7:
                    pair_copy(g, ROWS, 2 * ROWS).start()
                    pair_copy(g, 0, ROWS).start()
                else:
                    pair_copy(g).start()
            else:
                qkv[2 * g] = block
        to_natural(2 * g)

    def receive(g):
        if g == 7:
            pair_copy(g, ROWS, 2 * ROWS).wait()
        else:
            pair_copy(g).wait()
        to_natural(2 * g + 1)

    head = 2 * z + x_lo
    scores = (score_a, score_b)
    tops = (top_a, top_b)
    top_all[...] = jnp.full(top_all.shape, -1e30, F32)
    acc_all[...] = jnp.zeros(acc_all.shape, F32)

    def out_copy(g, odd, half):
        s = (g + 1) // 2
        if isinstance(g, int):
            batch = half if g in (0, 7) else (g + 1) % 2
        else:
            batch = lax.rem(g + 1, 2)
        to = (1 - x_lo if odd else x_lo) * 8 + lax.rem(z + (s if half else 8 - s), 8)
        n = 2 * odd + half
        return remote(
            ostage.at[g, n], attn.at[head, batch], os.at[4 * g + n], orr.at[2 * head + batch], f, to
        )

    def emit(g, o):
        both = isinstance(g, int) and g in (0, 7)
        o = jnp.concatenate([o, jnp.zeros((8, 2 * TOK), F32)], axis=0).astype(BF16)
        for odd in range(2):
            for half in range(2):
                n = 2 * odd + half
                ostage[g, n] = o[:, 128 * n : 128 * n + 128]
                if both and g + odd == 0:
                    attn[head, half] = ostage[g, n]
                elif not (both and half):
                    out_copy(g, odd, half).start()

    def score_steps(gq, gk, buf):
        q_t = jnp.concatenate([qkv[2 * gq, 0:ROWS, :], qkv[2 * gq + 1, 0:ROWS, :]], axis=1)
        state = [None]

        def one(u):
            at = pl.ds(pl.multiple_of(2 * TOK * gk + TOK * u, TOK), TOK)
            s = jnp.dot(kn[at, 0:ROWS], q_t, preferred_element_type=F32)
            scores[buf][TOK * u : TOK * u + TOK, :] = s
            m = jnp.max(s.reshape(TOK // 8, 8, 2 * TOK), axis=0)
            state[0] = m if state[0] is None else jnp.maximum(state[0], m)
            if u == 1:
                tops[buf][...] = state[0]

        return [lambda: one(0), lambda: one(1)]

    def job(gq, gk, buf, following, last):
        steps = score_steps(*following, 1 - buf) if following else None
        old = top_all[gq]
        m = jnp.maximum(old, jnp.max(tops[buf][...], axis=0, keepdims=True))
        acc = acc_all[gq] * jnp.exp2(old - m)
        for u in range(2):
            if steps:
                steps[u]()
            prob = jnp.exp2(scores[buf][TOK * u : TOK * u + TOK, :] - m).astype(BF16)
            acc += jnp.dot(
                qkv[2 * gk + u, 2 * ROWS : 3 * ROWS, :], prob, preferred_element_type=F32
            )
        if last:
            return acc[0:HEAD] / acc[HEAD : HEAD + 1]
        top_all[gq] = m
        acc_all[gq] = acc

    def jobs(pick, count, finish=False):
        for step in score_steps(*pick(0), 0):
            step()
        rest = 1 if count % 2 else 2

        def one(at, buf, following):
            o = job(*at, buf, following, finish)
            if finish:
                emit(at[0], o)

        def two(i, c):
            one(pick(2 * i), 0, pick(2 * i + 1))
            one(pick(2 * i + 1), 1, pick(2 * i + 2))
            return c

        if count > rest:
            lax.fori_loop(0, (count - rest) // 2, two, 0)
        for t in range(count - rest, count):
            following = pick(t + 1) if t + 1 < count else None
            one(pick(t), (t - count + rest) % 2, following)

    def group_jobs(g, begin, end):
        def pick(t):
            t = t + begin
            if isinstance(t, int):
                return (t, g) if t < g else (g, t - g)
            return jnp.where(t < g, t, g), jnp.where(t < g, g, t - g)

        jobs(pick, end - begin)

    arrive(1)

    def sel_take(i, c):
        peer = lax.rem(f + 2 * i, 16)
        sel_copy(wsel, peer, peer).wait_recv()
        remote(
            wsel_all.at[peer], wsel_all.at[peer], ss.at[peer + 1 - 2 * core], sr.at[peer], other_core, p
        ).start()
        return c

    lax.fori_loop(1, 8, sel_take, 0)

    def sel_swapped(i, c):
        n = lax.rem(other_core + 2 * i, 16)
        sel_copy(wsel, other_core, n).wait_recv()
        return c

    lax.fori_loop(0, 8, sel_swapped, 0)
    for j in range(8):
        a = wsel_all[2 * j, 0:72, :].astype(F32)
        b = wsel_all[2 * j + 1, 0:72, :].astype(F32)
        wc[144 * j : 144 * j + 144, :] = jnp.concatenate([a, b], axis=0).astype(BF16)
    project(0)
    project(1)
    arrive(2)
    project(2)
    receive(0)
    receive(1)
    group_jobs(0, 0, 1)
    group_jobs(1, 0, 3)
    arrive(3)
    near_rows(0)
    project(3)
    receive(2)
    group_jobs(2, 0, 5)
    arrive(4)
    near_rows(1)
    project(4)
    receive(3)
    group_jobs(3, 0, 7)
    arrive(5)
    far_rows(0)
    project(5)
    receive(4)
    group_jobs(4, 0, 9)
    receive(5)
    group_jobs(5, 0, 4)
    arrive(6)
    crossed_rows(0)
    project(6)
    group_jobs(5, 4, 11)
    far_rows(1)
    receive(6)
    group_jobs(6, 0, 4)
    arrive(7)
    project(7)
    last_rows(0)
    group_jobs(6, 4, 13)
    receive(7)

    jobs(lambda t: (0 if isinstance(t, int) and t == 3 else 5 - 2 * t, 7), 4, True)
    pair_copy(7, 0, ROWS).wait()
    jobs(lambda t: (7, t), 7)
    jobs(lambda t: (7, 7), 1, True)
    for g, odd in ((7, 0), (7, 1), (0, 1)):
        out_copy(g, odd, 1).start()
    jobs(lambda t: (6 - 2 * t, 7), 3, True)

    all_rows(0)
    crossed_rows(1)

    def source(i):
        d = jnp.where(i < 12, 3 - i // 4, jnp.where(i < 14, 0, 4))
        odd = jnp.where(i < 12, lax.rem(i, 4) // 2, lax.rem(i, 2))
        lo = jnp.where(odd == 1, 1 - x_lo, x_lo)
        at_z = lax.rem(z + jnp.where(lax.rem(i, 2) == 1, d, 8 - d), 8)
        return lo, at_z

    def lay_out(i, c):
        lo, at_z = source(i)
        first = HEAD * (2 * at_z + lo)
        from_row = first // 16 * 16
        shifted = first > from_row
        for half, lane, size in ((0, 0, EARLY), (1, EARLY, D - EARLY)):
            block = w[half, pl.ds(pl.multiple_of(from_row, 16), ROWS), 0:size].astype(F32)
            block = jnp.where(shifted, block[ROWS - HEAD :], block[:HEAD])
            block = jnp.concatenate([block, jnp.zeros((128 - HEAD, size), F32)], axis=0)
            to = pl.ds(pl.multiple_of(128 * i, 128), 128)
            wo[to, lane : lane + size] = block.astype(BF16)
        return c

    lax.fori_loop(0, HEADS, lay_out, 0)

    def rows16(ref, n):
        return ref.at[pl.ds(pl.multiple_of(16 * n, 16), 16)]

    def pack(value):
        rest = jnp.concatenate([value[:, EARLY:], jnp.zeros((128, 2 * EARLY - D), F32)], axis=1)
        sides = [value[:, :EARLY].reshape(16, 8, EARLY), rest.reshape(16, 8, EARLY)]
        return jnp.concatenate(sides, axis=1).reshape(TOK, EARLY).astype(BF16)

    def unpack(ref):
        value = ref[...].astype(F32).reshape(16, 16, EARLY)
        return jnp.concatenate([value[:, 0:8], value[:, 8:16, 0 : D - EARLY]], axis=2).reshape(128, D)

    steps = [(j // 4, j // 2 % 2, j % 2) for j in range(1, 16)]
    steps.sort(key=lambda j: -(min(j[0], 4 - j[0]) + 2 * j[1]))

    def swap_peer(n):
        dy, dx, dc = steps[n]
        at_x = 1 - x_hi if dx else x_hi
        return lax.rem(y + dy, 4) * 4 + at_x * 2 + (1 - core if dc else core)

    def swap_copy(source, target, ssem, rsem, b, n, to, at):
        return remote(
            rows16(source.at[b], to), rows16(target.at[b], at),
            ssem.at[16 * b + n], rsem.at[16 * b + at], to, p,
        )

    def swap_start(source, target, ssem, rsem, b):
        for n in range(15):
            swap_copy(source, target, ssem, rsem, b, n, swap_peer(n), f).start()
        here = pl.ds(pl.multiple_of(16 * f, 16), 16)
        target[b, here, :] = source[b, here, :]

    def swap_wait(source, target, ssem, rsem, b):
        for n in range(15):
            peer = swap_peer(n)
            swap_copy(source, target, ssem, rsem, b, n, peer, peer).wait()

    for b in range(2):
        def out_take(i, c, b=b):
            lo, at_z = source(i)
            h = 2 * at_z + lo

            @pl.when(i != 12)
            def _():
                remote(
                    ostage.at[0, 0], attn.at[h, b], os.at[0], orr.at[2 * h + b], f, lo * 8 + at_z
                ).wait_recv()

            block = attn[h, b].astype(F32)
            block = jnp.concatenate([block, jnp.zeros((128 - ROWS, 128), F32)], axis=0)
            heads[:, pl.ds(pl.multiple_of(128 * i, 128), 128)] = block.T.astype(BF16)
            return c

        lax.fori_loop(0, HEADS, out_take, 0)
        r = jnp.dot(heads[...], wo[...], preferred_element_type=F32)
        mid = hid[128 * b : 128 * b + 128, :].astype(F32) + mod[2:3] * r
        midp[b] = pack(mid)
        swap_start(midp, midt, ms, mr, b)

    for g in range(1, 8):
        for way in range(2):
            z_hop(g, way).wait_send()

    def sel_sent(i, c):
        sel_copy(wsel, other_core, lax.rem(f + 2 * i, 16)).wait_send()
        sel_copy(wsel, other_core, lax.rem(other_core + 2 * i, 16)).wait_send()
        return c

    lax.fori_loop(1, 8, sel_sent, 0)
    sel_copy(wsel, other_core, f).wait_send()
    for g in range(8):
        for odd in range(2):
            for half in range(2):
                if g + odd > 0:
                    out_copy(g, odd, half).wait_send()
    last_rows(1)
    for part in range(2):
        for way in range(2):
            cross_send(way, part).wait_send()
            y_pass(way, part).wait_send()
            for kind in range(2):
                y_send(way, kind, part).wait_send()
        for at_y in (y, y_prev, y_next, y_far):
            for kind in range(2):
                core_send(at_y, kind, part).wait_send()
    all_rows(1)

    ri = lax.broadcasted_iota(jnp.int32, (128, 128), 0)
    ci = lax.broadcasted_iota(jnp.int32, (128, 128), 1)
    same = lax.rem(ri, 8) == lax.rem(ci, 8)
    lane = lax.broadcasted_iota(jnp.int32, (128, TOK), 1)
    for b in range(2):
        swap_wait(midp, midt, ms, mr, b)
        value = unpack(midt.at[b])
        normed = norm_modulate(value, mod[3:4], mod[4:5]).astype(BF16)
        r = jnp.dot(normed, w[0, :, EARLY:HALF], preferred_element_type=F32)
        qkv_t[:, 0:D] = (r[:, 0:D] * Q_SCALE).astype(BF16)
        qkv_t[:, D : 2 * D] = r[:, D:].astype(BF16)
        r = jnp.dot(normed, w[1, :, EARLY : EARLY + D], preferred_element_type=F32)
        qkv_t[:, 2 * D :] = r.astype(BF16)
        acc_t[...] = jnp.zeros_like(acc_t)
        for h in range(HEADS):
            start = 128 * min(HEAD * h // 128, 7)
            low = HEAD * h - start
            inside = (lane >= low) & (lane < low + HEAD)
            q = qkv_t[:, start : start + 256]
            q = jnp.where(inside, q, jnp.zeros_like(q))
            k = qkv_t[:, D + start : D + start + 256]
            v = qkv_t[:, 2 * D + start : 2 * D + start + 256]
            s = lax.dot_general(q, k, (((1,), (1,)), ((), ())), preferred_element_type=F32)
            s = jnp.where(same, s, -1e30)
            prob = jnp.exp2(s - jnp.max(s, axis=1, keepdims=True))
            total = jnp.sum(prob, axis=1, keepdims=True)
            o = jnp.dot(prob.astype(BF16), v, preferred_element_type=F32) / total
            acc_t[:, start : start + 256] = jnp.where(inside, o, acc_t[:, start : start + 256])
        r = jnp.dot(acc_t[...].astype(BF16), w[1, :, EARLY + D : HALF], preferred_element_type=F32)
        osend[b] = pack(unpack(midt.at[b]) + mod[5:6] * r)
        swap_start(osend, outp, bs, br, b)

    def leave(b):
        at = pl.ds(128 * b, 128)
        return pltpu.make_async_copy(done.at[at], out.at[at], ls.at[b])

    for b in range(2):
        swap_wait(osend, outp, bs, br, b)
        done[128 * b : 128 * b + 128, :] = unpack(outp.at[b]).astype(BF16)
        leave(b).start()
    for b in range(2):
        leave(b).wait()


VMEM = pl.BlockSpec(memory_space=pltpu.VMEM)


def block_call(*args):
    dma = pltpu.SemaphoreType.DMA
    return pl.pallas_call(
        block_kernel,
        out_shape=jax.ShapeDtypeStruct((TOK, D), BF16),
        in_specs=[VMEM] * 6,
        out_specs=pl.BlockSpec(memory_space=pl.ANY),
        scratch_shapes=[
            pltpu.VMEM((8, TOK, D), BF16),
            pltpu.VMEM((ROWS, 512), BF16),
            pltpu.VMEM((2, ROWS, HALF), BF16),
            pltpu.VMEM((HEADS * 128, D), BF16),
            pltpu.VMEM((128, HEADS * 128), BF16),
            pltpu.VMEM((16, ROWS, 512), BF16),
            pltpu.VMEM((D, 512), BF16),
            pltpu.VMEM((16, 3 * ROWS, TOK), BF16),
            pltpu.VMEM((8, 3 * ROWS, TOK), BF16),
            pltpu.VMEM((4096, 128), BF16),
            pltpu.VMEM((8, 4, ROWS, 128), BF16),
            pltpu.VMEM((HEADS, 2, ROWS, 128), BF16),
            pltpu.VMEM((ROWS, HALF), BF16),
            pltpu.VMEM((2, D, HALF), BF16),
            pltpu.VMEM((2 * TOK, 2 * TOK), F32),
            pltpu.VMEM((2 * TOK, 2 * TOK), F32),
            pltpu.VMEM((8, 2 * TOK), F32),
            pltpu.VMEM((8, 2 * TOK), F32),
            pltpu.VMEM((8, 1, 2 * TOK), F32),
            pltpu.VMEM((8, ROWS, 2 * TOK), F32),
            pltpu.VMEM((2, TOK, EARLY), BF16),
            pltpu.VMEM((2, TOK, EARLY), BF16),
            pltpu.VMEM((128, 3 * D), BF16),
            pltpu.VMEM((128, D), F32),
            pltpu.VMEM((2, TOK, EARLY), BF16),
            pltpu.VMEM((2, TOK, EARLY), BF16),
            pltpu.VMEM((TOK, D), BF16),
            dma((16,)), dma((16,)),
            dma((16,)), dma((16,)),
            dma((9,)), dma((9,)),
            dma((32,)), dma((32,)),
            dma((34,)), dma((34,)),
            dma((32,)), dma((32,)),
            dma((32,)), dma((32,)),
            dma((2,)),
        ],
        compiler_params=pltpu.CompilerParams(
            collective_id=0, has_side_effects=True, vmem_limit_bytes=60 * 1024 * 1024
        ),
        name="block",
    )(*args)


def body(hidden_states, modulation, w_qkv_spatial, w_out_spatial, w_qkv_temporal, w_out_temporal):
    out = block_call(
        hidden_states.reshape(TOK, D),
        modulation,
        w_qkv_spatial,
        w_out_spatial,
        w_qkv_temporal,
        w_out_temporal,
    )
    return out.reshape(1, TOK, D)


def solution(mesh):
    in_specs = (
        P("frame", "patch", None),
        P(),
        P("frame", None),
        P("frame", None),
        P("frame", None),
        P("frame", None),
    )
    out_specs = P("frame", "patch", None)
    return jax.shard_map(body, mesh=mesh, in_specs=in_specs, out_specs=out_specs, check_vma=False)
```

```python
import math

import jax
import jax.numpy as jnp
from jax import lax
from jax.experimental import pallas as pl
from jax.experimental.pallas import tpu as pltpu
from jax.sharding import PartitionSpec as P

HEAD = 72
HEADS = 16
D = 1152
TOK = 256
ROWS = 80
HALF = 2944
EARLY = 640
Q_SCALE = HEAD ** (-0.5) * math.log2(math.e)
F32 = jnp.float32
BF16 = jnp.bfloat16


def remote(src, dst, send, recv, frame, patch):
    return pltpu.make_async_remote_copy(
        src_ref=src,
        dst_ref=dst,
        send_sem=send,
        recv_sem=recv,
        device_id={"frame": frame, "patch": patch},
        device_id_type=pl.DeviceIdType.MESH,
    )


def signal(sem, frame, patch):
    pl.semaphore_signal(
        sem, inc=1, device_id={"frame": frame, "patch": patch}, device_id_type=pl.DeviceIdType.MESH
    )


def norm_modulate(x, shift, scale):
    centred = x - jnp.mean(x, axis=-1, keepdims=True)
    variance = jnp.mean(centred * centred, axis=-1, keepdims=True)
    return centred * lax.rsqrt(variance + 1e-06) * (1.0 + scale) + shift


def block_kernel(
    hid, mod, w_qkv_s, w_out_s, w_qkv_t, w_out_t, out,
    nz, wsel, wrest, wo, heads, wsel_all, wc, qkv, stage, kn, ostage, attn, w1, w, score_a, score_b, top_a, top_b, top_all, acc_all,
    midp, midt, qkv_t, acc_t, osend,
    zs, zr, ss, sr, xs, xr, os, orr, ws, wr, ms, mr, bs, br, ls,
):
    f = lax.axis_index("frame")
    p = lax.axis_index("patch")
    core = lax.rem(f, 2)
    x_hi = lax.rem(f // 2, 2)
    y = f // 4
    x_lo = p // 8
    z = lax.rem(p, 8)
    chip = f // 2
    other_core = f + 1 - 2 * core
    cross_f = (y * 2 + 1 - x_hi) * 2 + core
    x_pair = (1 - x_lo) * 8 + z
    y_up = lax.rem(y + 1, 4) * 4 + x_hi * 2 + core
    y_dn = lax.rem(y + 3, 4) * 4 + x_hi * 2 + core
    z_up = x_lo * 8 + lax.rem(z + 1, 8)
    z_dn = x_lo * 8 + lax.rem(z + 7, 8)

    barrier = pltpu.get_barrier_semaphore()

    for i in range(1, 16):
        signal(barrier, f, lax.rem(p + i, 16))
        signal(barrier, lax.rem(f + i, 16), p)
    signal(barrier, cross_f, x_pair)

    def norm_rows(at):
        value = norm_modulate(hid[at : at + 128, :].astype(F32), mod[0:1], mod[1:2])
        nz[0, at : at + 128, :] = value.astype(BF16)

    norm_rows(0)

    pl.semaphore_wait(barrier, 31)

    def z_block(g, way):
        return nz.at[g, pl.ds(128 * way, 128)]

    def z_hop(g, way):
        if g <= 2:
            source = nz.at[0, pl.ds(128 * (g - 1), 128)]
        elif g <= 6:
            source = z_block(g - 2, way)
        else:
            source = z_block(5 + way, way)
        n = 2 * g + way
        return remote(source, z_block(g, way), zs.at[n], zr.at[n], f, z_dn if way else z_up)

    for g in (1, 2):
        if g == 2:
            norm_rows(128)
        for way in range(2):
            z_hop(g, way).start()

    def arrive(g):
        for way in range(2):
            z_hop(g, way).wait_recv()
            if g <= 4:
                z_hop(g + 2, way).start()
            elif g == 5 + way:
                z_hop(7, way).start()

    lanes = lax.broadcasted_iota(jnp.int32, (HEAD, TOK), 1)
    own, other = [], []
    for part in range(3):
        at = pl.ds(pl.multiple_of(D * part + 128 * z, 128), TOK)
        window = w_qkv_s[:, at].astype(F32)
        inside = (lanes >= HEAD * part) & (lanes < HEAD * part + HEAD)
        for which, found in ((x_lo, own), (1 - x_lo, other)):
            shift = lax.rem(2 * TOK - 16 * z - HEAD * which + HEAD * part, TOK)
            found.append(jnp.where(inside, pltpu.roll(window, shift, axis=1), 0.0))
    sel = jnp.concatenate([own[0] + own[1] + own[2], other[0] + other[1] + other[2]], axis=1)

    def to_rows(value):
        tail = jnp.zeros((ROWS - HEAD, value.shape[1]), F32)
        return jnp.concatenate([value.astype(F32), tail], axis=0).astype(BF16)

    wsel[...] = to_rows(sel)
    def sel_copy(source, peer, n):
        return remote(source, wsel_all.at[n], ss.at[n], sr.at[n], peer, p)

    sel_copy(wsel, other_core, f).start()

    def sel_send(i, c):
        peer = lax.rem(f + 2 * i, 16)
        remote(wsel, wsel_all.at[f], ss.at[peer], sr.at[f], peer, p).start()
        return c

    lax.fori_loop(1, 8, sel_send, 0)
    wsel_all[f] = wsel[...]

    wrest[0, :, 0:EARLY] = to_rows(w_out_s[:, 0:EARLY])
    wrest[0, :, EARLY:HALF] = to_rows(w_qkv_t[:, 0 : 2 * D])
    wrest[1, :, 0 : D - EARLY] = to_rows(w_out_s[:, EARLY:D])
    wrest[1, :, D - EARLY : EARLY] = jnp.zeros((ROWS, 2 * EARLY - D), BF16)
    wrest[1, :, EARLY : EARLY + D] = to_rows(w_qkv_t[:, 2 * D : 3 * D])
    wrest[1, :, EARLY + D : HALF] = to_rows(w_out_t[...])
    first = remote(wrest.at[1 - core], w1, ws.at[0], wr.at[0], other_core, p)
    first.start()


    first.wait()
    mine = wrest[core, 0:72, :].astype(F32)
    theirs = w1[0:72, :].astype(F32)
    is_first = core == 0
    low = jnp.where(is_first, mine, theirs)
    high = jnp.where(is_first, theirs, mine)
    w[core, pl.ds(pl.multiple_of(144 * chip, 144), 144), :] = jnp.concatenate(
        [low, high], axis=0
    ).astype(BF16)

    def chip_of(at_y, kind):
        return 2 * at_y + (x_hi if kind == 0 else 1 - x_hi)

    def rows(half, n, start, size, part):
        at = pl.ds(pl.multiple_of(144 * n + start, 16), size)
        return w.at[half, at, pl.ds(EARLY * part, HALF - EARLY if part else EARLY)]

    y_prev = lax.rem(y + 3, 4)
    y_next = lax.rem(y + 1, 4)
    y_far = lax.rem(y + 2, 4)

    def weight_copy(block, n, part, to_f, to_p):
        n = n + 17 * part
        return remote(block, block, ws.at[n], wr.at[n], to_f, to_p)

    def cross_send(far, part):
        block = rows(core, chip_of(y_far if far else y, 0), 0, 144, part)
        return weight_copy(block, 1 + far, part, cross_f, x_pair)

    def y_send(way, kind, part):
        block = rows(core, chip_of(y, kind), 0, 144, part)
        return weight_copy(block, 3 + way * 2 + kind, part, y_dn if way else y_up, p)

    def y_pass(way, part):
        n = chip_of(y_next if way else y_prev, 0)
        block = rows(core, n, 80 * way, 64 if way else 80, part)
        return weight_copy(block, 7 + way, part, y_dn if way else y_up, p)

    def y_pass_in(way, part):
        block = rows(core, chip_of(y_far, 0), 80 * way, 64 if way else 80, part)
        return weight_copy(block, 7 + way, part, other_core, p)

    def core_send(at_y, kind, part):
        n = chip_of(at_y, kind)
        return weight_copy(rows(core, n, 0, 144, part), 9 + n, part, other_core, p)

    def core_in(at_y, kind, part):
        n = chip_of(at_y, kind)
        return weight_copy(rows(1 - core, n, 0, 144, part), 9 + n, part, other_core, p)

    def near_rows(part):
        cross_send(0, part).wait_recv()
        for way in range(2):
            y_send(way, 0, part).wait_recv()
            y_pass(way, part).start()
        for way in range(2):
            y_send(way, 1, part).start()
        core_send(y, 1, part).start()
        core_send(y_prev, 0, part).start()
        core_send(y_next, 0, part).start()

    def far_rows(part):
        for way in range(2):
            y_pass_in(way, part).wait_recv()
        cross_send(1, part).start()
        core_send(y_far, 0, part).start()

    def crossed_rows(part):
        for way in range(2):
            y_send(way, 1, part).wait_recv()
        core_send(y_prev, 1, part).start()
        core_send(y_next, 1, part).start()

    def last_rows(part):
        cross_send(1, part).wait_recv()
        core_send(y_far, 1, part).start()

    def all_rows(part):
        for at_y in (y, y_prev, y_next, y_far):
            for kind in range(2):
                core_in(at_y, kind, part).wait_recv()

    for part in range(2):
        cross_send(0, part).start()
        for way in range(2):
            y_send(way, 0, part).start()
        core_send(y, 0, part).start()

    zero8 = jnp.zeros((8, TOK), F32)
    ones8 = jnp.where(lax.broadcasted_iota(jnp.int32, (8, TOK), 0) == 0, 1.0, 0.0)

    def to_natural(slot):
        kt = qkv[slot, ROWS : 2 * ROWS, :].astype(F32)
        kt = jnp.concatenate([kt, jnp.zeros((128 - ROWS, TOK), F32)], axis=0)
        kn[slot * TOK : slot * TOK + TOK, :] = kt.T.astype(BF16)

    def pair_copy(g, start=0, size=3 * ROWS):
        n = 8 if g == 7 and start == 0 else g
        at = pl.ds(start, size)
        return remote(stage.at[g, at], qkv.at[2 * g + 1, at], xs.at[n], xr.at[n], f, x_pair)

    def project(g):
        for lane in (256, 0):
            r = jnp.dot(nz[g], wc[:, lane : lane + 256], preferred_element_type=F32)
            t = r.T
            block = [t[0:72] * Q_SCALE, zero8, t[72:144], zero8, t[144:216], ones8]
            block = jnp.concatenate(block, axis=0).astype(BF16)
            if lane:
                stage[g] = block
                if g == 7:
                    pair_copy(g, ROWS, 2 * ROWS).start()
                    pair_copy(g, 0, ROWS).start()
                else:
                    pair_copy(g).start()
            else:
                qkv[2 * g] = block
        to_natural(2 * g)

    def receive(g):
        if g == 7:
            pair_copy(g, ROWS, 2 * ROWS).wait()
        else:
            pair_copy(g).wait()
        to_natural(2 * g + 1)

    head = 2 * z + x_lo
    scores = (score_a, score_b)
    tops = (top_a, top_b)
    top_all[...] = jnp.full(top_all.shape, -1e30, F32)
    acc_all[...] = jnp.zeros(acc_all.shape, F32)

    def out_copy(g, odd, half):
        s = (g + 1) // 2
        if isinstance(g, int):
            batch = half if g in (0, 7) else (g + 1) % 2
        else:
            batch = lax.rem(g + 1, 2)
        to = (1 - x_lo if odd else x_lo) * 8 + lax.rem(z + (s if half else 8 - s), 8)
        n = 2 * odd + half
        return remote(
            ostage.at[g, n], attn.at[head, batch], os.at[4 * g + n], orr.at[2 * head + batch], f, to
        )

    def emit(g, o):
        both = isinstance(g, int) and g in (0, 7)
        o = jnp.concatenate([o, jnp.zeros((8, 2 * TOK), F32)], axis=0).astype(BF16)
        for odd in range(2):
            for half in range(2):
                n = 2 * odd + half
                ostage[g, n] = o[:, 128 * n : 128 * n + 128]
                if both and g + odd == 0:
                    attn[head, half] = ostage[g, n]
                elif not (both and half):
                    out_copy(g, odd, half).start()

    def score_steps(gq, gk, buf):
        q_t = jnp.concatenate([qkv[2 * gq, 0:ROWS, :], qkv[2 * gq + 1, 0:ROWS, :]], axis=1)
        state = [None]

        def one(u):
            at = pl.ds(pl.multiple_of(2 * TOK * gk + TOK * u, TOK), TOK)
            s = jnp.dot(kn[at, 0:ROWS], q_t, preferred_element_type=F32)
            scores[buf][TOK * u : TOK * u + TOK, :] = s
            m = jnp.max(s.reshape(TOK // 8, 8, 2 * TOK), axis=0)
            state[0] = m if state[0] is None else jnp.maximum(state[0], m)
            if u == 1:
                tops[buf][...] = state[0]

        return [lambda: one(0), lambda: one(1)]

    def job(gq, gk, buf, following, last):
        steps = score_steps(*following, 1 - buf) if following else None
        old = top_all[gq]
        m = jnp.maximum(old, jnp.max(tops[buf][...], axis=0, keepdims=True))
        acc = acc_all[gq] * jnp.exp2(old - m)
        for u in range(2):
            if steps:
                steps[u]()
            prob = jnp.exp2(scores[buf][TOK * u : TOK * u + TOK, :] - m).astype(BF16)
            acc += jnp.dot(
                qkv[2 * gk + u, 2 * ROWS : 3 * ROWS, :], prob, preferred_element_type=F32
            )
        if last:
            return acc[0:HEAD] / acc[HEAD : HEAD + 1]
        top_all[gq] = m
        acc_all[gq] = acc

    def jobs(pick, count, finish=False):
        for step in score_steps(*pick(0), 0):
            step()
        rest = 1 if count % 2 else 2

        def one(at, buf, following):
            o = job(*at, buf, following, finish)
            if finish:
                emit(at[0], o)

        def two(i, c):
            one(pick(2 * i), 0, pick(2 * i + 1))
            one(pick(2 * i + 1), 1, pick(2 * i + 2))
            return c

        if count > rest:
            lax.fori_loop(0, (count - rest) // 2, two, 0)
        for t in range(count - rest, count):
            following = pick(t + 1) if t + 1 < count else None
            one(pick(t), (t - count + rest) % 2, following)

    def group_jobs(g, begin, end):
        def pick(t):
            t = t + begin
            if isinstance(t, int):
                return (t, g) if t < g else (g, t - g)
            return jnp.where(t < g, t, g), jnp.where(t < g, g, t - g)

        jobs(pick, end - begin)

    arrive(1)

    def sel_take(i, c):
        peer = lax.rem(f + 2 * i, 16)
        sel_copy(wsel, peer, peer).wait_recv()
        remote(
            wsel_all.at[peer], wsel_all.at[peer], ss.at[peer + 1 - 2 * core], sr.at[peer], other_core, p
        ).start()
        return c

    lax.fori_loop(1, 8, sel_take, 0)

    def sel_swapped(i, c):
        n = lax.rem(other_core + 2 * i, 16)
        sel_copy(wsel, other_core, n).wait_recv()
        return c

    lax.fori_loop(0, 8, sel_swapped, 0)
    for j in range(8):
        a = wsel_all[2 * j, 0:72, :].astype(F32)
        b = wsel_all[2 * j + 1, 0:72, :].astype(F32)
        wc[144 * j : 144 * j + 144, :] = jnp.concatenate([a, b], axis=0).astype(BF16)
    project(0)
    project(1)
    arrive(2)
    project(2)
    receive(0)
    receive(1)
    group_jobs(0, 0, 1)
    group_jobs(1, 0, 3)
    arrive(3)
    near_rows(0)
    project(3)
    receive(2)
    group_jobs(2, 0, 5)
    arrive(4)
    near_rows(1)
    project(4)
    receive(3)
    group_jobs(3, 0, 7)
    arrive(5)
    far_rows(0)
    project(5)
    receive(4)
    group_jobs(4, 0, 9)
    receive(5)
    group_jobs(5, 0, 4)
    arrive(6)
    crossed_rows(0)
    project(6)
    group_jobs(5, 4, 11)
    far_rows(1)
    receive(6)
    group_jobs(6, 0, 4)
    arrive(7)
    project(7)
    last_rows(0)
    group_jobs(6, 4, 13)
    receive(7)

    jobs(lambda t: (0 if isinstance(t, int) and t == 3 else 5 - 2 * t, 7), 4, True)
    pair_copy(7, 0, ROWS).wait()
    jobs(lambda t: (7, t), 7)
    jobs(lambda t: (7, 7), 1, True)
    for g, odd in ((7, 0), (7, 1), (0, 1)):
        out_copy(g, odd, 1).start()
    jobs(lambda t: (6 - 2 * t, 7), 3, True)

    all_rows(0)
    crossed_rows(1)

    def source(i):
        d = jnp.where(i < 12, 3 - i // 4, jnp.where(i < 14, 0, 4))
        odd = jnp.where(i < 12, lax.rem(i, 4) // 2, lax.rem(i, 2))
        lo = jnp.where(odd == 1, 1 - x_lo, x_lo)
        at_z = lax.rem(z + jnp.where(lax.rem(i, 2) == 1, d, 8 - d), 8)
        return lo, at_z

    def lay_out(i, c):
        lo, at_z = source(i)
        first = HEAD * (2 * at_z + lo)
        from_row = first // 16 * 16
        shifted = first > from_row
        for half, lane, size in ((0, 0, EARLY), (1, EARLY, D - EARLY)):
            block = w[half, pl.ds(pl.multiple_of(from_row, 16), ROWS), 0:size].astype(F32)
            block = jnp.where(shifted, block[ROWS - HEAD :], block[:HEAD])
            block = jnp.concatenate([block, jnp.zeros((128 - HEAD, size), F32)], axis=0)
            to = pl.ds(pl.multiple_of(128 * i, 128), 128)
            wo[to, lane : lane + size] = block.astype(BF16)
        return c

    lax.fori_loop(0, HEADS, lay_out, 0)

    def rows16(ref, n):
        return ref.at[pl.ds(pl.multiple_of(16 * n, 16), 16)]

    def pack(value):
        rest = jnp.concatenate([value[:, EARLY:], jnp.zeros((128, 2 * EARLY - D), F32)], axis=1)
        sides = [value[:, :EARLY].reshape(16, 8, EARLY), rest.reshape(16, 8, EARLY)]
        return jnp.concatenate(sides, axis=1).reshape(TOK, EARLY).astype(BF16)

    steps = [(j // 4, j // 2 % 2, j % 2) for j in range(1, 16)]
    steps.sort(key=lambda j: -(min(j[0], 4 - j[0]) + 2 * j[1]))

    def swap_peer(n):
        dy, dx, dc = steps[n]
        at_x = 1 - x_hi if dx else x_hi
        return lax.rem(y + dy, 4) * 4 + at_x * 2 + (1 - core if dc else core)

    def swap_copy(source, target, ssem, rsem, b, n, to, at):
        return remote(
            rows16(source.at[b], to), rows16(target.at[b], at),
            ssem.at[16 * b + n], rsem.at[16 * b + at], to, p,
        )

    def swap_start(source, target, ssem, rsem, b):
        for n in range(15):
            swap_copy(source, target, ssem, rsem, b, n, swap_peer(n), f).start()

    def swap_wait(source, target, ssem, rsem, b):
        for n in range(15):
            peer = swap_peer(n)
            swap_copy(source, target, ssem, rsem, b, n, peer, peer).wait()

    for b in range(2):
        def out_take(i, c, b=b):
            lo, at_z = source(i)
            h = 2 * at_z + lo

            @pl.when(i != 12)
            def _():
                remote(
                    ostage.at[0, 0], attn.at[h, b], os.at[0], orr.at[2 * h + b], f, lo * 8 + at_z
                ).wait_recv()

            block = attn[h, b].astype(F32)
            block = jnp.concatenate([block, jnp.zeros((128 - ROWS, 128), F32)], axis=0)
            heads[:, pl.ds(pl.multiple_of(128 * i, 128), 128)] = block.T.astype(BF16)
            return c

        lax.fori_loop(0, HEADS, out_take, 0)
        r = jnp.dot(heads[...], wo[...], preferred_element_type=F32)
        mid = hid[128 * b : 128 * b + 128, :].astype(F32) + mod[2:3] * r
        midp[b] = pack(mid)
        swap_start(midp, midt, ms, mr, b)
        here = pl.ds(pl.multiple_of(16 * f, 16), 16)
        midt[b, here, :] = midp[b, here, :]

    for g in range(1, 8):
        for way in range(2):
            z_hop(g, way).wait_send()

    def sel_sent(i, c):
        sel_copy(wsel, other_core, lax.rem(f + 2 * i, 16)).wait_send()
        sel_copy(wsel, other_core, lax.rem(other_core + 2 * i, 16)).wait_send()
        return c

    lax.fori_loop(1, 8, sel_sent, 0)
    sel_copy(wsel, other_core, f).wait_send()
    for g in range(8):
        for odd in range(2):
            for half in range(2):
                if g + odd > 0:
                    out_copy(g, odd, half).wait_send()
    last_rows(1)
    for part in range(2):
        for way in range(2):
            cross_send(way, part).wait_send()
            y_pass(way, part).wait_send()
            for kind in range(2):
                y_send(way, kind, part).wait_send()
        for at_y in (y, y_prev, y_next, y_far):
            for kind in range(2):
                core_send(at_y, kind, part).wait_send()
    all_rows(1)

    def keep(b):
        return pltpu.make_async_copy(rows16(osend.at[b], f), rows16(out.at[b], f), ls.at[b])

    ri = lax.broadcasted_iota(jnp.int32, (128, 128), 0)
    ci = lax.broadcasted_iota(jnp.int32, (128, 128), 1)
    same = lax.rem(ri, 8) == lax.rem(ci, 8)
    lane = lax.broadcasted_iota(jnp.int32, (128, TOK), 1)
    for b in range(2):
        swap_wait(midp, midt, ms, mr, b)
        value = unpack(midt.at[b])
        normed = norm_modulate(value, mod[3:4], mod[4:5]).astype(BF16)
        r = jnp.dot(normed, w[0, :, EARLY:HALF], preferred_element_type=F32)
        qkv_t[:, 0:D] = (r[:, 0:D] * Q_SCALE).astype(BF16)
        qkv_t[:, D : 2 * D] = r[:, D:].astype(BF16)
        r = jnp.dot(normed, w[1, :, EARLY : EARLY + D], preferred_element_type=F32)
        qkv_t[:, 2 * D :] = r.astype(BF16)
        acc_t[...] = jnp.zeros_like(acc_t)
        for h in range(HEADS):
            start = 128 * min(HEAD * h // 128, 7)
            low = HEAD * h - start
            inside = (lane >= low) & (lane < low + HEAD)
            q = qkv_t[:, start : start + 256]
            q = jnp.where(inside, q, jnp.zeros_like(q))
            k = qkv_t[:, D + start : D + start + 256]
            v = qkv_t[:, 2 * D + start : 2 * D + start + 256]
            s = lax.dot_general(q, k, (((1,), (1,)), ((), ())), preferred_element_type=F32)
            s = jnp.where(same, s, -1e30)
            prob = jnp.exp2(s - jnp.max(s, axis=1, keepdims=True))
            total = jnp.sum(prob, axis=1, keepdims=True)
            o = jnp.dot(prob.astype(BF16), v, preferred_element_type=F32) / total
            acc_t[:, start : start + 256] = jnp.where(inside, o, acc_t[:, start : start + 256])
        r = jnp.dot(acc_t[...].astype(BF16), w[1, :, EARLY + D : HALF], preferred_element_type=F32)
        osend[b] = pack(unpack(midt.at[b]) + mod[5:6] * r)
        swap_start(osend, out, bs, br, b)
        keep(b).start()

    for b in range(2):
        swap_wait(osend, out, bs, br, b)
        keep(b).wait()


def unpack(ref):
    value = ref[...].astype(F32).reshape(16, 16, EARLY)
    return jnp.concatenate([value[:, 0:8], value[:, 8:16, 0 : D - EARLY]], axis=2).reshape(128, D)


def unpack_kernel(packed, out):
    for b in range(2):
        out[128 * b : 128 * b + 128, :] = unpack(packed.at[b]).astype(BF16)


VMEM = pl.BlockSpec(memory_space=pltpu.VMEM)


def block_call(*args):
    dma = pltpu.SemaphoreType.DMA
    return pl.pallas_call(
        block_kernel,
        out_shape=jax.ShapeDtypeStruct((2, TOK, EARLY), BF16),
        in_specs=[VMEM] * 6,
        out_specs=pl.BlockSpec(memory_space=pl.ANY),
        scratch_shapes=[
            pltpu.VMEM((8, TOK, D), BF16),
            pltpu.VMEM((ROWS, 512), BF16),
            pltpu.VMEM((2, ROWS, HALF), BF16),
            pltpu.VMEM((HEADS * 128, D), BF16),
            pltpu.VMEM((128, HEADS * 128), BF16),
            pltpu.VMEM((16, ROWS, 512), BF16),
            pltpu.VMEM((D, 512), BF16),
            pltpu.VMEM((16, 3 * ROWS, TOK), BF16),
            pltpu.VMEM((8, 3 * ROWS, TOK), BF16),
            pltpu.VMEM((4096, 128), BF16),
            pltpu.VMEM((8, 4, ROWS, 128), BF16),
            pltpu.VMEM((HEADS, 2, ROWS, 128), BF16),
            pltpu.VMEM((ROWS, HALF), BF16),
            pltpu.VMEM((2, D, HALF), BF16),
            pltpu.VMEM((2 * TOK, 2 * TOK), F32),
            pltpu.VMEM((2 * TOK, 2 * TOK), F32),
            pltpu.VMEM((8, 2 * TOK), F32),
            pltpu.VMEM((8, 2 * TOK), F32),
            pltpu.VMEM((8, 1, 2 * TOK), F32),
            pltpu.VMEM((8, ROWS, 2 * TOK), F32),
            pltpu.VMEM((2, TOK, EARLY), BF16),
            pltpu.VMEM((2, TOK, EARLY), BF16),
            pltpu.VMEM((128, 3 * D), BF16),
            pltpu.VMEM((128, D), F32),
            pltpu.VMEM((2, TOK, EARLY), BF16),
            dma((16,)), dma((16,)),
            dma((16,)), dma((16,)),
            dma((9,)), dma((9,)),
            dma((32,)), dma((32,)),
            dma((34,)), dma((34,)),
            dma((32,)), dma((32,)),
            dma((32,)), dma((32,)),
            dma((2,)),
        ],
        compiler_params=pltpu.CompilerParams(
            collective_id=0, has_side_effects=True, vmem_limit_bytes=60 * 1024 * 1024
        ),
        name="block",
    )(*args)


def body(hidden_states, modulation, w_qkv_spatial, w_out_spatial, w_qkv_temporal, w_out_temporal):
    out = block_call(
        hidden_states.reshape(TOK, D),
        modulation,
        w_qkv_spatial,
        w_out_spatial,
        w_qkv_temporal,
        w_out_temporal,
    )
    out = pl.pallas_call(
        unpack_kernel,
        out_shape=jax.ShapeDtypeStruct((TOK, D), BF16),
        in_specs=[VMEM],
        out_specs=VMEM,
        name="unpack",
    )(out)
    return out.reshape(1, TOK, D)


def solution(mesh):
    in_specs = (
        P("frame", "patch", None),
        P(),
        P("frame", None),
        P("frame", None),
        P("frame", None),
        P("frame", None),
    )
    out_specs = P("frame", "patch", None)
    return jax.shard_map(body, mesh=mesh, in_specs=in_specs, out_specs=out_specs, check_vma=False)
```

```python
import math

import jax
import jax.numpy as jnp
from jax import lax
from jax.experimental import pallas as pl
from jax.experimental.pallas import tpu as pltpu
from jax.sharding import PartitionSpec as P

HEAD = 72
HEADS = 16
D = 1152
TOK = 256
ROWS = 80
HALF = 2944
EARLY = 640
Q_SCALE = HEAD ** (-0.5) * math.log2(math.e)
F32 = jnp.float32
BF16 = jnp.bfloat16


def remote(src, dst, send, recv, frame, patch):
    return pltpu.make_async_remote_copy(
        src_ref=src,
        dst_ref=dst,
        send_sem=send,
        recv_sem=recv,
        device_id={"frame": frame, "patch": patch},
        device_id_type=pl.DeviceIdType.MESH,
    )


def signal(sem, frame, patch):
    pl.semaphore_signal(
        sem, inc=1, device_id={"frame": frame, "patch": patch}, device_id_type=pl.DeviceIdType.MESH
    )


def norm_modulate(x, shift, scale):
    centred = x - jnp.mean(x, axis=-1, keepdims=True)
    variance = jnp.mean(centred * centred, axis=-1, keepdims=True)
    return centred * lax.rsqrt(variance + 1e-06) * (1.0 + scale) + shift


def block_kernel(
    hid, mod, w_qkv_s, w_out_s, w_qkv_t, w_out_t, out,
    nz, wsel, wrest, wo, heads, wsel_all, wc, qkv, stage, kn, ostage, attn, w1, w, score_a, score_b, top_a, top_b, top_all, acc_all,
    midp, midt, qkv_t, acc_t, osend,
    zs, zr, ss, sr, xs, xr, os, orr, ws, wr, ms, mr, bs, br, ls,
):
    f = lax.axis_index("frame")
    p = lax.axis_index("patch")
    core = lax.rem(f, 2)
    x_hi = lax.rem(f // 2, 2)
    y = f // 4
    x_lo = p // 8
    z = lax.rem(p, 8)
    chip = f // 2
    other_core = f + 1 - 2 * core
    cross_f = (y * 2 + 1 - x_hi) * 2 + core
    x_pair = (1 - x_lo) * 8 + z
    y_up = lax.rem(y + 1, 4) * 4 + x_hi * 2 + core
    y_dn = lax.rem(y + 3, 4) * 4 + x_hi * 2 + core
    z_up = x_lo * 8 + lax.rem(z + 1, 8)
    z_dn = x_lo * 8 + lax.rem(z + 7, 8)

    barrier = pltpu.get_barrier_semaphore()

    for i in range(1, 16):
        signal(barrier, f, lax.rem(p + i, 16))
        signal(barrier, lax.rem(f + i, 16), p)
    signal(barrier, cross_f, x_pair)

    def norm_rows(at):
        value = norm_modulate(hid[at : at + 128, :].astype(F32), mod[0:1], mod[1:2])
        nz[0, at : at + 128, :] = value.astype(BF16)

    norm_rows(0)

    pl.semaphore_wait(barrier, 31)

    def z_block(g, way):
        return nz.at[g, pl.ds(128 * way, 128)]

    def z_hop(g, way):
        if g <= 2:
            source = nz.at[0, pl.ds(128 * (g - 1), 128)]
        elif g <= 6:
            source = z_block(g - 2, way)
        else:
            source = z_block(5 + way, way)
        n = 2 * g + way
        return remote(source, z_block(g, way), zs.at[n], zr.at[n], f, z_dn if way else z_up)

    for g in (1, 2):
        if g == 2:
            norm_rows(128)
        for way in range(2):
            z_hop(g, way).start()

    def arrive(g):
        for way in range(2):
            z_hop(g, way).wait_recv()
            if g <= 4:
                z_hop(g + 2, way).start()
            elif g == 5 + way:
                z_hop(7, way).start()

    lanes = lax.broadcasted_iota(jnp.int32, (HEAD, TOK), 1)
    own, other = [], []
    for part in range(3):
        at = pl.ds(pl.multiple_of(D * part + 128 * z, 128), TOK)
        window = w_qkv_s[:, at].astype(F32)
        inside = (lanes >= HEAD * part) & (lanes < HEAD * part + HEAD)
        for which, found in ((x_lo, own), (1 - x_lo, other)):
            shift = lax.rem(2 * TOK - 16 * z - HEAD * which + HEAD * part, TOK)
            found.append(jnp.where(inside, pltpu.roll(window, shift, axis=1), 0.0))
    sel = jnp.concatenate([own[0] + own[1] + own[2], other[0] + other[1] + other[2]], axis=1)

    def to_rows(value):
        tail = jnp.zeros((ROWS - HEAD, value.shape[1]), F32)
        return jnp.concatenate([value.astype(F32), tail], axis=0).astype(BF16)

    wsel[...] = to_rows(sel)
    def sel_copy(source, peer, n):
        return remote(source, wsel_all.at[n], ss.at[n], sr.at[n], peer, p)

    sel_copy(wsel, other_core, f).start()

    def sel_send(i, c):
        peer = lax.rem(f + 2 * i, 16)
        remote(wsel, wsel_all.at[f], ss.at[peer], sr.at[f], peer, p).start()
        return c

    lax.fori_loop(1, 8, sel_send, 0)
    wsel_all[f] = wsel[...]

    wrest[0, :, 0:EARLY] = to_rows(w_out_s[:, 0:EARLY])
    wrest[0, :, EARLY:HALF] = to_rows(w_qkv_t[:, 0 : 2 * D])
    wrest[1, :, 0 : D - EARLY] = to_rows(w_out_s[:, EARLY:D])
    wrest[1, :, D - EARLY : EARLY] = jnp.zeros((ROWS, 2 * EARLY - D), BF16)
    wrest[1, :, EARLY : EARLY + D] = to_rows(w_qkv_t[:, 2 * D : 3 * D])
    wrest[1, :, EARLY + D : HALF] = to_rows(w_out_t[...])
    first = remote(wrest.at[1 - core], w1, ws.at[0], wr.at[0], other_core, p)
    first.start()


    first.wait()
    mine = wrest[core, 0:72, :].astype(F32)
    theirs = w1[0:72, :].astype(F32)
    is_first = core == 0
    low = jnp.where(is_first, mine, theirs)
    high = jnp.where(is_first, theirs, mine)
    w[core, pl.ds(pl.multiple_of(144 * chip, 144), 144), :] = jnp.concatenate(
        [low, high], axis=0
    ).astype(BF16)

    def chip_of(at_y, kind):
        return 2 * at_y + (x_hi if kind == 0 else 1 - x_hi)

    def rows(half, n, start, size, part):
        at = pl.ds(pl.multiple_of(144 * n + start, 16), size)
        return w.at[half, at, pl.ds(EARLY * part, HALF - EARLY if part else EARLY)]

    y_prev = lax.rem(y + 3, 4)
    y_next = lax.rem(y + 1, 4)
    y_far = lax.rem(y + 2, 4)

    def weight_copy(block, n, part, to_f, to_p):
        n = n + 17 * part
        return remote(block, block, ws.at[n], wr.at[n], to_f, to_p)

    def cross_send(far, part):
        block = rows(core, chip_of(y_far if far else y, 0), 0, 144, part)
        return weight_copy(block, 1 + far, part, cross_f, x_pair)

    def y_send(way, kind, part):
        block = rows(core, chip_of(y, kind), 0, 144, part)
        return weight_copy(block, 3 + way * 2 + kind, part, y_dn if way else y_up, p)

    def y_pass(way, part):
        n = chip_of(y_next if way else y_prev, 0)
        block = rows(core, n, 80 * way, 64 if way else 80, part)
        return weight_copy(block, 7 + way, part, y_dn if way else y_up, p)

    def y_pass_in(way, part):
        block = rows(core, chip_of(y_far, 0), 80 * way, 64 if way else 80, part)
        return weight_copy(block, 7 + way, part, other_core, p)

    def core_send(at_y, kind, part):
        n = chip_of(at_y, kind)
        return weight_copy(rows(core, n, 0, 144, part), 9 + n, part, other_core, p)

    def core_in(at_y, kind, part):
        n = chip_of(at_y, kind)
        return weight_copy(rows(1 - core, n, 0, 144, part), 9 + n, part, other_core, p)

    def near_rows(part):
        cross_send(0, part).wait_recv()
        for way in range(2):
            y_send(way, 0, part).wait_recv()
            y_pass(way, part).start()
        for way in range(2):
            y_send(way, 1, part).start()
        core_send(y, 1, part).start()
        core_send(y_prev, 0, part).start()
        core_send(y_next, 0, part).start()

    def far_rows(part):
        for way in range(2):
            y_pass_in(way, part).wait_recv()
        cross_send(1, part).start()
        core_send(y_far, 0, part).start()

    def crossed_rows(part):
        for way in range(2):
            y_send(way, 1, part).wait_recv()
        core_send(y_prev, 1, part).start()
        core_send(y_next, 1, part).start()

    def last_rows(part):
        cross_send(1, part).wait_recv()
        core_send(y_far, 1, part).start()

    def all_rows(part):
        for at_y in (y, y_prev, y_next, y_far):
            for kind in range(2):
                core_in(at_y, kind, part).wait_recv()

    for part in range(2):
        cross_send(0, part).start()
        for way in range(2):
            y_send(way, 0, part).start()
        core_send(y, 0, part).start()

    zero8 = jnp.zeros((8, TOK), F32)
    ones8 = jnp.where(lax.broadcasted_iota(jnp.int32, (8, TOK), 0) == 0, 1.0, 0.0)

    def to_natural(slot):
        kt = qkv[slot, ROWS : 2 * ROWS, :].astype(F32)
        kt = jnp.concatenate([kt, jnp.zeros((128 - ROWS, TOK), F32)], axis=0)
        kn[slot * TOK : slot * TOK + TOK, :] = kt.T.astype(BF16)

    def pair_copy(g, start=0, size=3 * ROWS):
        n = 8 if g == 7 and start == 0 else g
        at = pl.ds(start, size)
        return remote(stage.at[g, at], qkv.at[2 * g + 1, at], xs.at[n], xr.at[n], f, x_pair)

    def project(g):
        for lane in (256, 0):
            r = jnp.dot(nz[g], wc[:, lane : lane + 256], preferred_element_type=F32)
            t = r.T
            block = [t[0:72] * Q_SCALE, zero8, t[72:144], zero8, t[144:216], ones8]
            block = jnp.concatenate(block, axis=0).astype(BF16)
            if lane:
                stage[g] = block
                if g == 7:
                    pair_copy(g, ROWS, 2 * ROWS).start()
                    pair_copy(g, 0, ROWS).start()
                else:
                    pair_copy(g).start()
            else:
                qkv[2 * g] = block
        to_natural(2 * g)

    def receive(g):
        if g == 7:
            pair_copy(g, ROWS, 2 * ROWS).wait()
        else:
            pair_copy(g).wait()
        to_natural(2 * g + 1)

    head = 2 * z + x_lo
    scores = (score_a, score_b)
    tops = (top_a, top_b)
    top_all[...] = jnp.full(top_all.shape, -1e30, F32)
    acc_all[...] = jnp.zeros(acc_all.shape, F32)

    def out_copy(g, odd, half):
        s = (g + 1) // 2
        if isinstance(g, int):
            batch = half if g in (0, 7) else (g + 1) % 2
        else:
            batch = lax.rem(g + 1, 2)
        to = (1 - x_lo if odd else x_lo) * 8 + lax.rem(z + (s if half else 8 - s), 8)
        n = 2 * odd + half
        return remote(
            ostage.at[g, n], attn.at[head, batch], os.at[4 * g + n], orr.at[2 * head + batch], f, to
        )

    def emit(g, o):
        both = isinstance(g, int) and g in (0, 7)
        o = jnp.concatenate([o, jnp.zeros((8, 2 * TOK), F32)], axis=0).astype(BF16)
        for odd in range(2):
            for half in range(2):
                n = 2 * odd + half
                ostage[g, n] = o[:, 128 * n : 128 * n + 128]
                if both and g + odd == 0:
                    attn[head, half] = ostage[g, n]
                elif not (both and half):
                    out_copy(g, odd, half).start()

    def score_steps(gq, gk, buf):
        q_t = jnp.concatenate([qkv[2 * gq, 0:ROWS, :], qkv[2 * gq + 1, 0:ROWS, :]], axis=1)
        state = [None]

        def one(u):
            at = pl.ds(pl.multiple_of(2 * TOK * gk + TOK * u, TOK), TOK)
            s = jnp.dot(kn[at, 0:ROWS], q_t, preferred_element_type=F32)
            scores[buf][TOK * u : TOK * u + TOK, :] = s
            m = jnp.max(s.reshape(TOK // 8, 8, 2 * TOK), axis=0)
            state[0] = m if state[0] is None else jnp.maximum(state[0], m)
            if u == 1:
                tops[buf][...] = state[0]

        return [lambda: one(0), lambda: one(1)]

    def job(gq, gk, buf, following, last):
        steps = score_steps(*following, 1 - buf) if following else None
        old = top_all[gq]
        m = jnp.maximum(old, jnp.max(tops[buf][...], axis=0, keepdims=True))
        acc = acc_all[gq] * jnp.exp2(old - m)
        for u in range(2):
            if steps:
                steps[u]()
            prob = jnp.exp2(scores[buf][TOK * u : TOK * u + TOK, :] - m).astype(BF16)
            acc += jnp.dot(
                qkv[2 * gk + u, 2 * ROWS : 3 * ROWS, :], prob, preferred_element_type=F32
            )
        if last:
            return acc[0:HEAD] / acc[HEAD : HEAD + 1]
        top_all[gq] = m
        acc_all[gq] = acc

    def jobs(pick, count, finish=False):
        for step in score_steps(*pick(0), 0):
            step()
        rest = 1 if count % 2 else 2

        def one(at, buf, following):
            o = job(*at, buf, following, finish)
            if finish:
                emit(at[0], o)

        def two(i, c):
            one(pick(2 * i), 0, pick(2 * i + 1))
            one(pick(2 * i + 1), 1, pick(2 * i + 2))
            return c

        if count > rest:
            lax.fori_loop(0, (count - rest) // 2, two, 0)
        for t in range(count - rest, count):
            following = pick(t + 1) if t + 1 < count else None
            one(pick(t), (t - count + rest) % 2, following)

    def group_jobs(g, begin, end):
        def pick(t):
            t = t + begin
            if isinstance(t, int):
                return (t, g) if t < g else (g, t - g)
            return jnp.where(t < g, t, g), jnp.where(t < g, g, t - g)

        jobs(pick, end - begin)

    arrive(1)

    def sel_take(i, c):
        peer = lax.rem(f + 2 * i, 16)
        sel_copy(wsel, peer, peer).wait_recv()
        remote(
            wsel_all.at[peer], wsel_all.at[peer], ss.at[peer + 1 - 2 * core], sr.at[peer], other_core, p
        ).start()
        return c

    lax.fori_loop(1, 8, sel_take, 0)

    def sel_swapped(i, c):
        n = lax.rem(other_core + 2 * i, 16)
        sel_copy(wsel, other_core, n).wait_recv()
        return c

    lax.fori_loop(0, 8, sel_swapped, 0)
    for j in range(8):
        a = wsel_all[2 * j, 0:72, :].astype(F32)
        b = wsel_all[2 * j + 1, 0:72, :].astype(F32)
        wc[144 * j : 144 * j + 144, :] = jnp.concatenate([a, b], axis=0).astype(BF16)
    project(0)
    project(1)
    arrive(2)
    project(2)
    receive(0)
    receive(1)
    group_jobs(0, 0, 1)
    group_jobs(1, 0, 3)
    arrive(3)
    near_rows(0)
    project(3)
    receive(2)
    group_jobs(2, 0, 5)
    arrive(4)
    near_rows(1)
    project(4)
    receive(3)
    group_jobs(3, 0, 7)
    arrive(5)
    far_rows(0)
    project(5)
    receive(4)
    group_jobs(4, 0, 9)
    receive(5)
    group_jobs(5, 0, 4)
    arrive(6)
    crossed_rows(0)
    project(6)
    group_jobs(5, 4, 11)
    far_rows(1)
    receive(6)
    group_jobs(6, 0, 4)
    arrive(7)
    project(7)
    last_rows(0)
    group_jobs(6, 4, 13)
    receive(7)

    jobs(lambda t: (0 if isinstance(t, int) and t == 3 else 5 - 2 * t, 7), 4, True)
    pair_copy(7, 0, ROWS).wait()
    jobs(lambda t: (7, t), 7)
    jobs(lambda t: (7, 7), 1, True)
    for g, odd in ((7, 0), (7, 1), (0, 1)):
        out_copy(g, odd, 1).start()
    jobs(lambda t: (6 - 2 * t, 7), 3, True)

    all_rows(0)
    crossed_rows(1)

    def source(i):
        d = jnp.where(i < 12, 3 - i // 4, jnp.where(i < 14, 0, 4))
        odd = jnp.where(i < 12, lax.rem(i, 4) // 2, lax.rem(i, 2))
        lo = jnp.where(odd == 1, 1 - x_lo, x_lo)
        at_z = lax.rem(z + jnp.where(lax.rem(i, 2) == 1, d, 8 - d), 8)
        return lo, at_z

    def lay_out(i, c):
        lo, at_z = source(i)
        first = HEAD * (2 * at_z + lo)
        from_row = first // 16 * 16
        shifted = first > from_row
        for half, lane, size in ((0, 0, EARLY), (1, EARLY, D - EARLY)):
            block = w[half, pl.ds(pl.multiple_of(from_row, 16), ROWS), 0:size].astype(F32)
            block = jnp.where(shifted, block[ROWS - HEAD :], block[:HEAD])
            block = jnp.concatenate([block, jnp.zeros((128 - HEAD, size), F32)], axis=0)
            to = pl.ds(pl.multiple_of(128 * i, 128), 128)
            wo[to, lane : lane + size] = block.astype(BF16)
        return c

    lax.fori_loop(0, HEADS, lay_out, 0)

    def rows16(ref, n):
        return ref.at[pl.ds(pl.multiple_of(16 * n, 16), 16)]

    def pack(value):
        rest = jnp.concatenate([value[:, EARLY:], jnp.zeros((128, 2 * EARLY - D), F32)], axis=1)
        sides = [value[:, :EARLY].reshape(16, 8, EARLY), rest.reshape(16, 8, EARLY)]
        return jnp.concatenate(sides, axis=1).reshape(TOK, EARLY).astype(BF16)

    steps = [(j // 4, j // 2 % 2, j % 2) for j in range(1, 16)]
    steps.sort(key=lambda j: -(min(j[0], 4 - j[0]) + 2 * j[1]))

    def swap_peer(n):
        dy, dx, dc = steps[n]
        at_x = 1 - x_hi if dx else x_hi
        return lax.rem(y + dy, 4) * 4 + at_x * 2 + (1 - core if dc else core)

    def swap_copy(source, target, ssem, rsem, b, n, to, at):
        return remote(
            rows16(source.at[b], to), rows16(target.at[b], at),
            ssem.at[16 * b + n], rsem.at[16 * b + at], to, p,
        )

    def swap_start(source, target, ssem, rsem, b):
        for n in range(15):
            swap_copy(source, target, ssem, rsem, b, n, swap_peer(n), f).start()

    def swap_wait(source, target, ssem, rsem, b):
        for n in range(15):
            peer = swap_peer(n)
            swap_copy(source, target, ssem, rsem, b, n, peer, peer).wait()

    for b in range(2):
        def out_take(i, c, b=b):
            lo, at_z = source(i)
            h = 2 * at_z + lo

            @pl.when(i != 12)
            def _():
                remote(
                    ostage.at[0, 0], attn.at[h, b], os.at[0], orr.at[2 * h + b], f, lo * 8 + at_z
                ).wait_recv()

            block = attn[h, b].astype(F32)
            block = jnp.concatenate([block, jnp.zeros((128 - ROWS, 128), F32)], axis=0)
            heads[:, pl.ds(pl.multiple_of(128 * i, 128), 128)] = block.T.astype(BF16)
            return c

        late = 8 if b else 12
        if b:
            lax.fori_loop(12, HEADS, out_take, 0)
        lax.fori_loop(0, late, out_take, 0)
        r = jnp.dot(heads[:, 0 : 128 * late], wo[0 : 128 * late, :], preferred_element_type=F32)
        if b:
            r += jnp.dot(heads[:, 1536:], wo[1536:, :], preferred_element_type=F32)
        acc_t[...] = r
        lax.fori_loop(late, late + 4, out_take, 0)
        at = slice(128 * late, 128 * late + 512)
        r = acc_t[...] + jnp.dot(heads[:, at], wo[at, :], preferred_element_type=F32)
        mid = hid[128 * b : 128 * b + 128, :].astype(F32) + mod[2:3] * r
        midp[b] = pack(mid)
        swap_start(midp, midt, ms, mr, b)
        here = pl.ds(pl.multiple_of(16 * f, 16), 16)
        midt[b, here, :] = midp[b, here, :]

    for g in range(1, 8):
        for way in range(2):
            z_hop(g, way).wait_send()

    def sel_sent(i, c):
        sel_copy(wsel, other_core, lax.rem(f + 2 * i, 16)).wait_send()
        sel_copy(wsel, other_core, lax.rem(other_core + 2 * i, 16)).wait_send()
        return c

    lax.fori_loop(1, 8, sel_sent, 0)
    sel_copy(wsel, other_core, f).wait_send()
    for g in range(8):
        for odd in range(2):
            for half in range(2):
                if g + odd > 0:
                    out_copy(g, odd, half).wait_send()
    last_rows(1)
    for part in range(2):
        for way in range(2):
            cross_send(way, part).wait_send()
            y_pass(way, part).wait_send()
            for kind in range(2):
                y_send(way, kind, part).wait_send()
        for at_y in (y, y_prev, y_next, y_far):
            for kind in range(2):
                core_send(at_y, kind, part).wait_send()
    all_rows(1)

    def keep(b):
        return pltpu.make_async_copy(rows16(osend.at[b], f), rows16(out.at[b], f), ls.at[b])

    ri = lax.broadcasted_iota(jnp.int32, (128, 128), 0)
    ci = lax.broadcasted_iota(jnp.int32, (128, 128), 1)
    same = lax.rem(ri, 8) == lax.rem(ci, 8)
    lane = lax.broadcasted_iota(jnp.int32, (128, TOK), 1)
    for b in range(2):
        swap_wait(midp, midt, ms, mr, b)
        value = unpack(midt.at[b])
        normed = norm_modulate(value, mod[3:4], mod[4:5]).astype(BF16)
        r = jnp.dot(normed, w[0, :, EARLY:HALF], preferred_element_type=F32)
        qkv_t[:, 0:D] = (r[:, 0:D] * Q_SCALE).astype(BF16)
        qkv_t[:, D : 2 * D] = r[:, D:].astype(BF16)
        r = jnp.dot(normed, w[1, :, EARLY : EARLY + D], preferred_element_type=F32)
        qkv_t[:, 2 * D :] = r.astype(BF16)
        acc_t[...] = jnp.zeros_like(acc_t)
        for h in range(HEADS):
            start = 128 * min(HEAD * h // 128, 7)
            low = HEAD * h - start
            inside = (lane >= low) & (lane < low + HEAD)
            q = qkv_t[:, start : start + 256]
            q = jnp.where(inside, q, jnp.zeros_like(q))
            k = qkv_t[:, D + start : D + start + 256]
            v = qkv_t[:, 2 * D + start : 2 * D + start + 256]
            s = lax.dot_general(q, k, (((1,), (1,)), ((), ())), preferred_element_type=F32)
            s = jnp.where(same, s, -1e30)
            prob = jnp.exp2(s - jnp.max(s, axis=1, keepdims=True))
            total = jnp.sum(prob, axis=1, keepdims=True)
            o = jnp.dot(prob.astype(BF16), v, preferred_element_type=F32) / total
            acc_t[:, start : start + 256] = jnp.where(inside, o, acc_t[:, start : start + 256])
        r = jnp.dot(acc_t[...].astype(BF16), w[1, :, EARLY + D : HALF], preferred_element_type=F32)
        osend[b] = pack(unpack(midt.at[b]) + mod[5:6] * r)
        swap_start(osend, out, bs, br, b)
        keep(b).start()

    for b in range(2):
        swap_wait(osend, out, bs, br, b)
        keep(b).wait()


def unpack(ref):
    value = ref[...].astype(F32).reshape(16, 16, EARLY)
    return jnp.concatenate([value[:, 0:8], value[:, 8:16, 0 : D - EARLY]], axis=2).reshape(128, D)


def unpack_kernel(packed, out):
    for b in range(2):
        out[128 * b : 128 * b + 128, :] = unpack(packed.at[b]).astype(BF16)


VMEM = pl.BlockSpec(memory_space=pltpu.VMEM)


def block_call(*args):
    dma = pltpu.SemaphoreType.DMA
    return pl.pallas_call(
        block_kernel,
        out_shape=jax.ShapeDtypeStruct((2, TOK, EARLY), BF16),
        in_specs=[VMEM] * 6,
        out_specs=pl.BlockSpec(memory_space=pl.ANY),
        scratch_shapes=[
            pltpu.VMEM((8, TOK, D), BF16),
            pltpu.VMEM((ROWS, 512), BF16),
            pltpu.VMEM((2, ROWS, HALF), BF16),
            pltpu.VMEM((HEADS * 128, D), BF16),
            pltpu.VMEM((128, HEADS * 128), BF16),
            pltpu.VMEM((16, ROWS, 512), BF16),
            pltpu.VMEM((D, 512), BF16),
            pltpu.VMEM((16, 3 * ROWS, TOK), BF16),
            pltpu.VMEM((8, 3 * ROWS, TOK), BF16),
            pltpu.VMEM((4096, 128), BF16),
            pltpu.VMEM((8, 4, ROWS, 128), BF16),
            pltpu.VMEM((HEADS, 2, ROWS, 128), BF16),
            pltpu.VMEM((ROWS, HALF), BF16),
            pltpu.VMEM((2, D, HALF), BF16),
            pltpu.VMEM((2 * TOK, 2 * TOK), F32),
            pltpu.VMEM((2 * TOK, 2 * TOK), F32),
            pltpu.VMEM((8, 2 * TOK), F32),
            pltpu.VMEM((8, 2 * TOK), F32),
            pltpu.VMEM((8, 1, 2 * TOK), F32),
            pltpu.VMEM((8, ROWS, 2 * TOK), F32),
            pltpu.VMEM((2, TOK, EARLY), BF16),
            pltpu.VMEM((2, TOK, EARLY), BF16),
            pltpu.VMEM((128, 3 * D), BF16),
            pltpu.VMEM((128, D), F32),
            pltpu.VMEM((2, TOK, EARLY), BF16),
            dma((16,)), dma((16,)),
            dma((16,)), dma((16,)),
            dma((9,)), dma((9,)),
            dma((32,)), dma((32,)),
            dma((34,)), dma((34,)),
            dma((32,)), dma((32,)),
            dma((32,)), dma((32,)),
            dma((2,)),
        ],
        compiler_params=pltpu.CompilerParams(
            collective_id=0, has_side_effects=True, vmem_limit_bytes=60 * 1024 * 1024
        ),
        name="block",
    )(*args)


def body(hidden_states, modulation, w_qkv_spatial, w_out_spatial, w_qkv_temporal, w_out_temporal):
    out = block_call(
        hidden_states.reshape(TOK, D),
        modulation,
        w_qkv_spatial,
        w_out_spatial,
        w_qkv_temporal,
        w_out_temporal,
    )
    out = pl.pallas_call(
        unpack_kernel,
        out_shape=jax.ShapeDtypeStruct((TOK, D), BF16),
        in_specs=[VMEM],
        out_specs=VMEM,
        name="unpack",
    )(out)
    return out.reshape(1, TOK, D)


def solution(mesh):
    in_specs = (
        P("frame", "patch", None),
        P(),
        P("frame", None),
        P("frame", None),
        P("frame", None),
        P("frame", None),
    )
    out_specs = P("frame", "patch", None)
    return jax.shard_map(body, mesh=mesh, in_specs=in_specs, out_specs=out_specs, check_vma=False)
```
